32 devices in a mesh: tbit: 4 (over y, x), box: 8 (over z, core).
Axes of the slice: x: 2, y: 2, z: 4, core: 2. Of those that a mesh axis runs over, the one named last changes fastest.
Arguments:
- coeffs: float32 [64, 16, 4, 64, 256], P(None, 'box', 'tbit'), may hold values from -6 to 6
- skeleton_first: int32 [64, 16, 4, 64], P(None, 'box'), may hold values from 0 to 16383, as said below
- skeleton_second: int32 [64, 16, 4, 64], P(None, 'box'), may hold values from 0 to 32767, as said below
- skeleton_third: int32 [64, 16, 4, 64], P(None, 'box'), may hold values from 0 to 65535, as said below
- checks_first: int32 [128, 64], replicated, may hold values from 0 to 8191, as said below
- checks_second: int32 [256, 64], replicated, may hold values from 0 to 4095, as said below
- checks_third: int32 [512, 64], replicated, may hold values from 0 to 2047, as said below
- ranks_first: int32 [64, 16, 4], P(None, 'box', 'tbit'), may hold values from 32 to 64
- ranks_second: int32 [64, 16, 4], P(None, 'box', 'tbit'), may hold values from 32 to 64
- ranks_third: int32 [64, 4, 2, 8], replicated, may hold values from 32 to 64
- interpolants: float32 [3, 64, 64], replicated, may hold values from -0.09375 to 0.09375
- owners: int32 [4, 64], replicated, may hold values from 0 to 7, as said below
Outputs:
- switched: float32 [4, 8, 2, 16, 8, 64, 256], P('tbit', 'box')
The draws below stay inside these ranges and needn't reach their ends.
Inputs may be any that keep to these rules, and one draw needn't show every extreme that they name: `skeleton_first`: entry r lies in the r-th of 64 equal parts of its source box of 16384 points. `skeleton_second`: entry r lies in the r-th of 64 equal parts of its source box of 32768 points. `skeleton_third`: entry r lies in the r-th of 64 equal parts of its source box of 65536 points. `checks_first`: entry r lies in the r-th of 64 equal parts of its target box. `checks_second`: entry r lies in the r-th of 64 equal parts of its target box. `checks_third`: entry r lies in the r-th of 64 equal parts of its target box. `owners`: in each row no box index is named more than 16 times, and some index exactly 16 times.
All inputs are finite; a program needn't handle non-finite values.
Results may differ from the reference program's by a relative error of at most 0.0003.
Values sent between devices are 32-bit elements; how exact they have to be, the bound alone decides.
No kernel may reach another device: no remote copies, remote signals or barrier semaphores. Data moves between devices by JAX's collectives and lax.ppermute only.
A program may use at most 128 MiB of HBM per device.

```python
import math
import jax
import jax.numpy as jnp
from jax import lax

R = 64
NPTS = 1048576
A0 = 64
NV = 256
NB = 8
NH = 16
CAP = 16


def box_offsets(key, shape, box_points):
    step_size = box_points // R
    spread = jnp.arange(R, dtype=jnp.int32) * step_size
    return spread + jax.random.randint(key, shape, 0, step_size, dtype=jnp.int32)


def draw_skeleton_first(key, part):
    return box_offsets(jax.random.fold_in(key, 11), (A0, NH, 4, R), NPTS // (4 * NH))


def draw_skeleton_second(key, part):
    return box_offsets(jax.random.fold_in(key, 12), (A0, NH, 4, R), NPTS // (2 * NH))


def draw_skeleton_third(key, part):
    return box_offsets(jax.random.fold_in(key, 13), (A0, NH, 4, R), NPTS // NH)


def draw_checks_first(key, part):
    return box_offsets(jax.random.fold_in(key, 21), (2 * A0, R), NPTS // (2 * A0))


def draw_checks_second(key, part):
    return box_offsets(jax.random.fold_in(key, 22), (4 * A0, R), NPTS // (4 * A0))


def draw_checks_third(key, part):
    return box_offsets(jax.random.fold_in(key, 23), (8 * A0, R), NPTS // (8 * A0))


def draw_owners(key, part):
    box_total = NH // 2

    def one_row(row_key):
        first_key, second_key, third_key = jax.random.split(row_key, 3)
        busiest = jax.random.randint(first_key, (), 0, box_total, dtype=jnp.int32)
        others = jax.random.permutation(second_key, (box_total - 1) * CAP)[:A0 - CAP].astype(jnp.int32) // CAP
        others = (others + (others >= busiest).astype(jnp.int32)).astype(jnp.int32)
        assigned = jnp.concatenate([jnp.full((CAP,), busiest, dtype=jnp.int32), others])
        return jax.random.permutation(third_key, assigned).astype(jnp.int32)
    return jax.vmap(one_row)(jax.random.split(jax.random.fold_in(key, 41), 4))


def with_ends(drawn, stream_key, least, high):
    index_at = [jax.random.randint(jax.random.fold_in(stream_key, axis), (), 0, length) for axis, length in enumerate(drawn.shape)]
    longest = drawn.shape.index(max(drawn.shape))
    next_to = index_at[:longest] + [(index_at[longest] + 1) % drawn.shape[longest]] + index_at[longest + 1:]
    return drawn.at[tuple(index_at)].set(least).at[tuple(next_to)].set(high)


def block_scale(own_key, shape, cuts, smallest, largest):
    loudness = 1.0
    for position, shards_of in cuts:
        draws = jax.random.uniform(jax.random.fold_in(jax.random.fold_in(own_key, 6), position), (shards_of,), jnp.float32, smallest / len(cuts), largest / len(cuts))
        loudness = loudness * jnp.repeat(jnp.exp(draws), shape[position] // shards_of).reshape((-1,) + (1,) * (len(shape) - 1 - position))
    return loudness


def centred(stream_key, extent, scale, bound, cuts=(), held_as=jnp.bfloat16):
    result = jax.random.normal(stream_key, extent, jnp.float32) * scale
    if len(cuts) > 0:
        result = block_scale(stream_key, extent, cuts, -0.22, 0.18) * result
    return jnp.clip(result, min=-bound, max=bound).astype(held_as)


def setup_inputs(seed: int = 0) -> dict:
    key_of = jax.random.split(jax.random.key(seed), 13)
    return {
        "coeffs": centred(key_of[0], (A0, NH, 4, R, NV), 1.0, 6.0, ((1, 8), (2, 4)), jnp.float32),
        "skeleton_first": draw_skeleton_first(jax.random.fold_in(key_of[12], 71), 0),
        "skeleton_second": draw_skeleton_second(jax.random.fold_in(key_of[12], 71), 0),
        "skeleton_third": draw_skeleton_third(jax.random.fold_in(key_of[12], 71), 0),
        "checks_first": draw_checks_first(jax.random.fold_in(key_of[12], 71), 0),
        "checks_second": draw_checks_second(jax.random.fold_in(key_of[12], 71), 0),
        "checks_third": draw_checks_third(jax.random.fold_in(key_of[12], 71), 0),
        "ranks_first": with_ends(jax.random.randint(key_of[7], (A0, NH, 4), R // 2, R + 1), jax.random.fold_in(key_of[7], 1), R // 2, R).astype(jnp.int32),
        "ranks_second": with_ends(jax.random.randint(key_of[8], (A0, NH, 4), R // 2, R + 1), jax.random.fold_in(key_of[8], 1), R // 2, R).astype(jnp.int32),
        "ranks_third": with_ends(jax.random.randint(key_of[9], (A0, 4, 2, NB), R // 2, R + 1), jax.random.fold_in(key_of[9], 1), R // 2, R).astype(jnp.int32),
        "interpolants": centred(key_of[10], (3, R, R), (R * R) ** -0.5, 0.09375, (), jnp.float32),
        "owners": draw_owners(jax.random.fold_in(key_of[12], 71), 0),
    }


two_pi = 2.0 * math.pi
highest = lax.Precision.HIGHEST


def kernel_block(targets, sources):
    target_rows = targets[..., :, None]
    source_cols = sources[..., None, :]
    upper_part = target_rows // 1024
    lower_part = target_rows % 1024
    phases = ((upper_part * source_cols) % 1024 * 1024 + lower_part * source_cols) % NPTS
    return jnp.cos(phases.astype(jnp.float32) * (two_pi / NPTS))


def merge_block(checks, points, stacked, matrix, rank_rows):
    kernels = kernel_block(checks, points)
    images = jnp.einsum('...cs,...sn->...cn', kernels, stacked, precision=highest)
    rank_width = matrix.shape[0]
    images = images.reshape(images.shape[:-2] + (images.shape[-2] // rank_width, rank_width, images.shape[-1]))
    merged = jnp.einsum('ij,...tjn->...tin', matrix, images, precision=highest)
    live_rows = jnp.arange(rank_width, dtype=jnp.int32) < rank_rows[..., None]
    return jnp.where(live_rows[..., None], merged, 0.0)


def apply_level(checks, points, stacked, matrix, rank_rows):
    def one_parent(pieces):
        check_row, point_rows, coeff_rows, rank_part = pieces
        spread = jnp.broadcast_to(check_row, (point_rows.shape[0],) + check_row.shape)
        return merge_block(spread, point_rows, coeff_rows, matrix, rank_part)
    return lax.map(one_parent, (checks, points, stacked, rank_rows))


def slot_table(owner_row, box_count, capacity):
    parent_count = owner_row.shape[0]
    onehot = (owner_row[:, None] == jnp.arange(box_count, dtype=jnp.int32)[None, :]).astype(jnp.int32)
    earlier = jnp.cumsum(onehot, axis=0, dtype=jnp.int32) - onehot
    slot_of = jnp.sum(earlier * onehot, axis=1, dtype=jnp.int32)
    matches = (onehot.T[:, None, :] == 1) & (slot_of[None, None, :] == jnp.arange(capacity, dtype=jnp.int32)[None, :, None])
    slot_parent = jnp.sum(jnp.where(matches, jnp.arange(parent_count, dtype=jnp.int32)[None, None, :], 0), axis=2).astype(jnp.int32)
    slot_used = jnp.any(matches, axis=2)
    return slot_parent, slot_used


def reference(coeffs, skeleton_first, skeleton_second, skeleton_third, checks_first, checks_second, checks_third, ranks_first, ranks_second, ranks_third, interpolants, owners):
    local_boxes = jnp.arange(NH, dtype=jnp.int32)[None, :, None, None]
    four_slots = jnp.arange(4, dtype=jnp.int32)[None, None, :, None]
    points_first = (4 * local_boxes + 2 * (four_slots % 2) + four_slots // 2) * (NPTS // (4 * NH)) + skeleton_first
    points_second = (2 * local_boxes + four_slots % 2) * (NPTS // (2 * NH)) + skeleton_second
    points_third = local_boxes * (NPTS // NH) + skeleton_third
    targets_first = jnp.arange(2 * A0, dtype=jnp.int32)[:, None] * (NPTS // (2 * A0)) + checks_first
    targets_second = jnp.arange(4 * A0, dtype=jnp.int32)[:, None] * (NPTS // (4 * A0)) + checks_second
    targets_third = jnp.arange(8 * A0, dtype=jnp.int32)[:, None] * (NPTS // (8 * A0)) + checks_third

    level_one = []
    for member in range(4):
        lowbit = member % 2
        highbit = member // 2
        points = jnp.concatenate([points_first[:, :, lowbit], points_first[:, :, 2 + lowbit]], axis=2)
        stacked = jnp.concatenate([coeffs[:, :, lowbit], coeffs[:, :, 2 + lowbit]], axis=2)
        checks = targets_first.reshape(A0, 2, R)[:, highbit]
        level_one.append(apply_level(checks, points, stacked, interpolants[0], ranks_first[:, :, member, None]))
    merged_one = jnp.concatenate(level_one, axis=2)

    level_two = []
    for member in range(4):
        first_of = 2 * (member // 2)
        points = jnp.concatenate([points_second[:, :, first_of], points_second[:, :, first_of + 1]], axis=2)
        stacked = jnp.concatenate([merged_one[:, :, first_of], merged_one[:, :, first_of + 1]], axis=2)
        checks = targets_second.reshape(A0, 4, R)[:, member]
        level_two.append(apply_level(checks, points, stacked, interpolants[1], ranks_second[:, :, member, None]))
    merged_two = jnp.concatenate(level_two, axis=2)

    outputs = []
    for member in range(4):
        points = points_third[:, :, member].reshape(A0, NB, 2 * R)
        stacked = merged_two[:, :, member].reshape(A0, NB, 2 * R, NV)
        checks = targets_third.reshape(A0, 4, 2 * R)[:, member]
        rank_rows = jnp.transpose(ranks_third[:, member], (0, 2, 1))
        merged = apply_level(checks, points, stacked, interpolants[2], rank_rows)
        slot_parent, slot_used = slot_table(owners[member], NB, CAP)
        picked = jnp.take(merged, slot_parent, axis=0)
        picked = jnp.where(slot_used[:, :, None, None, None, None], picked, 0.0)
        outputs.append(jnp.transpose(picked, (0, 3, 1, 2, 4, 5)))
    return jnp.stack(outputs, axis=0)
```

```python
import functools
import math

import jax
import jax.numpy as jnp
from jax import lax
from jax.experimental import pallas as pl
from jax.experimental.pallas import tpu as pltpu
from jax.sharding import PartitionSpec as P

NPTS = 1048576
PHASE_BITS = 20
CHUNKS = 8

SIN_TERMS = (
    1.0,
    -1.0 / 6.0,
    1.0 / 120.0,
    -1.0 / 5040.0,
    1.0 / 362880.0,
    -1.0 / 39916800.0,
    1.0 / 6227020800.0,
)


def swapped(value, axis, bit):
    mask = 2**bit
    pairs = [(source, source ^ mask) for source in range(lax.axis_size(axis))]
    return lax.ppermute(value, axis, pairs)


def slot_table(owner_row, box_count, capacity):
    parent_count = owner_row.shape[0]
    onehot = (owner_row[:, None] == jnp.arange(box_count, dtype=jnp.int32)[None, :]).astype(
        jnp.int32
    )
    earlier = jnp.cumsum(onehot, axis=0, dtype=jnp.int32) - onehot
    slot_of = jnp.sum(earlier * onehot, axis=1, dtype=jnp.int32)
    matches = (onehot.T[:, None, :] == 1) & (
        slot_of[None, None, :] == jnp.arange(capacity, dtype=jnp.int32)[None, :, None]
    )
    slot_parent = jnp.sum(
        jnp.where(matches, jnp.arange(parent_count, dtype=jnp.int32)[None, None, :], 0), axis=2
    )
    slot_used = jnp.any(matches, axis=2)
    return (slot_parent, slot_used)


def pick_slot(values, position):
    return lax.dynamic_index_in_dim(values, position, 2, keepdims=False)


def cos_kernel(targets, points):
    shift = 32 - PHASE_BITS
    phase = lax.shift_right_arithmetic(
        lax.shift_left(targets * points, jnp.int32(shift)), jnp.int32(shift)
    )
    offset = NPTS // 4 - jnp.abs(phase)
    y = offset.astype(jnp.float32) * jnp.float32(2.0 * math.pi / NPTS)
    square = y * y
    total = jnp.float32(SIN_TERMS[-1])
    for term in SIN_TERMS[-2::-1]:
        total = total * square + jnp.float32(term)
    return total * y


def split(value):
    high = value.astype(jnp.bfloat16)
    low = (value - high.astype(jnp.float32)).astype(jnp.bfloat16)
    return high, low


def product(left, right):
    rows = left.shape[0]
    left_high, left_low = split(left)
    right_high, right_low = split(right)
    both = jnp.dot(
        jnp.concatenate([left_high, left_low], axis=0),
        right_high,
        preferred_element_type=jnp.float32,
    )
    rest = jnp.dot(left_high, right_low, preferred_element_type=jnp.float32)
    return both[:rows] + both[rows:] + rest


def live(weights, rank):
    rows = lax.broadcasted_iota(jnp.int32, weights.shape, 0)
    return jnp.where(rows < rank, weights, 0.0)


def first_kernel(chunk, ranks, targets, points, matrix, mine, arrived, merged):
    step = pl.program_id(0)
    parents, boxes = mine.shape[0], mine.shape[1]
    for parent in range(parents):
        row = (chunk * pl.num_programs(0) + step) * parents + parent
        for box in range(boxes):
            kernel = cos_kernel(targets[parent], points[parent, box : box + 1, :])
            weights = live(product(matrix[...], kernel), ranks[row * boxes + box])
            stacked = jnp.concatenate([mine[parent, box], arrived[parent, box]], axis=0)
            merged[parent, box] = product(weights, stacked)


def later_kernel(
    chunk,
    ranks_second,
    ranks_third,
    targets_second,
    points_second,
    targets_third,
    points_third,
    matrices,
    mine,
    arrived,
    merged,
):
    step = pl.program_id(0)
    parents, boxes, rank_width = mine.shape[0], mine.shape[1], mine.shape[2]
    for parent in range(parents):
        row = (chunk * pl.num_programs(0) + step) * parents + parent
        seconds = []
        for box in range(boxes):
            kernel = cos_kernel(targets_second[parent], points_second[parent, box : box + 1, :])
            weights = live(product(matrices[0], kernel), ranks_second[row * boxes + box])
            stacked = jnp.concatenate([mine[parent, box], arrived[parent, box]], axis=0)
            seconds.append(product(weights, stacked))
        kernel = cos_kernel(targets_third[parent], points_third[parent])
        weights = []
        for child in range(2):
            part = product(matrices[1], kernel[child * rank_width : (child + 1) * rank_width])
            weights.append(live(part, ranks_third[row * 2 + child]))
        third = product(jnp.concatenate(weights, axis=0), jnp.concatenate(seconds, axis=0))
        for child in range(2):
            merged[parent, child] = third[child * rank_width : (child + 1) * rank_width]


def chunk_spec(shape, chunk, steps, per_step):
    block = (per_step,) + tuple(shape[1:])
    rest = (0,) * (len(shape) - 1)
    return pl.BlockSpec(block, lambda step, *_: (chunk * steps + step,) + rest)


def whole_spec(shape):
    rest = (0,) * len(shape)
    return pl.BlockSpec(tuple(shape), lambda step, *_: rest)


def first_level(chunk, count, ranks, targets, points, matrix, mine, arrived):
    per_step = 2
    steps = count // per_step
    return pl.pallas_call(
        functools.partial(first_kernel, chunk),
        grid_spec=pltpu.PrefetchScalarGridSpec(
            num_scalar_prefetch=1,
            grid=(steps,),
            in_specs=[
                chunk_spec(targets.shape, chunk, steps, per_step),
                chunk_spec(points.shape, chunk, steps, per_step),
                whole_spec(matrix.shape),
                chunk_spec(mine.shape, chunk, steps, per_step),
                chunk_spec(arrived.shape, 0, steps, per_step),
            ],
            out_specs=chunk_spec(arrived.shape, 0, steps, per_step),
        ),
        out_shape=jax.ShapeDtypeStruct(arrived.shape, jnp.float32),
        compiler_params=pltpu.CompilerParams(vmem_limit_bytes=32 * 1024 * 1024),
        name="first_level",
    )(ranks, targets, points, matrix, mine, arrived)


def later_levels(
    chunk, count, ranks, targets_second, points_second, targets_third, points_third, matrices, mine, arrived
):
    per_step = 2
    steps = count // per_step
    return pl.pallas_call(
        functools.partial(later_kernel, chunk),
        grid_spec=pltpu.PrefetchScalarGridSpec(
            num_scalar_prefetch=2,
            grid=(steps,),
            in_specs=[
                chunk_spec(targets_second.shape, chunk, steps, per_step),
                chunk_spec(points_second.shape, chunk, steps, per_step),
                chunk_spec(targets_third.shape, chunk, steps, per_step),
                chunk_spec(points_third.shape, chunk, steps, per_step),
                whole_spec(matrices.shape),
                chunk_spec(mine.shape, 0, steps, per_step),
                chunk_spec(arrived.shape, 0, steps, per_step),
            ],
            out_specs=chunk_spec(arrived.shape, 0, steps, per_step),
        ),
        out_shape=jax.ShapeDtypeStruct(arrived.shape, jnp.float32),
        compiler_params=pltpu.CompilerParams(vmem_limit_bytes=32 * 1024 * 1024),
        name="later_levels",
    )(
        ranks[0],
        ranks[1],
        targets_second,
        points_second,
        targets_third,
        points_third,
        matrices,
        mine,
        arrived,
    )


def per_device(
    coeffs,
    skeleton_first,
    skeleton_second,
    skeleton_third,
    checks_first,
    checks_second,
    checks_third,
    ranks_first,
    ranks_second,
    ranks_third,
    interpolants,
    owners,
):
    tbit_index = lax.axis_index("tbit")
    box_index = lax.axis_index("box")
    box_count = lax.axis_size("box")
    parent_count = coeffs.shape[0]
    rank_width = coeffs.shape[3]
    capacity = 2 * parent_count // box_count
    group_count = 2 * box_count
    local_boxes = 2 * box_index + jnp.arange(2, dtype=jnp.int32)[None, :, None]

    def targets_of(checks, per_parent, picked, width):
        boxes = per_parent * parent_count
        absolute = jnp.arange(boxes, dtype=jnp.int32)[:, None] * (NPTS // boxes) + checks
        mine = lax.dynamic_index_in_dim(
            absolute.reshape(parent_count, -1, width), picked, 1, keepdims=False
        )
        return mine[:, :, None]

    def first_points(slot):
        box = 4 * local_boxes + 2 * (slot % 2) + slot // 2
        return box * (NPTS // (4 * group_count)) + pick_slot(skeleton_first, slot)

    def second_points(slot):
        box = 2 * local_boxes + slot % 2
        return box * (NPTS // (2 * group_count)) + pick_slot(skeleton_second, slot)

    partner_high = jnp.bitwise_xor(tbit_index, 2)
    partner_low = jnp.bitwise_xor(tbit_index, 1)
    points_first = jnp.concatenate([first_points(tbit_index), first_points(partner_high)], axis=2)
    points_second = jnp.concatenate([second_points(tbit_index), second_points(partner_low)], axis=2)
    points_third = (
        local_boxes * (NPTS // group_count) + pick_slot(skeleton_third, tbit_index)
    ).reshape(parent_count, 1, 2 * rank_width)
    targets_first = targets_of(checks_first, 2, tbit_index // 2, rank_width)
    targets_second = targets_of(checks_second, 4, tbit_index, rank_width)
    targets_third = targets_of(checks_third, 8, tbit_index, 2 * rank_width)
    rank_one = ranks_first.reshape(-1)
    rank_two = ranks_second.reshape(-1)
    rank_three = lax.dynamic_index_in_dim(
        lax.dynamic_index_in_dim(ranks_third, tbit_index, 1, keepdims=False),
        box_index,
        2,
        keepdims=False,
    ).reshape(-1)

    mine = coeffs[:, :, 0]
    count = parent_count // CHUNKS
    arrived = []
    for chunk in range(CHUNKS):
        outgoing = mine[chunk * count : (chunk + 1) * count]
        if chunk > 0:
            outgoing, _ = lax.optimization_barrier((outgoing, arrived[-1]))
        arrived.append(swapped(outgoing, "tbit", 1))
    merged = []
    second_arrived = []
    for chunk in range(CHUNKS):
        first = first_level(
            chunk, count, rank_one, targets_first, points_first, interpolants[0], mine, arrived[chunk]
        )
        outgoing = first
        if chunk > 0:
            outgoing, _ = lax.optimization_barrier((outgoing, second_arrived[-1]))
        second_arrived.append(swapped(outgoing, "tbit", 0))
        merged.append(
            later_levels(
                chunk,
                count,
                (rank_two, rank_three),
                targets_second,
                points_second,
                targets_third,
                points_third,
                interpolants[1:],
                first,
                second_arrived[chunk],
            )
        )
    merged = jnp.concatenate(merged, axis=0)

    slot_parent, slot_used = slot_table(
        lax.dynamic_index_in_dim(owners, tbit_index, 0, keepdims=False), box_count, capacity
    )
    outgoing = jnp.take(jnp.swapaxes(merged, 0, 1), slot_parent.T, axis=1)
    outgoing = jnp.where(slot_used.T[None, :, :, None, None], outgoing, 0.0)
    switched = lax.all_to_all(outgoing, "box", split_axis=2, concat_axis=2, tiled=True)
    return switched[None, None]


def solution(mesh):
    return jax.shard_map(
        per_device,
        mesh=mesh,
        in_specs=(
            P(None, "box", "tbit", None, None),
            P(None, "box", None, None),
            P(None, "box", None, None),
            P(None, "box", None, None),
            P(),
            P(),
            P(),
            P(None, "box", "tbit"),
            P(None, "box", "tbit"),
            P(),
            P(),
            P(),
        ),
        out_specs=P("tbit", "box", None, None, None, None, None),
        check_vma=False,
    )
```

```python
import functools
import math

import jax
import jax.numpy as jnp
from jax import lax
from jax.experimental import pallas as pl
from jax.experimental.pallas import tpu as pltpu
from jax.sharding import PartitionSpec as P

NPTS = 1048576
PHASE_BITS = 20
CHUNKS = 8
LANES = 8
LAG = 2
STATIC_ROUNDS = 11

SIN_TERMS = (
    1.0,
    -1.0 / 6.0,
    1.0 / 120.0,
    -1.0 / 5040.0,
    1.0 / 362880.0,
    -1.0 / 39916800.0,
    1.0 / 6227020800.0,
)


def swapped(value, axis, bit):
    mask = 2**bit
    pairs = [(source, source ^ mask) for source in range(lax.axis_size(axis))]
    return lax.ppermute(value, axis, pairs)


def slot_table(owner_row, box_count, capacity):
    parent_count = owner_row.shape[0]
    onehot = (owner_row[:, None] == jnp.arange(box_count, dtype=jnp.int32)[None, :]).astype(
        jnp.int32
    )
    earlier = jnp.cumsum(onehot, axis=0, dtype=jnp.int32) - onehot
    slot_of = jnp.sum(earlier * onehot, axis=1, dtype=jnp.int32)
    matches = (onehot.T[:, None, :] == 1) & (
        slot_of[None, None, :] == jnp.arange(capacity, dtype=jnp.int32)[None, :, None]
    )
    slot_parent = jnp.sum(
        jnp.where(matches, jnp.arange(parent_count, dtype=jnp.int32)[None, None, :], 0), axis=2
    )
    slot_used = jnp.any(matches, axis=2)
    return (slot_parent, slot_used)


def pick_slot(values, position):
    return lax.dynamic_index_in_dim(values, position, 2, keepdims=False)


def cos_kernel(targets, points):
    shift = 32 - PHASE_BITS
    phase = lax.shift_right_arithmetic(
        lax.shift_left(targets * points, jnp.int32(shift)), jnp.int32(shift)
    )
    offset = NPTS // 4 - jnp.abs(phase)
    y = offset.astype(jnp.float32) * jnp.float32(2.0 * math.pi / NPTS)
    square = y * y
    total = jnp.float32(SIN_TERMS[-1])
    for term in SIN_TERMS[-2::-1]:
        total = total * square + jnp.float32(term)
    return total * y


def split(value):
    high = value.astype(jnp.bfloat16)
    low = (value - high.astype(jnp.float32)).astype(jnp.bfloat16)
    return high, low


def product(left, right):
    rows = left.shape[0]
    left_high, left_low = split(left)
    right_high, right_low = split(right)
    both = jnp.dot(
        jnp.concatenate([left_high, left_low], axis=0),
        right_high,
        preferred_element_type=jnp.float32,
    )
    rest = jnp.dot(left_high, right_low, preferred_element_type=jnp.float32)
    return both[:rows] + both[rows:] + rest


def live(weights, rank):
    rows = lax.broadcasted_iota(jnp.int32, weights.shape, 0)
    return jnp.where(rows < rank, weights, 0.0)


def first_kernel(chunk, ranks, targets, points, matrix, mine, arrived, merged):
    step = pl.program_id(0)
    parents, boxes = mine.shape[0], mine.shape[1]
    for parent in range(parents):
        row = (chunk * pl.num_programs(0) + step) * parents + parent
        for box in range(boxes):
            kernel = cos_kernel(targets[parent], points[parent, box : box + 1, :])
            weights = live(product(matrix[...], kernel), ranks[row * boxes + box])
            stacked = jnp.concatenate([mine[parent, box], arrived[parent, box]], axis=0)
            merged[parent, box] = product(weights, stacked)


def later_kernel(
    chunk,
    ranks_second,
    ranks_third,
    place,
    targets_second,
    points_second,
    targets_third,
    points_third,
    matrices,
    mine,
    arrived,
    *pool,
):
    merged = pool[-1]
    step = pl.program_id(0)
    parents, boxes, rank_width = mine.shape[0], mine.shape[1], mine.shape[2]
    for parent in range(parents):
        row = (chunk * pl.num_programs(0) + step) * parents + parent
        seconds = []
        for box in range(boxes):
            kernel = cos_kernel(targets_second[parent], points_second[parent, box : box + 1, :])
            weights = live(product(matrices[0], kernel), ranks_second[row * boxes + box])
            stacked = jnp.concatenate([mine[parent, box], arrived[parent, box]], axis=0)
            seconds.append(product(weights, stacked))
        kernel = cos_kernel(targets_third[parent], points_third[parent])
        weights = []
        for child in range(2):
            part = product(matrices[1], kernel[child * rank_width : (child + 1) * rank_width])
            weights.append(live(part, ranks_third[row * 2 + child]))
        third = product(jnp.concatenate(weights, axis=0), jnp.concatenate(seconds, axis=0))
        for child in range(2):
            merged[parent, child] = third[child * rank_width : (child + 1) * rank_width]


def chunk_spec(shape, chunk, steps, per_step):
    block = (per_step,) + tuple(shape[1:])
    rest = (0,) * (len(shape) - 1)
    return pl.BlockSpec(block, lambda step, *_: (chunk * steps + step,) + rest)


def whole_spec(shape):
    rest = (0,) * len(shape)
    return pl.BlockSpec(tuple(shape), lambda step, *_: rest)


def first_level(chunk, count, ranks, targets, points, matrix, mine, arrived):
    per_step = 2
    steps = count // per_step
    return pl.pallas_call(
        functools.partial(first_kernel, chunk),
        grid_spec=pltpu.PrefetchScalarGridSpec(
            num_scalar_prefetch=1,
            grid=(steps,),
            in_specs=[
                chunk_spec(targets.shape, chunk, steps, per_step),
                chunk_spec(points.shape, chunk, steps, per_step),
                whole_spec(matrix.shape),
                chunk_spec(mine.shape, chunk, steps, per_step),
                chunk_spec(arrived.shape, 0, steps, per_step),
            ],
            out_specs=chunk_spec(arrived.shape, 0, steps, per_step),
        ),
        out_shape=jax.ShapeDtypeStruct(arrived.shape, jnp.float32),
        compiler_params=pltpu.CompilerParams(vmem_limit_bytes=32 * 1024 * 1024),
        name="first_level",
    )(ranks, targets, points, matrix, mine, arrived)


def later_levels(
    chunk,
    count,
    ranks,
    place,
    targets_second,
    points_second,
    targets_third,
    points_third,
    matrices,
    mine,
    arrived,
    pool_shape,
    pool,
):
    per_step = 2
    steps = count // per_step
    parents = targets_second.shape[0]

    def pool_block(step, ranks_second, ranks_third, place):
        return (place[0] * (parents // per_step) + chunk * steps + step, 0, 0, 0)

    return pl.pallas_call(
        functools.partial(later_kernel, chunk),
        grid_spec=pltpu.PrefetchScalarGridSpec(
            num_scalar_prefetch=3,
            grid=(steps,),
            in_specs=[
                chunk_spec(targets_second.shape, chunk, steps, per_step),
                chunk_spec(points_second.shape, chunk, steps, per_step),
                chunk_spec(targets_third.shape, chunk, steps, per_step),
                chunk_spec(points_third.shape, chunk, steps, per_step),
                whole_spec(matrices.shape),
                chunk_spec(mine.shape, 0, steps, per_step),
                chunk_spec(arrived.shape, 0, steps, per_step),
            ]
            + [pl.BlockSpec(memory_space=pl.ANY)] * len(pool),
            out_specs=pl.BlockSpec((per_step,) + pool_shape[1:], pool_block),
        ),
        out_shape=jax.ShapeDtypeStruct(pool_shape, jnp.float32),
        input_output_aliases={10: 0} if pool else {},
        compiler_params=pltpu.CompilerParams(vmem_limit_bytes=32 * 1024 * 1024),
        name="later_levels",
    )(
        ranks[0],
        ranks[1],
        place,
        targets_second,
        points_second,
        targets_third,
        points_third,
        matrices,
        mine,
        arrived,
        *pool,
    )


def plan_kernel(chips, lanes, limit, capacity, chunks, owners, place, table, slots, rounds, own, ahead, used):
    parents = owners.shape[0]
    count = parents // chunks
    z = place[0]
    span = limit * lanes

    def clear(index, carry):
        table[index] = -1
        return carry

    lax.fori_loop(0, 4 * span, clear, 0)
    for box in range(2 * chips):
        used[box] = 0

    def take_slot(parent, carry):
        owner = owners[parent]
        slots[parent] = owner * capacity + used[owner]
        used[owner] = used[owner] + 1
        return carry

    lax.fori_loop(0, parents, take_slot, 0)
    width = chips * parents
    pairs = [(chip, goal) for chip in range(1, chips) for goal in range(chip + 1, chips)]
    last = []
    for direction in range(2):

        def true_chip(chip):
            return chip if direction == 0 else chips - 1 - chip

        total = 0
        for box in range(2 * chips):
            hops = true_chip(box // 2)
            total = total + used[box] * (hops * (hops + 1) // 2)

        def one_round(state):
            step, left, ready, own_head, head, tail, older = state
            ready, own_head, head, tail = list(ready), list(own_head), list(head), list(tail)

            def add_own(index, ready):
                parent = jnp.minimum(step * count + index, parents - 1)
                goal = owners[parent] // 2
                goal = goal if direction == 0 else chips - 1 - goal
                fresh = []
                for chip in range(1, chips):
                    here = (goal == chip) & (step < chunks)

                    @pl.when(here)
                    def _(chip=chip):
                        own[chip * parents + ready[chip]] = parent

                    fresh.append(ready[chip] + here.astype(jnp.int32))
                return (ready[0],) + tuple(fresh)

            for index in range(count):
                ready = add_own(index, ready)
            seen = older[0]
            newer = list(older[1:])
            sent = jnp.int32(0)
            for chip in range(chips - 1):
                for lane in range(lanes):
                    code, taken = jnp.int32(-1), jnp.bool_(False)
                    for goal in range(chips - 1, chip, -1):
                        which = (chip, goal)
                        if which in pairs:
                            place_of = pairs.index(which)
                            can = jnp.logical_not(taken) & (head[place_of] < seen[place_of])
                            value = ahead[place_of * width + jnp.minimum(head[place_of], width - 1)]
                            code = jnp.where(can, value, code)
                            head[place_of] = head[place_of] + can.astype(jnp.int32)
                            taken = taken | can
                            if (chip + 1, goal) in pairs:
                                onward(ahead, pairs.index((chip + 1, goal)), width, tail, value, can)
                        queue = chip * chips + goal
                        can = jnp.logical_not(taken) & (own_head[queue] < ready[goal])
                        value = own[goal * parents + jnp.minimum(own_head[queue], parents - 1)]
                        value = true_chip(chip) * parents + value
                        code = jnp.where(can, value, code)
                        own_head[queue] = own_head[queue] + can.astype(jnp.int32)
                        taken = taken | can
                        if (chip + 1, goal) in pairs:
                            onward(ahead, pairs.index((chip + 1, goal)), width, tail, value, can)
                    sent = sent + taken.astype(jnp.int32)
                    spot = direction * span + step * lanes + lane

                    @pl.when(z == true_chip(chip))
                    def _(code=code, spot=spot):
                        table[spot] = code

                    @pl.when(z == true_chip(chip + 1))
                    def _(code=code, spot=spot):
                        table[2 * span + spot] = code

            newer.append(tuple(tail))
            return (
                step + 1,
                left - sent,
                tuple(ready),
                tuple(own_head),
                tuple(head),
                tuple(tail),
                tuple(newer),
            )

        zero = jnp.int32(0)
        none = (zero,) * len(pairs)
        state = lax.while_loop(
            lambda state: (state[1] > 0) & (state[0] < limit),
            one_round,
            (zero, jnp.int32(total), (zero,) * chips, (zero,) * (chips * chips), none, none, (none,) * LAG),
        )
        last.append(state[0])
    rounds[0] = jnp.maximum(last[0], last[1])


def onward(ahead, place_of, width, tail, value, can):
    @pl.when(can)
    def _(spot=tail[place_of]):
        ahead[place_of * width + spot] = value

    tail[place_of] = tail[place_of] + can.astype(jnp.int32)


def plan_switch(owner_row, place, chips, capacity):
    parents = owner_row.shape[0]
    limit = round_limit(parents)
    smem = pl.BlockSpec(memory_space=pltpu.SMEM)
    return pl.pallas_call(
        functools.partial(plan_kernel, chips, LANES, limit, capacity, CHUNKS),
        in_specs=[smem, smem],
        out_specs=[smem, smem, smem],
        out_shape=[
            jax.ShapeDtypeStruct((4 * limit * LANES,), jnp.int32),
            jax.ShapeDtypeStruct((parents,), jnp.int32),
            jax.ShapeDtypeStruct((1,), jnp.int32),
        ],
        scratch_shapes=[
            pltpu.SMEM((chips * parents,), jnp.int32),
            pltpu.SMEM((chips * chips * chips * parents,), jnp.int32),
            pltpu.SMEM((2 * chips,), jnp.int32),
        ],
        name="plan_switch",
    )(owner_row, place)


def round_limit(parents):
    return 5 * parents // LANES


def round_kernel(
    lanes,
    limit,
    parents,
    capacity,
    receives,
    fresh,
    sends,
    table,
    slots,
    place,
    now,
    *refs,
):
    received = refs[: 2 * receives]
    refs = refs[2 * receives + 3 :]
    pool, out, stage = refs[:3]
    outgoing = refs[3 : 3 + 2 * sends]
    sems = refs[-1]
    z, core = place[0], place[1]
    span = limit * lanes

    def to_home(index, code, source, begin):
        parent = lax.rem(jnp.maximum(code, 0), parents)
        from_chip = lax.div(jnp.maximum(code, 0), parents)
        spot = slots[parent]
        owner, slot = lax.div(spot, capacity), lax.rem(spot, capacity)
        here = (code >= 0) & (lax.div(owner, 2) == z)

        @pl.when(here & (lax.rem(owner, 2) == core))
        def _():
            copy = pltpu.make_async_copy(source, out.at[:, slot, from_chip, core], sems.at[index])
            copy.start() if begin else copy.wait()

        @pl.when(here & (lax.rem(owner, 2) != core))
        def _():
            copy = pltpu.make_async_copy(source, stage.at[:, slot, from_chip], sems.at[index])
            copy.start() if begin else copy.wait()

        return here

    def take_in(begin):
        index = 0
        for back in range(receives):
            for direction in range(2):
                for lane in range(lanes):
                    step = now[0] - LAG + back
                    code = table[(2 + direction) * span + jnp.maximum(step, 0) * lanes + lane]
                    code = jnp.where(step >= 0, code, -1)
                    source = received[2 * back + direction].at[lane]
                    here = to_home(index, code, source, begin)

                    @pl.when((code >= 0) & jnp.logical_not(here))
                    def _(code=code, source=source, index=index):
                        copy = pltpu.make_async_copy(source, pool.at[code], sems.at[index])
                        copy.start() if begin else copy.wait()

                    index += 1
        for member in range(fresh):
            code = z * parents + now[0] * fresh + member
            to_home(index, code, pool.at[code], begin)
            index += 1

    def send(begin):
        for direction in range(2):
            for lane in range(lanes):
                code = table[direction * span + now[0] * lanes + lane]

                @pl.when(code >= 0)
                def _(code=code, direction=direction, lane=lane):
                    copy = pltpu.make_async_copy(
                        pool.at[code], outgoing[direction].at[lane], sems.at[direction * lanes + lane]
                    )
                    copy.start() if begin else copy.wait()

    take_in(True)
    take_in(False)
    if sends:
        send(True)
        send(False)


def switch_round(plan, place, now, received, state, fresh, sends):
    table, slots = plan
    pool, out, stage = state
    parents = slots.shape[0]
    capacity = out.shape[1]
    receives = len(received)
    flat = [array for pair in received for array in pair]
    anywhere = pl.BlockSpec(memory_space=pl.ANY)
    lane_shape = jax.ShapeDtypeStruct((LANES,) + pool.shape[1:], jnp.float32)
    first = 4 + len(flat)
    results = pl.pallas_call(
        functools.partial(
            round_kernel, LANES, round_limit(parents), parents, capacity, receives, fresh, int(sends)
        ),
        grid_spec=pltpu.PrefetchScalarGridSpec(
            num_scalar_prefetch=4,
            grid=(),
            in_specs=[anywhere] * (len(flat) + 3),
            out_specs=[anywhere] * (3 + 2 * int(sends)),
            scratch_shapes=[pltpu.SemaphoreType.DMA((2 * LANES * max(receives, 1) + fresh,))],
        ),
        out_shape=[jax.ShapeDtypeStruct(array.shape, array.dtype) for array in state]
        + [lane_shape] * (2 * int(sends)),
        input_output_aliases={first: 0, first + 1: 1, first + 2: 2},
        name="switch_round",
    )(table, slots, place, now, *flat, *state)
    return tuple(results[:3]), tuple(results[3:])


def join_kernel(place, arrived, out_before, out, sem):
    copy = pltpu.make_async_copy(arrived, out.at[:, :, :, 1 - place[1]], sem)
    copy.start()
    copy.wait()


def join_cores(place, arrived, out):
    anywhere = pl.BlockSpec(memory_space=pl.ANY)
    return pl.pallas_call(
        join_kernel,
        grid_spec=pltpu.PrefetchScalarGridSpec(
            num_scalar_prefetch=1,
            grid=(),
            in_specs=[anywhere, anywhere],
            out_specs=anywhere,
            scratch_shapes=[pltpu.SemaphoreType.DMA],
        ),
        out_shape=jax.ShapeDtypeStruct(out.shape, out.dtype),
        input_output_aliases={2: 0},
        name="join_cores",
    )(place, arrived, out)


def along_line(value, chips, up):
    pairs = []
    for chip in range(chips - 1):
        for core in range(2):
            low, high = 2 * chip + core, 2 * (chip + 1) + core
            pairs.append((low, high) if up else (high, low))
    return lax.ppermute(value, "box", pairs)


def per_device(
    coeffs,
    skeleton_first,
    skeleton_second,
    skeleton_third,
    checks_first,
    checks_second,
    checks_third,
    ranks_first,
    ranks_second,
    ranks_third,
    interpolants,
    owners,
):
    tbit_index = lax.axis_index("tbit")
    box_index = lax.axis_index("box")
    box_count = lax.axis_size("box")
    parent_count = coeffs.shape[0]
    rank_width = coeffs.shape[3]
    capacity = 2 * parent_count // box_count
    group_count = 2 * box_count
    local_boxes = 2 * box_index + jnp.arange(2, dtype=jnp.int32)[None, :, None]

    def targets_of(checks, per_parent, picked, width):
        boxes = per_parent * parent_count
        absolute = jnp.arange(boxes, dtype=jnp.int32)[:, None] * (NPTS // boxes) + checks
        mine = lax.dynamic_index_in_dim(
            absolute.reshape(parent_count, -1, width), picked, 1, keepdims=False
        )
        return mine[:, :, None]

    def first_points(slot):
        box = 4 * local_boxes + 2 * (slot % 2) + slot // 2
        return box * (NPTS // (4 * group_count)) + pick_slot(skeleton_first, slot)

    def second_points(slot):
        box = 2 * local_boxes + slot % 2
        return box * (NPTS // (2 * group_count)) + pick_slot(skeleton_second, slot)

    partner_high = jnp.bitwise_xor(tbit_index, 2)
    partner_low = jnp.bitwise_xor(tbit_index, 1)
    points_first = jnp.concatenate([first_points(tbit_index), first_points(partner_high)], axis=2)
    points_second = jnp.concatenate([second_points(tbit_index), second_points(partner_low)], axis=2)
    points_third = (
        local_boxes * (NPTS // group_count) + pick_slot(skeleton_third, tbit_index)
    ).reshape(parent_count, 1, 2 * rank_width)
    targets_first = targets_of(checks_first, 2, tbit_index // 2, rank_width)
    targets_second = targets_of(checks_second, 4, tbit_index, rank_width)
    targets_third = targets_of(checks_third, 8, tbit_index, 2 * rank_width)
    rank_one = ranks_first.reshape(-1)
    rank_two = ranks_second.reshape(-1)
    rank_three = lax.dynamic_index_in_dim(
        lax.dynamic_index_in_dim(ranks_third, tbit_index, 1, keepdims=False),
        box_index,
        2,
        keepdims=False,
    ).reshape(-1)

    mine = coeffs[:, :, 0]
    count = parent_count // CHUNKS
    chips = box_count // 2
    networked = chips <= 4
    place = jnp.stack([box_index // 2, box_index % 2]).astype(jnp.int32)
    owner_row = lax.dynamic_index_in_dim(owners, tbit_index, 0, keepdims=False)
    width = coeffs.shape[-1]
    if networked:
        table, slots, rounds = plan_switch(owner_row, place, chips, capacity)
        pool_shape = (chips * parent_count, 2, rank_width, width)
    else:
        place = jnp.zeros_like(place)
        pool_shape = (parent_count, 2, rank_width, width)

    arrived = []
    for chunk in range(CHUNKS):
        outgoing = mine[chunk * count : (chunk + 1) * count]
        if chunk > 0:
            outgoing, _ = lax.optimization_barrier((outgoing, arrived[-1]))
        arrived.append(swapped(outgoing, "tbit", 1))

    second_arrived = []

    def levels(chunk, pool):
        first = first_level(
            chunk, count, rank_one, targets_first, points_first, interpolants[0], mine, arrived[chunk]
        )
        outgoing = first
        if chunk > 0:
            outgoing, _ = lax.optimization_barrier((outgoing, second_arrived[-1]))
        second_arrived.append(swapped(outgoing, "tbit", 0))
        return later_levels(
            chunk,
            count,
            (rank_two, rank_three),
            place,
            targets_second,
            points_second,
            targets_third,
            points_third,
            interpolants[1:],
            first,
            second_arrived[chunk],
            pool_shape,
            pool,
        )

    if not networked:
        pool = levels(0, ())
        for chunk in range(1, CHUNKS):
            pool = levels(chunk, (pool,))
        slot_parent, slot_used = slot_table(owner_row, box_count, capacity)
        outgoing = jnp.take(jnp.swapaxes(pool, 0, 1), slot_parent.T, axis=1)
        outgoing = jnp.where(slot_used.T[None, :, :, None, None], outgoing, 0.0)
        switched = lax.all_to_all(outgoing, "box", split_axis=2, concat_axis=2, tiled=True)
        return switched[None, None]

    out = jnp.zeros((2, capacity, chips, 2, rank_width, width), jnp.float32)
    stage = jnp.zeros((2, capacity, chips, rank_width, width), jnp.float32)
    state = (None, out, stage)
    plan = (table, slots)
    received = []

    def exchange(packed):
        return (along_line(packed[0], chips, True), along_line(packed[1], chips, False))

    for step in range(STATIC_ROUNDS):
        fresh = 0
        if step < CHUNKS:
            state = (levels(step, state[:1] if step else ()),) + state[1:]
            fresh = count
        now = jnp.full((1,), step, jnp.int32)
        oldest = received[step - LAG : step - LAG + 1] if step >= LAG else []
        state, packed = switch_round(plan, place, now, oldest, state, fresh, True)
        received.append(exchange(packed))

    most = jnp.maximum(lax.pmax(rounds[0], "tbit"), STATIC_ROUNDS)

    def more(carry):
        return carry[0] < most

    def again(carry):
        step, state, waiting = carry
        state, packed = switch_round(plan, place, step[None], waiting[:1], state, 0, True)
        return (step + 1, state, waiting[1:] + (exchange(packed),))

    step, state, waiting = lax.while_loop(
        more, again, (jnp.int32(STATIC_ROUNDS), state, tuple(received[-LAG:]))
    )
    state, _ = switch_round(plan, place, step[None], waiting, state, 0, False)
    _, out, stage = state
    crossed = lax.ppermute(stage, "box", [(box, box ^ 1) for box in range(box_count)])
    out = join_cores(place, crossed, out)
    return out.reshape(1, 1, 2, capacity, box_count, rank_width, width)


def solution(mesh):
    return jax.shard_map(
        per_device,
        mesh=mesh,
        in_specs=(
            P(None, "box", "tbit", None, None),
            P(None, "box", None, None),
            P(None, "box", None, None),
            P(None, "box", None, None),
            P(),
            P(),
            P(),
            P(None, "box", "tbit"),
            P(None, "box", "tbit"),
            P(),
            P(),
            P(),
        ),
        out_specs=P("tbit", "box", None, None, None, None, None),
        check_vma=False,
    )
```

```python
import functools
import math

import jax
import jax.numpy as jnp
from jax import lax
from jax.experimental import pallas as pl
from jax.experimental.pallas import tpu as pltpu
from jax.sharding import PartitionSpec as P

NPTS = 1048576
PHASE_BITS = 20
CHUNKS = 8
LANES = 8
LAG = 2
STATIC_ROUNDS = 12
PER_STEP = 4
VMEM_BYTES = 32 * 1024 * 1024
CODE_SHIFT = 16
SLOT_SHIFT = 16
POINTS_SECOND = 2
POINTS_THIRD = 4
TARGETS_LOW = 5
TARGETS_HIGH = 6

SIN_TERMS = (
    1.0,
    -1.0 / 6.0,
    1.0 / 120.0,
    -1.0 / 5040.0,
    1.0 / 362880.0,
    -1.0 / 39916800.0,
    1.0 / 6227020800.0,
)


def swapped(value, axis, bit):
    mask = 2**bit
    pairs = [(source, source ^ mask) for source in range(lax.axis_size(axis))]
    return lax.ppermute(value, axis, pairs)


def slot_table(owner_row, box_count, capacity):
    parent_count = owner_row.shape[0]
    onehot = (owner_row[:, None] == jnp.arange(box_count, dtype=jnp.int32)[None, :]).astype(
        jnp.int32
    )
    earlier = jnp.cumsum(onehot, axis=0, dtype=jnp.int32) - onehot
    slot_of = jnp.sum(earlier * onehot, axis=1, dtype=jnp.int32)
    matches = (onehot.T[:, None, :] == 1) & (
        slot_of[None, None, :] == jnp.arange(capacity, dtype=jnp.int32)[None, :, None]
    )
    slot_parent = jnp.sum(
        jnp.where(matches, jnp.arange(parent_count, dtype=jnp.int32)[None, None, :], 0), axis=2
    )
    slot_used = jnp.any(matches, axis=2)
    return (slot_parent, slot_used)


def pick_slot(values, position):
    return lax.dynamic_index_in_dim(values, position, 2, keepdims=False)


def cos_kernel(targets, points):
    shift = 32 - PHASE_BITS
    phase = lax.shift_right_arithmetic(
        lax.shift_left(targets * points, jnp.int32(shift)), jnp.int32(shift)
    )
    offset = NPTS // 4 - jnp.abs(phase)
    y = offset.astype(jnp.float32) * jnp.float32(2.0 * math.pi / NPTS)
    square = y * y
    total = jnp.float32(SIN_TERMS[-1])
    for term in SIN_TERMS[-2::-1]:
        total = total * square + jnp.float32(term)
    return total * y


def split(value):
    high = value.astype(jnp.bfloat16)
    low = (value - high.astype(jnp.float32)).astype(jnp.bfloat16)
    return high, low


def product(left, right):
    rows = left.shape[0]
    left_high, left_low = split(left)
    right_high, right_low = split(right)
    both = jnp.dot(
        jnp.concatenate([left_high, left_low], axis=0),
        right_high,
        preferred_element_type=jnp.float32,
    )
    rest = jnp.dot(left_high, right_low, preferred_element_type=jnp.float32)
    return both[:rows] + both[rows:] + rest


def live(weights, rank):
    rows = lax.broadcasted_iota(jnp.int32, weights.shape, 0)
    return jnp.where(rows < rank, weights, 0.0)


def column(tile, row, begin, length):
    return jnp.transpose(tile)[begin : begin + length, row : row + 1]


def pair_weights(matrix, left, right, left_rank, right_rank):
    width = left.shape[1]
    both = product(matrix, jnp.concatenate([left, right], axis=1))
    return live(both[:, :width], left_rank), live(both[:, width:], right_rank)


def first_kernel(chunk, ranks, points, matrix, mine, arrived, merged):
    step = pl.program_id(0)
    parents, boxes, rank_width = mine.shape[0], mine.shape[1], mine.shape[2]
    for parent in range(parents):
        row = (chunk * pl.num_programs(0) + step) * parents + parent
        tile = points[parent]
        targets = column(tile, TARGETS_LOW, 0, rank_width)
        kernels = [cos_kernel(targets, tile[box : box + 1]) for box in range(boxes)]
        weights = pair_weights(matrix[...], *kernels, ranks[row * boxes], ranks[row * boxes + 1])
        for box in range(boxes):
            stacked = jnp.concatenate([mine[parent, box], arrived[parent, box]], axis=0)
            merged[parent, box] = product(weights[box], stacked)


def later_kernel(chunk, ranks_second, ranks_third, place, points, matrices, mine, arrived, *pool):
    merged = pool[-1]
    step = pl.program_id(0)
    parents, boxes, rank_width = mine.shape[0], mine.shape[1], mine.shape[2]
    for parent in range(parents):
        row = (chunk * pl.num_programs(0) + step) * parents + parent
        tile = points[parent]
        targets = column(tile, TARGETS_LOW, rank_width, rank_width)
        kernels = [
            cos_kernel(targets, tile[POINTS_SECOND + box : POINTS_SECOND + box + 1])
            for box in range(boxes)
        ]
        weights = pair_weights(
            matrices[0], *kernels, ranks_second[row * boxes], ranks_second[row * boxes + 1]
        )
        seconds = []
        for box in range(boxes):
            stacked = jnp.concatenate([mine[parent, box], arrived[parent, box]], axis=0)
            seconds.append(product(weights[box], stacked))
        targets = column(tile, TARGETS_HIGH, 0, 2 * rank_width)
        kernel = cos_kernel(targets, tile[POINTS_THIRD : POINTS_THIRD + 1])
        weights = pair_weights(
            matrices[1],
            kernel[:rank_width],
            kernel[rank_width:],
            ranks_third[row * 2],
            ranks_third[row * 2 + 1],
        )
        third = product(jnp.concatenate(weights, axis=0), jnp.concatenate(seconds, axis=0))
        for child in range(2):
            merged[parent, child] = third[child * rank_width : (child + 1) * rank_width]


def chunk_spec(shape, chunk, steps, per_step):
    block = (per_step,) + tuple(shape[1:])
    rest = (0,) * (len(shape) - 1)
    return pl.BlockSpec(block, lambda step, *_: (chunk * steps + step,) + rest)


def whole_spec(shape):
    rest = (0,) * len(shape)
    return pl.BlockSpec(tuple(shape), lambda step, *_: rest)


def first_level(chunk, ranks, points, matrix, mine, arrived):
    per_step = PER_STEP
    steps = mine.shape[0] // per_step
    return pl.pallas_call(
        functools.partial(first_kernel, chunk),
        grid_spec=pltpu.PrefetchScalarGridSpec(
            num_scalar_prefetch=1,
            grid=(steps,),
            in_specs=[
                chunk_spec(points.shape, chunk, steps, per_step),
                whole_spec(matrix.shape),
                chunk_spec(mine.shape, 0, steps, per_step),
                chunk_spec(arrived.shape, 0, steps, per_step),
            ],
            out_specs=chunk_spec(arrived.shape, 0, steps, per_step),
        ),
        out_shape=jax.ShapeDtypeStruct(arrived.shape, jnp.float32),
        compiler_params=pltpu.CompilerParams(vmem_limit_bytes=VMEM_BYTES),
        name="first_level",
    )(ranks, points, matrix, mine, arrived)


def later_levels(chunk, ranks, place, points, matrices, mine, arrived, pool_shape, pool):
    per_step = PER_STEP
    steps = mine.shape[0] // per_step
    parents = points.shape[0]

    def pool_block(step, ranks_second, ranks_third, place):
        return (place[0] * (parents // per_step) + chunk * steps + step, 0, 0, 0)

    return pl.pallas_call(
        functools.partial(later_kernel, chunk),
        grid_spec=pltpu.PrefetchScalarGridSpec(
            num_scalar_prefetch=3,
            grid=(steps,),
            in_specs=[
                chunk_spec(points.shape, chunk, steps, per_step),
                whole_spec(matrices.shape),
                chunk_spec(mine.shape, 0, steps, per_step),
                chunk_spec(arrived.shape, 0, steps, per_step),
            ]
            + [pl.BlockSpec(memory_space=pl.ANY)] * len(pool),
            out_specs=pl.BlockSpec((per_step,) + pool_shape[1:], pool_block),
        ),
        out_shape=jax.ShapeDtypeStruct(pool_shape, jnp.float32),
        input_output_aliases={7: 0} if pool else {},
        compiler_params=pltpu.CompilerParams(vmem_limit_bytes=VMEM_BYTES),
        name="later_levels",
    )(ranks[0], ranks[1], place, points, matrices, mine, arrived, *pool)


def plan_kernel(chips, limit, chunks, owners, table, counts, slots, rounds, own, ahead, used):
    parents = owners.shape[0]
    count = parents // chunks
    rows = chips + 1
    span = limit * LANES

    def clear(index, carry):
        counts[index] = 0
        return carry

    lax.fori_loop(0, 2 * rows * limit, clear, 0)
    for box in range(2 * chips):
        used[box] = 0

    def take_slot(parent, carry):
        owner = owners[parent]
        slot = used[owner]
        slots[parent] = (owner << SLOT_SHIFT) | slot
        used[owner] = slot + 1
        return carry

    lax.fori_loop(0, parents, take_slot, 0)
    width = chips * parents
    pairs = [(chip, goal) for chip in range(1, chips) for goal in range(chip + 1, chips)]
    last = []
    for direction in range(2):

        def true_chip(chip):
            return chip if direction == 0 else chips - 1 - chip

        total = 0
        for box in range(2 * chips):
            hops = true_chip(box // 2)
            total = total + used[box] * (hops * (hops + 1) // 2)

        def one_round(state):
            step, left, ready, own_head, head, tail, older = state
            ready, own_head, head, tail = list(ready), list(own_head), list(head), list(tail)
            for index in range(count):
                parent = jnp.minimum(step * count + index, parents - 1)
                goal = owners[parent] >> 1
                goal = goal if direction == 0 else chips - 1 - goal
                for chip in range(1, chips):
                    own[chip * parents + jnp.minimum(ready[chip], parents - 1)] = parent
                    here = (goal == chip) & (step < chunks)
                    ready[chip] = ready[chip] + here.astype(jnp.int32)
            seen = older[0]
            for chip in range(chips - 1):
                row = (direction * rows + 1 + chip) * limit + step
                sent = jnp.int32(0)
                for goal in range(chips - 1, chip, -1):
                    onward = pairs.index((chip + 1, goal)) if (chip + 1, goal) in pairs else None
                    for forwarded in (True, False):
                        if forwarded and (chip, goal) not in pairs:
                            continue
                        if forwarded:
                            queue = pairs.index((chip, goal))
                            start, stop = head[queue], seen[queue]
                        else:
                            queue = chip * chips + goal
                            start, stop = own_head[queue], ready[goal]
                        number = jnp.minimum(stop - start, LANES - sent)

                        def move(index, carry):
                            if forwarded:
                                code = ahead[queue * width + start + index]
                            else:
                                code = own[goal * parents + start + index]
                                code = code | (true_chip(chip) << CODE_SHIFT)
                            table[row * LANES + sent + index] = code
                            if onward is not None:
                                ahead[onward * width + tail[onward] + index] = code
                            return carry

                        lax.fori_loop(0, number, move, 0)
                        sent = sent + number
                        if onward is not None:
                            tail[onward] = tail[onward] + number
                        if forwarded:
                            head[queue] = start + number
                        else:
                            own_head[queue] = start + number
                counts[row] = sent
                left = left - sent
            return (
                step + 1,
                left,
                tuple(ready),
                tuple(own_head),
                tuple(head),
                tuple(tail),
                tuple(older[1:]) + (tuple(tail),),
            )

        zero = jnp.int32(0)
        none = (zero,) * len(pairs)
        state = lax.while_loop(
            lambda state: (state[1] > 0) & (state[0] < limit),
            one_round,
            (zero, jnp.int32(total), (zero,) * chips, (zero,) * (chips * chips), none, none, (none,) * LAG),
        )
        last.append(state[0])
    rounds[0] = jnp.maximum(last[0], last[1])


def plan_switch(owner_row, chips):
    parents = owner_row.shape[0]
    limit = round_limit(parents)
    smem = pl.BlockSpec(memory_space=pltpu.SMEM)
    return pl.pallas_call(
        functools.partial(plan_kernel, chips, limit, CHUNKS),
        in_specs=[smem],
        out_specs=[smem] * 4,
        out_shape=[
            jax.ShapeDtypeStruct((2 * (chips + 1) * limit * LANES,), jnp.int32),
            jax.ShapeDtypeStruct((2 * (chips + 1) * limit,), jnp.int32),
            jax.ShapeDtypeStruct((parents,), jnp.int32),
            jax.ShapeDtypeStruct((1,), jnp.int32),
        ],
        scratch_shapes=[
            pltpu.SMEM((chips * parents,), jnp.int32),
            pltpu.SMEM((chips * chips * chips * parents,), jnp.int32),
            pltpu.SMEM((2 * chips,), jnp.int32),
        ],
        name="plan_switch",
    )(owner_row)


def round_limit(parents):
    return 5 * parents // LANES


def round_kernel(chips, limit, parents, receives, fresh, sends, table, counts, slots, place, now, *refs):
    received = refs[: 2 * receives]
    refs = refs[2 * receives + 3 :]
    pool, out, stage = refs[:3]
    outgoing = refs[3 : 3 + 2 * sends]
    kept, sems = refs[-2:]
    z, core = place[0], place[1]
    spots = (z, chips - 1 - z)

    def home(sem, from_chip, parent, source, begin):
        spot = slots[parent]
        owner, slot = spot >> SLOT_SHIFT, spot & ((1 << SLOT_SHIFT) - 1)
        here = (owner >> 1) == z
        same = (owner & 1) == core

        @pl.when(here & same)
        def _():
            copy = pltpu.make_async_copy(source, out.at[:, slot, from_chip, core], sem)
            copy.start() if begin else copy.wait()

        @pl.when(here & jnp.logical_not(same))
        def _():
            copy = pltpu.make_async_copy(source, stage.at[:, slot, from_chip], sem)
            copy.start() if begin else copy.wait()

        return here

    def of_code(code):
        from_chip, parent = code >> CODE_SHIFT, code & ((1 << CODE_SHIFT) - 1)
        return from_chip, parent, from_chip * parents + parent

    def take_in(begin):
        for back in range(receives):
            for direction in range(2):
                step = now[0] - LAG + back
                row = (direction * (chips + 1) + spots[direction]) * limit + jnp.maximum(step, 0)
                number = jnp.where(step >= 0, counts[row], 0)
                base = (2 * back + direction) * LANES

                def one(lane, carry):
                    from_chip, parent, held = of_code(table[row * LANES + lane])
                    source = received[2 * back + direction].at[lane]
                    sem = sems.at[base + lane]
                    here = home(sem, from_chip, parent, source, begin)

                    @pl.when(jnp.logical_not(here))
                    def _():
                        copy = pltpu.make_async_copy(source, pool.at[held], sem)
                        copy.start() if begin else copy.wait()

                    return carry

                lax.fori_loop(0, number, one, 0)

    def send(begin):
        for direction in range(2):
            row = (direction * (chips + 1) + 1 + spots[direction]) * limit + now[0]

            def one(lane, carry):
                _, _, held = of_code(table[row * LANES + lane])
                copy = pltpu.make_async_copy(
                    pool.at[held], outgoing[direction].at[lane], sems.at[direction * LANES + lane]
                )
                copy.start() if begin else copy.wait()
                return carry

            lax.fori_loop(0, counts[row], one, 0)

    def keep(begin):
        def one(member, carry):
            parent = now[0] * fresh + member
            home(sems.at[2 * LANES * max(receives, 1) + member], z, parent, kept.at[member], begin)
            return carry

        lax.fori_loop(0, fresh, one, 0)

    if fresh:
        load = pltpu.make_async_copy(
            pool.at[pl.ds(z * parents + now[0] * fresh, fresh)], kept, sems.at[2 * LANES * max(receives, 1) + fresh]
        )
        load.start()
    take_in(True)
    if fresh:
        load.wait()
        keep(True)
    take_in(False)
    if sends:
        send(True)
    if fresh:
        keep(False)
    if sends:
        send(False)


def switch_round(plan, place, now, received, state, fresh, sends):
    table, counts, slots = plan
    pool, out, stage = state
    parents = slots.shape[0]
    chips = out.shape[2]
    receives = len(received)
    flat = [array for pair in received for array in pair]
    anywhere = pl.BlockSpec(memory_space=pl.ANY)
    inside = pl.BlockSpec(memory_space=pltpu.VMEM)
    lane_shape = jax.ShapeDtypeStruct((LANES,) + pool.shape[1:], jnp.float32)
    first = 5 + len(flat)
    results = pl.pallas_call(
        functools.partial(
            round_kernel, chips, round_limit(parents), parents, receives, fresh, int(sends)
        ),
        grid_spec=pltpu.PrefetchScalarGridSpec(
            num_scalar_prefetch=5,
            grid=(),
            in_specs=[inside] * len(flat) + [anywhere] * 3,
            out_specs=[anywhere] * 3 + [inside] * (2 * int(sends)),
            scratch_shapes=[
                pltpu.VMEM((max(fresh, 1),) + pool.shape[1:], jnp.float32),
                pltpu.SemaphoreType.DMA((2 * LANES * max(receives, 1) + fresh + 1,)),
            ],
        ),
        out_shape=[jax.ShapeDtypeStruct(array.shape, array.dtype) for array in state]
        + [lane_shape] * (2 * int(sends)),
        input_output_aliases={first: 0, first + 1: 1, first + 2: 2},
        compiler_params=pltpu.CompilerParams(vmem_limit_bytes=VMEM_BYTES),
        name="switch_round",
    )(table, counts, slots, place, now, *flat, *state)
    return tuple(results[:3]), tuple(results[3:])


def join_kernel(place, arrived, out_before, out):
    for child in range(2):
        for chip in range(arrived.shape[2]):
            out[child, 0, chip, 0] = arrived[child, 0, chip]


def join_cores(place, arrived, out):
    children, capacity, chips, _, rank_width, width = out.shape
    return pl.pallas_call(
        join_kernel,
        grid_spec=pltpu.PrefetchScalarGridSpec(
            num_scalar_prefetch=1,
            grid=(capacity,),
            in_specs=[
                pl.BlockSpec(
                    (children, 1, chips, rank_width, width), lambda slot, place: (0, slot, 0, 0, 0)
                ),
                pl.BlockSpec(memory_space=pl.ANY),
            ],
            out_specs=pl.BlockSpec(
                (children, 1, chips, 1, rank_width, width),
                lambda slot, place: (0, slot, 0, 1 - place[1], 0, 0),
            ),
        ),
        out_shape=jax.ShapeDtypeStruct(out.shape, out.dtype),
        input_output_aliases={2: 0},
        compiler_params=pltpu.CompilerParams(vmem_limit_bytes=VMEM_BYTES),
        name="join_cores",
    )(place, arrived, out)


def along_line(value, chips, up):
    pairs = []
    for chip in range(chips - 1):
        for core in range(2):
            low, high = 2 * chip + core, 2 * (chip + 1) + core
            pairs.append((low, high) if up else (high, low))
    return lax.ppermute(value, "box", pairs)


def per_device(
    coeffs,
    skeleton_first,
    skeleton_second,
    skeleton_third,
    checks_first,
    checks_second,
    checks_third,
    ranks_first,
    ranks_second,
    ranks_third,
    interpolants,
    owners,
):
    tbit_index = lax.axis_index("tbit")
    box_index = lax.axis_index("box")
    box_count = lax.axis_size("box")
    parent_count = coeffs.shape[0]
    rank_width = coeffs.shape[3]
    capacity = 2 * parent_count // box_count
    group_count = 2 * box_count
    local_boxes = 2 * box_index + jnp.arange(2, dtype=jnp.int32)[None, :, None]

    def targets_of(checks, per_parent, picked, width):
        boxes = per_parent * parent_count
        absolute = jnp.arange(boxes, dtype=jnp.int32)[:, None] * (NPTS // boxes) + checks
        return lax.dynamic_index_in_dim(absolute.reshape(parent_count, -1, width), picked, 1)

    def first_points(slot):
        box = 4 * local_boxes + 2 * (slot % 2) + slot // 2
        return box * (NPTS // (4 * group_count)) + pick_slot(skeleton_first, slot)

    def second_points(slot):
        box = 2 * local_boxes + slot % 2
        return box * (NPTS // (2 * group_count)) + pick_slot(skeleton_second, slot)

    partner_high = jnp.bitwise_xor(tbit_index, 2)
    partner_low = jnp.bitwise_xor(tbit_index, 1)
    points_third = local_boxes * (NPTS // group_count) + pick_slot(skeleton_third, tbit_index)
    low_targets = jnp.concatenate(
        [
            targets_of(checks_first, 2, tbit_index // 2, rank_width),
            targets_of(checks_second, 4, tbit_index, rank_width),
        ],
        axis=2,
    )
    high_targets = targets_of(checks_third, 8, tbit_index, 2 * rank_width)
    points = jnp.concatenate(
        [
            jnp.concatenate([first_points(tbit_index), first_points(partner_high)], axis=2),
            jnp.concatenate([second_points(tbit_index), second_points(partner_low)], axis=2),
            points_third.reshape(parent_count, 1, 2 * rank_width),
            low_targets,
            high_targets,
            jnp.zeros_like(high_targets),
        ],
        axis=1,
    )
    rank_one = ranks_first.reshape(-1)
    rank_two = ranks_second.reshape(-1)
    rank_three = lax.dynamic_index_in_dim(
        lax.dynamic_index_in_dim(ranks_third, tbit_index, 1, keepdims=False),
        box_index,
        2,
        keepdims=False,
    ).reshape(-1)

    mine = coeffs[:, :, 0]
    count = parent_count // CHUNKS
    chips = box_count // 2
    networked = chips <= 4
    place = jnp.stack([box_index // 2, box_index % 2]).astype(jnp.int32)
    owner_row = lax.dynamic_index_in_dim(owners, tbit_index, 0, keepdims=False)
    width = coeffs.shape[-1]
    pool_shape = (chips * parent_count, 2, rank_width, width)
    if not networked:
        place = jnp.zeros_like(place)
        pool_shape = (parent_count, 2, rank_width, width)

    parts, arrived = [], []
    for chunk in range(CHUNKS):
        source = mine
        if chunk > 0:
            source, _ = lax.optimization_barrier((mine, arrived[-1]))
        parts.append(source[chunk * count : (chunk + 1) * count])
        arrived.append(swapped(parts[-1], "tbit", 1))

    if networked:
        *plan, rounds = plan_switch(owner_row, chips)
        out = jnp.zeros((2, capacity, chips, 2, rank_width, width), jnp.float32)
        stage = jnp.zeros((2, capacity, chips, rank_width, width), jnp.float32)
        arrived[0], points, plan, rounds, out, stage = lax.optimization_barrier(
            (arrived[0], points, plan, rounds, out, stage)
        )
        most = jnp.broadcast_to(rounds, (8, 128))
        most = jnp.maximum(most, swapped(most, "tbit", 1))
        most = jnp.maximum(most, swapped(most, "tbit", 0))
        most = jnp.maximum(most[0, 0], STATIC_ROUNDS)
        arrived[2], most = lax.optimization_barrier((arrived[2], most))

    second_arrived = []

    def levels(chunk, pool):
        first = first_level(chunk, rank_one, points, interpolants[0], parts[chunk], arrived[chunk])
        outgoing = first
        if chunk > 0:
            outgoing, _ = lax.optimization_barrier((outgoing, second_arrived[-1]))
        second_arrived.append(swapped(outgoing, "tbit", 0))
        return later_levels(
            chunk,
            (rank_two, rank_three),
            place,
            points,
            interpolants[1:],
            first,
            second_arrived[chunk],
            pool_shape,
            pool,
        )

    if not networked:
        pool = levels(0, ())
        for chunk in range(1, CHUNKS):
            pool = levels(chunk, (pool,))
        slot_parent, slot_used = slot_table(owner_row, box_count, capacity)
        outgoing = jnp.take(jnp.swapaxes(pool, 0, 1), slot_parent.T, axis=1)
        outgoing = jnp.where(slot_used.T[None, :, :, None, None], outgoing, 0.0)
        switched = lax.all_to_all(outgoing, "box", split_axis=2, concat_axis=2, tiled=True)
        return switched[None, None]

    state = (None, out, stage)
    received = []

    def exchange(packed):
        return (along_line(packed[0], chips, True), along_line(packed[1], chips, False))

    for step in range(STATIC_ROUNDS):
        fresh = 0
        if step < CHUNKS:
            state = (levels(step, state[:1] if step else ()),) + state[1:]
            fresh = count
        now = jnp.full((1,), step, jnp.int32)
        oldest = received[step - LAG : step - LAG + 1] if step >= LAG else []
        state, packed = switch_round(plan, place, now, oldest, state, fresh, True)
        received.append(exchange(packed))

    def more(carry):
        return carry[0] < most

    def again(carry):
        step, state, waiting = carry
        state, packed = switch_round(plan, place, step[None], waiting[:1], state, 0, True)
        return (step + 1, state, waiting[1:] + (exchange(packed),))

    step, state, waiting = lax.while_loop(
        more, again, (jnp.int32(STATIC_ROUNDS), state, tuple(received[-LAG:]))
    )
    state, _ = switch_round(plan, place, step[None], waiting, state, 0, False)
    _, out, stage = state
    crossed = lax.ppermute(stage, "box", [(box, box ^ 1) for box in range(box_count)])
    out = join_cores(place, crossed, out)
    return out.reshape(1, 1, 2, capacity, box_count, rank_width, width)


def solution(mesh):
    return jax.shard_map(
        per_device,
        mesh=mesh,
        in_specs=(
            P(None, "box", "tbit", None, None),
            P(None, "box", None, None),
            P(None, "box", None, None),
            P(None, "box", None, None),
            P(),
            P(),
            P(),
            P(None, "box", "tbit"),
            P(None, "box", "tbit"),
            P(),
            P(),
            P(),
        ),
        out_specs=P("tbit", "box", None, None, None, None, None),
        check_vma=False,
    )
```

```python
import functools
import math

import jax
import jax.numpy as jnp
from jax import lax
from jax.experimental import pallas as pl
from jax.experimental.pallas import tpu as pltpu
from jax.sharding import PartitionSpec as P

NPTS = 1048576
PHASE_BITS = 20
CHUNKS = 16
LANES = 4
LAG = 2
STATIC_ROUNDS = 22
PER_STEP = 4
VMEM_BYTES = 32 * 1024 * 1024
CODE_SHIFT = 16
SLOT_SHIFT = 16
POINTS_SECOND = 2
POINTS_THIRD = 4
TARGETS_LOW = 5
TARGETS_HIGH = 6

SIN_TERMS = (
    1.0,
    -1.0 / 6.0,
    1.0 / 120.0,
    -1.0 / 5040.0,
    1.0 / 362880.0,
    -1.0 / 39916800.0,
    1.0 / 6227020800.0,
)


def swapped(value, axis, bit):
    mask = 2**bit
    pairs = [(source, source ^ mask) for source in range(lax.axis_size(axis))]
    return lax.ppermute(value, axis, pairs)


def slot_table(owner_row, box_count, capacity):
    parent_count = owner_row.shape[0]
    onehot = (owner_row[:, None] == jnp.arange(box_count, dtype=jnp.int32)[None, :]).astype(
        jnp.int32
    )
    earlier = jnp.cumsum(onehot, axis=0, dtype=jnp.int32) - onehot
    slot_of = jnp.sum(earlier * onehot, axis=1, dtype=jnp.int32)
    matches = (onehot.T[:, None, :] == 1) & (
        slot_of[None, None, :] == jnp.arange(capacity, dtype=jnp.int32)[None, :, None]
    )
    slot_parent = jnp.sum(
        jnp.where(matches, jnp.arange(parent_count, dtype=jnp.int32)[None, None, :], 0), axis=2
    )
    slot_used = jnp.any(matches, axis=2)
    return (slot_parent, slot_used)


def pick_slot(values, position):
    return lax.dynamic_index_in_dim(values, position, 2, keepdims=False)


def cos_kernel(targets, points):
    shift = 32 - PHASE_BITS
    phase = lax.shift_right_arithmetic(
        lax.shift_left(targets * points, jnp.int32(shift)), jnp.int32(shift)
    )
    offset = NPTS // 4 - jnp.abs(phase)
    y = offset.astype(jnp.float32) * jnp.float32(2.0 * math.pi / NPTS)
    square = y * y
    total = jnp.float32(SIN_TERMS[-1])
    for term in SIN_TERMS[-2::-1]:
        total = total * square + jnp.float32(term)
    return total * y


def split(value):
    high = value.astype(jnp.bfloat16)
    low = (value - high.astype(jnp.float32)).astype(jnp.bfloat16)
    return high, low


def stack_left(value):
    high, low = split(value)
    return jnp.concatenate(
        [jnp.concatenate([high, high], axis=1), jnp.concatenate([low, low], axis=1)], axis=0
    )


def product(left, right):
    rows = left.shape[0] // 2
    both = jnp.dot(
        left, jnp.concatenate(split(right), axis=0), preferred_element_type=jnp.float32
    )
    return both[:rows] + both[rows:]


def live(weights, rank):
    rows = lax.broadcasted_iota(jnp.int32, weights.shape, 0)
    return jnp.where(rows < rank, weights, 0.0)


def column(tile, row, begin, length):
    return jnp.transpose(tile)[begin : begin + length, row : row + 1]


def pair_weights(matrix, left, right, left_rank, right_rank):
    width = left.shape[1]
    both = product(matrix, jnp.concatenate([left, right], axis=1))
    return live(both[:, :width], left_rank), live(both[:, width:], right_rank)


def first_kernel(chunk, ranks, points, matrix, mine, arrived, merged):
    step = pl.program_id(0)
    parents, boxes, rank_width = mine.shape[0], mine.shape[1], mine.shape[2]
    for parent in range(parents):
        row = (chunk * pl.num_programs(0) + step) * parents + parent
        tile = points[parent]
        targets = column(tile, TARGETS_LOW, 0, rank_width)
        kernels = [cos_kernel(targets, tile[box : box + 1]) for box in range(boxes)]
        weights = pair_weights(matrix[...], *kernels, ranks[row * boxes], ranks[row * boxes + 1])
        for box in range(boxes):
            stacked = jnp.concatenate([mine[parent, box], arrived[parent, box]], axis=0)
            merged[parent, box] = product(stack_left(weights[box]), stacked)


def later_kernel(chunk, ranks_second, ranks_third, place, points, matrices, mine, arrived, *pool):
    merged = pool[-1]
    step = pl.program_id(0)
    parents, boxes, rank_width = mine.shape[0], mine.shape[1], mine.shape[2]
    for parent in range(parents):
        row = (chunk * pl.num_programs(0) + step) * parents + parent
        tile = points[parent]
        targets = column(tile, TARGETS_LOW, rank_width, rank_width)
        kernels = [
            cos_kernel(targets, tile[POINTS_SECOND + box : POINTS_SECOND + box + 1])
            for box in range(boxes)
        ]
        weights = pair_weights(
            matrices[0], *kernels, ranks_second[row * boxes], ranks_second[row * boxes + 1]
        )
        seconds = []
        for box in range(boxes):
            stacked = jnp.concatenate([mine[parent, box], arrived[parent, box]], axis=0)
            seconds.append(product(stack_left(weights[box]), stacked))
        targets = column(tile, TARGETS_HIGH, 0, 2 * rank_width)
        kernel = cos_kernel(targets, tile[POINTS_THIRD : POINTS_THIRD + 1])
        weights = pair_weights(
            matrices[1],
            kernel[:rank_width],
            kernel[rank_width:],
            ranks_third[row * 2],
            ranks_third[row * 2 + 1],
        )
        stacked = jnp.concatenate(seconds, axis=0)
        third = product(stack_left(jnp.concatenate(weights, axis=0)), stacked)
        for child in range(2):
            merged[parent, child] = third[child * rank_width : (child + 1) * rank_width]


def chunk_spec(shape, chunk, steps, per_step):
    block = (per_step,) + tuple(shape[1:])
    rest = (0,) * (len(shape) - 1)
    return pl.BlockSpec(block, lambda step, *_: (chunk * steps + step,) + rest)


def whole_spec(shape):
    rest = (0,) * len(shape)
    return pl.BlockSpec(tuple(shape), lambda step, *_: rest)


def first_level(chunk, ranks, points, matrix, mine, arrived):
    per_step = PER_STEP
    steps = mine.shape[0] // per_step
    return pl.pallas_call(
        functools.partial(first_kernel, chunk),
        grid_spec=pltpu.PrefetchScalarGridSpec(
            num_scalar_prefetch=1,
            grid=(steps,),
            in_specs=[
                chunk_spec(points.shape, chunk, steps, per_step),
                whole_spec(matrix.shape),
                chunk_spec(mine.shape, 0, steps, per_step),
                chunk_spec(arrived.shape, 0, steps, per_step),
            ],
            out_specs=chunk_spec(arrived.shape, 0, steps, per_step),
        ),
        out_shape=jax.ShapeDtypeStruct(arrived.shape, jnp.float32),
        compiler_params=pltpu.CompilerParams(vmem_limit_bytes=VMEM_BYTES),
        name="first_level",
    )(ranks, points, matrix, mine, arrived)


def later_levels(chunk, ranks, place, points, matrices, mine, arrived, pool_shape, pool):
    per_step = PER_STEP
    steps = mine.shape[0] // per_step
    parents = points.shape[0]

    def pool_block(step, ranks_second, ranks_third, place):
        return (place[0] * (parents // per_step) + chunk * steps + step, 0, 0, 0)

    return pl.pallas_call(
        functools.partial(later_kernel, chunk),
        grid_spec=pltpu.PrefetchScalarGridSpec(
            num_scalar_prefetch=3,
            grid=(steps,),
            in_specs=[
                chunk_spec(points.shape, chunk, steps, per_step),
                whole_spec(matrices.shape),
                chunk_spec(mine.shape, 0, steps, per_step),
                chunk_spec(arrived.shape, 0, steps, per_step),
            ]
            + [pl.BlockSpec(memory_space=pl.ANY)] * len(pool),
            out_specs=pl.BlockSpec((per_step,) + pool_shape[1:], pool_block),
        ),
        out_shape=jax.ShapeDtypeStruct(pool_shape, jnp.float32),
        input_output_aliases={7: 0} if pool else {},
        compiler_params=pltpu.CompilerParams(vmem_limit_bytes=VMEM_BYTES),
        name="later_levels",
    )(ranks[0], ranks[1], place, points, matrices, mine, arrived, *pool)


def plan_kernel(chips, limit, chunks, owners, table, counts, slots, rounds, own, ahead, used):
    parents = owners.shape[0]
    count = parents // chunks
    rows = chips + 1
    span = limit * LANES

    def clear(index, carry):
        counts[index] = 0
        return carry

    lax.fori_loop(0, 2 * rows * limit, clear, 0)
    for box in range(2 * chips):
        used[box] = 0

    def take_slot(parent, carry):
        owner = owners[parent]
        slot = used[owner]
        slots[parent] = (owner << SLOT_SHIFT) | slot
        used[owner] = slot + 1
        return carry

    lax.fori_loop(0, parents, take_slot, 0)
    width = chips * parents
    pairs = [(chip, goal) for chip in range(1, chips) for goal in range(chip + 1, chips)]
    last = []
    for direction in range(2):

        def true_chip(chip):
            return chip if direction == 0 else chips - 1 - chip

        total = 0
        for box in range(2 * chips):
            hops = true_chip(box // 2)
            total = total + used[box] * (hops * (hops + 1) // 2)

        def one_round(state):
            step, left, ready, own_head, head, tail, older = state
            ready, own_head, head, tail = list(ready), list(own_head), list(head), list(tail)
            for index in range(count):
                parent = jnp.minimum(step * count + index, parents - 1)
                goal = owners[parent] >> 1
                goal = goal if direction == 0 else chips - 1 - goal
                for chip in range(1, chips):
                    own[chip * parents + jnp.minimum(ready[chip], parents - 1)] = parent
                    here = (goal == chip) & (step < chunks)
                    ready[chip] = ready[chip] + here.astype(jnp.int32)
            seen = older[0]
            for chip in range(chips - 1):
                row = (direction * rows + 1 + chip) * limit + step
                sent = jnp.int32(0)
                for goal in range(chips - 1, chip, -1):
                    onward = pairs.index((chip + 1, goal)) if (chip + 1, goal) in pairs else None
                    for forwarded in (True, False):
                        if forwarded and (chip, goal) not in pairs:
                            continue
                        if forwarded:
                            queue = pairs.index((chip, goal))
                            start, stop = head[queue], seen[queue]
                        else:
                            queue = chip * chips + goal
                            start, stop = own_head[queue], ready[goal]
                        number = jnp.minimum(stop - start, LANES - sent)

                        def move(index, carry):
                            if forwarded:
                                code = ahead[queue * width + start + index]
                            else:
                                code = own[goal * parents + start + index]
                                code = code | (true_chip(chip) << CODE_SHIFT)
                            table[row * LANES + sent + index] = code
                            if onward is not None:
                                ahead[onward * width + tail[onward] + index] = code
                            return carry

                        lax.fori_loop(0, number, move, 0)
                        sent = sent + number
                        if onward is not None:
                            tail[onward] = tail[onward] + number
                        if forwarded:
                            head[queue] = start + number
                        else:
                            own_head[queue] = start + number
                counts[row] = sent
                left = left - sent
            return (
                step + 1,
                left,
                tuple(ready),
                tuple(own_head),
                tuple(head),
                tuple(tail),
                tuple(older[1:]) + (tuple(tail),),
            )

        zero = jnp.int32(0)
        none = (zero,) * len(pairs)
        state = lax.while_loop(
            lambda state: (state[1] > 0) & (state[0] < limit),
            one_round,
            (zero, jnp.int32(total), (zero,) * chips, (zero,) * (chips * chips), none, none, (none,) * LAG),
        )
        last.append(state[0])
    rounds[0] = jnp.maximum(last[0], last[1])


def plan_switch(owner_row, chips):
    parents = owner_row.shape[0]
    limit = round_limit(parents)
    smem = pl.BlockSpec(memory_space=pltpu.SMEM)
    return pl.pallas_call(
        functools.partial(plan_kernel, chips, limit, CHUNKS),
        in_specs=[smem],
        out_specs=[smem] * 4,
        out_shape=[
            jax.ShapeDtypeStruct((2 * (chips + 1) * limit * LANES,), jnp.int32),
            jax.ShapeDtypeStruct((2 * (chips + 1) * limit,), jnp.int32),
            jax.ShapeDtypeStruct((parents,), jnp.int32),
            jax.ShapeDtypeStruct((1,), jnp.int32),
        ],
        scratch_shapes=[
            pltpu.SMEM((chips * parents,), jnp.int32),
            pltpu.SMEM((chips * chips * chips * parents,), jnp.int32),
            pltpu.SMEM((2 * chips,), jnp.int32),
        ],
        name="plan_switch",
    )(owner_row)


def round_limit(parents):
    return 4 * parents // LANES


def round_kernel(
    chips, limit, parents, receives, crossings, staging, fresh, sends, table, counts, slots, place, now, *refs
):
    sources = receives + crossings
    received = refs[: 2 * len(sources)]
    refs = refs[2 * len(sources) + 3 :]
    pool, out, stage = refs[:3]
    outgoing = refs[3 : 3 + 2 * sends]
    kept, sems = refs[-2:]
    z, core = place[0], place[1]
    spots = (z, chips - 1 - z)

    def home(sem, from_chip, parent, source, begin, crossed=False):
        spot = slots[parent]
        owner, slot = spot >> SLOT_SHIFT, spot & ((1 << SLOT_SHIFT) - 1)
        here = (owner >> 1) == z
        same = (owner & 1) == core

        @pl.when(here & same)
        def _():
            from_core = 1 - core if crossed else core
            copy = pltpu.make_async_copy(source, out.at[:, slot, from_chip, from_core], sem)
            copy.start() if begin else copy.wait()

        if staging and not crossed:

            @pl.when(here & jnp.logical_not(same))
            def _():
                copy = pltpu.make_async_copy(source, stage.at[:, slot, from_chip], sem)
                copy.start() if begin else copy.wait()

        return here

    def of_code(code):
        from_chip, parent = code >> CODE_SHIFT, code & ((1 << CODE_SHIFT) - 1)
        return from_chip, parent, from_chip * parents + parent

    def take_in(begin):
        for place_of, back in enumerate(sources):
            crossed = place_of >= len(receives)
            for direction in range(2):
                step = now[0] - back
                row = (direction * (chips + 1) + spots[direction]) * limit + jnp.maximum(step, 0)
                number = jnp.where(step >= 0, counts[row], 0)
                base = (2 * place_of + direction) * LANES

                def one(lane, carry):
                    from_chip, parent, held = of_code(table[row * LANES + lane])
                    source = received[2 * place_of + direction].at[lane]
                    sem = sems.at[base + lane]
                    here = home(sem, from_chip, parent, source, begin, crossed)
                    if not crossed:

                        @pl.when(jnp.logical_not(here))
                        def _():
                            copy = pltpu.make_async_copy(source, pool.at[held], sem)
                            copy.start() if begin else copy.wait()

                    return carry

                lax.fori_loop(0, number, one, 0)

    def send(begin):
        for direction in range(2):
            row = (direction * (chips + 1) + 1 + spots[direction]) * limit + now[0]

            def one(lane, carry):
                _, _, held = of_code(table[row * LANES + lane])
                copy = pltpu.make_async_copy(
                    pool.at[held], outgoing[direction].at[lane], sems.at[direction * LANES + lane]
                )
                copy.start() if begin else copy.wait()
                return carry

            lax.fori_loop(0, counts[row], one, 0)

    def keep(begin):
        def one(member, carry):
            parent = now[0] * fresh + member
            home(sems.at[2 * LANES * max(len(sources), 1) + member], z, parent, kept.at[member], begin)
            return carry

        lax.fori_loop(0, fresh, one, 0)

    if fresh:
        load = pltpu.make_async_copy(
            pool.at[pl.ds(z * parents + now[0] * fresh, fresh)], kept, sems.at[2 * LANES * max(len(sources), 1) + fresh]
        )
        load.start()
    take_in(True)
    if fresh:
        load.wait()
        keep(True)
    take_in(False)
    if sends:
        send(True)
    if fresh:
        keep(False)
    if sends:
        send(False)


def switch_round(plan, place, now, received, crossed, state, staging, fresh, sends):
    table, counts, slots = plan
    pool, out, stage = state
    parents = slots.shape[0]
    chips = out.shape[2]
    flat = [array for pair in [*received.values(), *crossed.values()] for array in pair]
    anywhere = pl.BlockSpec(memory_space=pl.ANY)
    inside = pl.BlockSpec(memory_space=pltpu.VMEM)
    lane_shape = jax.ShapeDtypeStruct((LANES,) + pool.shape[1:], jnp.float32)
    first = 5 + len(flat)
    results = pl.pallas_call(
        functools.partial(
            round_kernel,
            chips,
            round_limit(parents),
            parents,
            tuple(received),
            tuple(crossed),
            staging,
            fresh,
            int(sends),
        ),
        grid_spec=pltpu.PrefetchScalarGridSpec(
            num_scalar_prefetch=5,
            grid=(),
            in_specs=[inside] * len(flat) + [anywhere] * 3,
            out_specs=[anywhere] * 3 + [inside] * (2 * int(sends)),
            scratch_shapes=[
                pltpu.VMEM((max(fresh, 1),) + pool.shape[1:], jnp.float32),
                pltpu.SemaphoreType.DMA((LANES * max(len(flat), 2) + fresh + 1,)),
            ],
        ),
        out_shape=[jax.ShapeDtypeStruct(array.shape, array.dtype) for array in state]
        + [lane_shape] * (2 * int(sends)),
        input_output_aliases={first: 0, first + 1: 1, first + 2: 2},
        compiler_params=pltpu.CompilerParams(vmem_limit_bytes=VMEM_BYTES),
        name="switch_round",
    )(table, counts, slots, place, now, *flat, *state)
    return tuple(results[:3]), tuple(results[3:])


def join_kernel(place, arrived, out_before, out):
    for child in range(2):
        for chip in range(arrived.shape[2]):
            out[child, 0, chip, 0] = arrived[child, 0, chip]


def join_cores(place, arrived, out):
    children, capacity, chips, _, rank_width, width = out.shape
    return pl.pallas_call(
        join_kernel,
        grid_spec=pltpu.PrefetchScalarGridSpec(
            num_scalar_prefetch=1,
            grid=(capacity,),
            in_specs=[
                pl.BlockSpec(
                    (children, 1, chips, rank_width, width), lambda slot, place: (0, slot, 0, 0, 0)
                ),
                pl.BlockSpec(memory_space=pl.ANY),
            ],
            out_specs=pl.BlockSpec(
                (children, 1, chips, 1, rank_width, width),
                lambda slot, place: (0, slot, 0, 1 - place[1], 0, 0),
            ),
        ),
        out_shape=jax.ShapeDtypeStruct(out.shape, out.dtype),
        input_output_aliases={2: 0},
        compiler_params=pltpu.CompilerParams(vmem_limit_bytes=VMEM_BYTES),
        name="join_cores",
    )(place, arrived, out)


def along_line(value, chips, up):
    pairs = []
    for chip in range(chips - 1):
        for core in range(2):
            low, high = 2 * chip + core, 2 * (chip + 1) + core
            pairs.append((low, high) if up else (high, low))
    return lax.ppermute(value, "box", pairs)


def per_device(
    coeffs,
    skeleton_first,
    skeleton_second,
    skeleton_third,
    checks_first,
    checks_second,
    checks_third,
    ranks_first,
    ranks_second,
    ranks_third,
    interpolants,
    owners,
):
    tbit_index = lax.axis_index("tbit")
    box_index = lax.axis_index("box")
    box_count = lax.axis_size("box")
    parent_count = coeffs.shape[0]
    rank_width = coeffs.shape[3]
    capacity = 2 * parent_count // box_count
    group_count = 2 * box_count
    local_boxes = 2 * box_index + jnp.arange(2, dtype=jnp.int32)[None, :, None]

    def targets_of(checks, per_parent, picked, width):
        boxes = per_parent * parent_count
        absolute = jnp.arange(boxes, dtype=jnp.int32)[:, None] * (NPTS // boxes) + checks
        return lax.dynamic_index_in_dim(absolute.reshape(parent_count, -1, width), picked, 1)

    def first_points(slot):
        box = 4 * local_boxes + 2 * (slot % 2) + slot // 2
        return box * (NPTS // (4 * group_count)) + pick_slot(skeleton_first, slot)

    def second_points(slot):
        box = 2 * local_boxes + slot % 2
        return box * (NPTS // (2 * group_count)) + pick_slot(skeleton_second, slot)

    partner_high = jnp.bitwise_xor(tbit_index, 2)
    partner_low = jnp.bitwise_xor(tbit_index, 1)
    points_third = local_boxes * (NPTS // group_count) + pick_slot(skeleton_third, tbit_index)
    low_targets = jnp.concatenate(
        [
            targets_of(checks_first, 2, tbit_index // 2, rank_width),
            targets_of(checks_second, 4, tbit_index, rank_width),
        ],
        axis=2,
    )
    high_targets = targets_of(checks_third, 8, tbit_index, 2 * rank_width)
    points = jnp.concatenate(
        [
            jnp.concatenate([first_points(tbit_index), first_points(partner_high)], axis=2),
            jnp.concatenate([second_points(tbit_index), second_points(partner_low)], axis=2),
            points_third.reshape(parent_count, 1, 2 * rank_width),
            low_targets,
            high_targets,
            jnp.zeros_like(high_targets),
        ],
        axis=1,
    )
    rank_one = ranks_first.reshape(-1)
    rank_two = ranks_second.reshape(-1)
    rank_three = lax.dynamic_index_in_dim(
        lax.dynamic_index_in_dim(ranks_third, tbit_index, 1, keepdims=False),
        box_index,
        2,
        keepdims=False,
    ).reshape(-1)

    mine = coeffs[:, :, 0]
    count = parent_count // CHUNKS
    chips = box_count // 2
    networked = chips <= 4
    place = jnp.stack([box_index // 2, box_index % 2]).astype(jnp.int32)
    owner_row = lax.dynamic_index_in_dim(owners, tbit_index, 0, keepdims=False)
    width = coeffs.shape[-1]
    pool_shape = (chips * parent_count, 2, rank_width, width)
    if not networked:
        place = jnp.zeros_like(place)
        pool_shape = (parent_count, 2, rank_width, width)

    parts, arrived = [], []
    for chunk in range(CHUNKS):
        source = mine
        if chunk > 0:
            source, _ = lax.optimization_barrier((mine, arrived[-1]))
        parts.append(source[chunk * count : (chunk + 1) * count])
        arrived.append(swapped(parts[-1], "tbit", 1))

    if networked:
        *plan, rounds = plan_switch(owner_row, chips)
        out = jnp.zeros((2, capacity, chips, 2, rank_width, width), jnp.float32)
        stage = jnp.zeros((2, capacity, chips, rank_width, width), jnp.float32)
        arrived[0], points, plan, rounds, out, stage = lax.optimization_barrier(
            (arrived[0], points, plan, rounds, out, stage)
        )
        most = jnp.broadcast_to(rounds, (8, 128))
        most = jnp.maximum(most, swapped(most, "tbit", 1))
        most = jnp.maximum(most, swapped(most, "tbit", 0))
        most = jnp.maximum(most[0, 0], STATIC_ROUNDS)
        arrived[3], most = lax.optimization_barrier((arrived[3], most))

    firsts, second_arrived = [], []

    high = lax.reduce_precision(interpolants, exponent_bits=8, mantissa_bits=7)
    low = (interpolants - high).astype(jnp.bfloat16)
    high = high.astype(jnp.bfloat16)
    matrices = jnp.concatenate(
        [jnp.concatenate([high, high], axis=2), jnp.concatenate([low, low], axis=2)], axis=1
    )

    def low_level(chunk):
        first = first_level(chunk, rank_one, points, matrices[0], parts[chunk], arrived[chunk])
        firsts.append(first)
        if chunk > 0:
            first, _ = lax.optimization_barrier((first, second_arrived[-1]))
        second_arrived.append(swapped(first, "tbit", 0))

    def high_levels(chunk, pool):
        return later_levels(
            chunk,
            (rank_two, rank_three),
            place,
            points,
            matrices[1:],
            firsts[chunk],
            second_arrived[chunk],
            pool_shape,
            pool,
        )

    low_level(0)
    if not networked:
        pool = high_levels(0, ())
        for chunk in range(1, CHUNKS):
            low_level(chunk)
            pool = high_levels(chunk, (pool,))
        slot_parent, slot_used = slot_table(owner_row, box_count, capacity)
        outgoing = jnp.take(jnp.swapaxes(pool, 0, 1), slot_parent.T, axis=1)
        outgoing = jnp.where(slot_used.T[None, :, :, None, None], outgoing, 0.0)
        switched = lax.all_to_all(outgoing, "box", split_axis=2, concat_axis=2, tiled=True)
        return switched[None, None]

    state = (None, out, stage)
    received, crossed = {}, {}

    def exchange(packed):
        return (along_line(packed[0], chips, True), along_line(packed[1], chips, False))

    def cross(value):
        return lax.ppermute(value, "box", [(box, box ^ 1) for box in range(box_count)])

    def cross_pair(pair):
        return (cross(pair[0]), cross(pair[1]))

    staged = CHUNKS - LAG + 1
    for step in range(STATIC_ROUNDS):
        fresh = 0
        if step < CHUNKS:
            if step + 1 < CHUNKS:
                low_level(step + 1)
                second_arrived[step], _ = lax.optimization_barrier(
                    (second_arrived[step], firsts[step + 1])
                )
            state = (high_levels(step, state[:1] if step else ()),) + state[1:]
            fresh = count
        state, packed = switch_round(
            plan,
            place,
            jnp.full((1,), step, jnp.int32),
            {LAG: received[step - LAG]} if step >= LAG else {},
            {LAG + 1: crossed[step - LAG - 1]} if step - LAG - 1 >= staged else {},
            state,
            step <= CHUNKS,
            fresh,
            True,
        )
        if step + 2 < CHUNKS:
            arrived[step + 2], _ = lax.optimization_barrier((arrived[step + 2], packed[0]))
        received[step] = exchange(packed)
        if step >= staged:
            crossed[step] = cross_pair(received[step])
        if step == CHUNKS:
            stage_crossed = cross(state[2])
        if step == CHUNKS + 1:
            state = (state[0], join_cores(place, stage_crossed, state[1]), state[2])

    def more(carry):
        return carry[0] < most

    def again(carry):
        step, state, (older, newer), (older_crossed, newer_crossed) = carry
        state, packed = switch_round(
            plan, place, step[None], {LAG: older}, {LAG + 1: older_crossed}, state, False, 0, True
        )
        return (
            step + 1,
            state,
            (newer, exchange(packed)),
            (newer_crossed, cross_pair(newer)),
        )

    final = STATIC_ROUNDS
    step, state, (older, newer), (older_crossed, newer_crossed) = lax.while_loop(
        more,
        again,
        (
            jnp.int32(final),
            state,
            (received[final - 2], received[final - 1]),
            (crossed[final - 3], crossed[final - 2]),
        ),
    )
    state, _ = switch_round(
        plan,
        place,
        step[None],
        {2: older, 1: newer},
        {3: older_crossed, 2: newer_crossed, 1: cross_pair(newer)},
        state,
        False,
        0,
        False,
    )
    return state[1].reshape(1, 1, 2, capacity, box_count, rank_width, width)


def solution(mesh):
    return jax.shard_map(
        per_device,
        mesh=mesh,
        in_specs=(
            P(None, "box", "tbit", None, None),
            P(None, "box", None, None),
            P(None, "box", None, None),
            P(None, "box", None, None),
            P(),
            P(),
            P(),
            P(None, "box", "tbit"),
            P(None, "box", "tbit"),
            P(),
            P(),
            P(),
        ),
        out_specs=P("tbit", "box", None, None, None, None, None),
        check_vma=False,
    )
```

```python
import functools
import math

import jax
import jax.numpy as jnp
from jax import lax
from jax.experimental import pallas as pl
from jax.experimental.pallas import tpu as pltpu
from jax.sharding import PartitionSpec as P

NPTS = 1048576
PHASE_BITS = 20
CHUNKS = 16
LANES = 4
LAG = 2
STATIC_ROUNDS = 22
PER_STEP = 4
VMEM_BYTES = 32 * 1024 * 1024
CODE_SHIFT = 16
SLOT_SHIFT = 16
POINTS_SECOND = 2
POINTS_THIRD = 4
TARGETS_LOW = 5
TARGETS_HIGH = 6

SIN_TERMS = (
    1.0,
    -1.0 / 6.0,
    1.0 / 120.0,
    -1.0 / 5040.0,
    1.0 / 362880.0,
    -1.0 / 39916800.0,
    1.0 / 6227020800.0,
)


def swapped(value, axis, bit):
    mask = 2**bit
    pairs = [(source, source ^ mask) for source in range(lax.axis_size(axis))]
    return lax.ppermute(value, axis, pairs)


def slot_table(owner_row, box_count, capacity):
    parent_count = owner_row.shape[0]
    onehot = (owner_row[:, None] == jnp.arange(box_count, dtype=jnp.int32)[None, :]).astype(
        jnp.int32
    )
    earlier = jnp.cumsum(onehot, axis=0, dtype=jnp.int32) - onehot
    slot_of = jnp.sum(earlier * onehot, axis=1, dtype=jnp.int32)
    matches = (onehot.T[:, None, :] == 1) & (
        slot_of[None, None, :] == jnp.arange(capacity, dtype=jnp.int32)[None, :, None]
    )
    slot_parent = jnp.sum(
        jnp.where(matches, jnp.arange(parent_count, dtype=jnp.int32)[None, None, :], 0), axis=2
    )
    slot_used = jnp.any(matches, axis=2)
    return (slot_parent, slot_used)


def pick_slot(values, position):
    return lax.dynamic_index_in_dim(values, position, 2, keepdims=False)


def cos_kernel(targets, points):
    shift = 32 - PHASE_BITS
    phase = lax.shift_right_arithmetic(
        lax.shift_left(targets * points, jnp.int32(shift)), jnp.int32(shift)
    )
    offset = NPTS // 4 - jnp.abs(phase)
    y = offset.astype(jnp.float32) * jnp.float32(2.0 * math.pi / NPTS)
    square = y * y
    total = jnp.float32(SIN_TERMS[-1])
    for term in SIN_TERMS[-2::-1]:
        total = total * square + jnp.float32(term)
    return total * y


def split(value):
    high = value.astype(jnp.bfloat16)
    low = (value - high.astype(jnp.float32)).astype(jnp.bfloat16)
    return high, low


def stack_left(value):
    high, low = split(value)
    return jnp.concatenate(
        [jnp.concatenate([high, high], axis=1), jnp.concatenate([low, low], axis=1)], axis=0
    )


def product(left, right):
    rows = left.shape[0] // 2
    both = jnp.dot(
        left, jnp.concatenate(split(right), axis=0), preferred_element_type=jnp.float32
    )
    return both[:rows] + both[rows:]


def live(weights, rank):
    rows = lax.broadcasted_iota(jnp.int32, weights.shape, 0)
    return jnp.where(rows < rank, weights, 0.0)


def column(tile, row, begin, length):
    return jnp.transpose(tile)[begin : begin + length, row : row + 1]


def pair_weights(matrix, left, right, left_rank, right_rank):
    width = left.shape[1]
    both = product(matrix, jnp.concatenate([left, right], axis=1))
    return live(both[:, :width], left_rank), live(both[:, width:], right_rank)


def first_kernel(chunk, ranks, points, matrix, mine, arrived, merged):
    step = pl.program_id(0)
    parents, boxes, rank_width = mine.shape[0], mine.shape[1], mine.shape[2]
    for parent in range(parents):
        row = (chunk * pl.num_programs(0) + step) * parents + parent
        tile = points[parent]
        targets = column(tile, TARGETS_LOW, 0, rank_width)
        kernels = [cos_kernel(targets, tile[box : box + 1]) for box in range(boxes)]
        weights = pair_weights(matrix[...], *kernels, ranks[row * boxes], ranks[row * boxes + 1])
        for box in range(boxes):
            stacked = jnp.concatenate([mine[parent, box], arrived[parent, box]], axis=0)
            merged[parent, box] = product(stack_left(weights[box]), stacked)


def later_kernel(chunk, ranks_second, ranks_third, place, points, matrices, mine, arrived, *pool):
    merged = pool[-1]
    step = pl.program_id(0)
    parents, boxes, rank_width = mine.shape[0], mine.shape[1], mine.shape[2]
    for parent in range(parents):
        row = (chunk * pl.num_programs(0) + step) * parents + parent
        tile = points[parent]
        targets = column(tile, TARGETS_LOW, rank_width, rank_width)
        kernels = [
            cos_kernel(targets, tile[POINTS_SECOND + box : POINTS_SECOND + box + 1])
            for box in range(boxes)
        ]
        weights = pair_weights(
            matrices[0], *kernels, ranks_second[row * boxes], ranks_second[row * boxes + 1]
        )
        seconds = []
        for box in range(boxes):
            stacked = jnp.concatenate([mine[parent, box], arrived[parent, box]], axis=0)
            seconds.append(product(stack_left(weights[box]), stacked))
        targets = column(tile, TARGETS_HIGH, 0, 2 * rank_width)
        kernel = cos_kernel(targets, tile[POINTS_THIRD : POINTS_THIRD + 1])
        weights = pair_weights(
            matrices[1],
            kernel[:rank_width],
            kernel[rank_width:],
            ranks_third[row * 2],
            ranks_third[row * 2 + 1],
        )
        stacked = jnp.concatenate(seconds, axis=0)
        third = product(stack_left(jnp.concatenate(weights, axis=0)), stacked)
        for child in range(2):
            merged[parent, child] = third[child * rank_width : (child + 1) * rank_width]


def chunk_spec(shape, chunk, steps, per_step):
    block = (per_step,) + tuple(shape[1:])
    rest = (0,) * (len(shape) - 1)
    return pl.BlockSpec(block, lambda step, *_: (chunk * steps + step,) + rest)


def whole_spec(shape):
    rest = (0,) * len(shape)
    return pl.BlockSpec(tuple(shape), lambda step, *_: rest)


def first_level(chunk, ranks, points, matrix, mine, arrived):
    per_step = PER_STEP
    steps = mine.shape[0] // per_step
    return pl.pallas_call(
        functools.partial(first_kernel, chunk),
        grid_spec=pltpu.PrefetchScalarGridSpec(
            num_scalar_prefetch=1,
            grid=(steps,),
            in_specs=[
                chunk_spec(points.shape, chunk, steps, per_step),
                whole_spec(matrix.shape),
                chunk_spec(mine.shape, 0, steps, per_step),
                chunk_spec(arrived.shape, 0, steps, per_step),
            ],
            out_specs=chunk_spec(arrived.shape, 0, steps, per_step),
        ),
        out_shape=jax.ShapeDtypeStruct(arrived.shape, jnp.float32),
        compiler_params=pltpu.CompilerParams(vmem_limit_bytes=VMEM_BYTES),
        name="first_level",
    )(ranks, points, matrix, mine, arrived)


def later_levels(chunk, ranks, place, points, matrices, mine, arrived, pool_shape, pool):
    per_step = PER_STEP
    steps = mine.shape[0] // per_step
    parents = points.shape[0]

    def pool_block(step, ranks_second, ranks_third, place):
        return (place[0] * (parents // per_step) + chunk * steps + step, 0, 0, 0)

    return pl.pallas_call(
        functools.partial(later_kernel, chunk),
        grid_spec=pltpu.PrefetchScalarGridSpec(
            num_scalar_prefetch=3,
            grid=(steps,),
            in_specs=[
                chunk_spec(points.shape, chunk, steps, per_step),
                whole_spec(matrices.shape),
                chunk_spec(mine.shape, 0, steps, per_step),
                chunk_spec(arrived.shape, 0, steps, per_step),
            ]
            + [pl.BlockSpec(memory_space=pl.ANY)] * len(pool),
            out_specs=pl.BlockSpec((per_step,) + pool_shape[1:], pool_block),
        ),
        out_shape=jax.ShapeDtypeStruct(pool_shape, jnp.float32),
        input_output_aliases={7: 0} if pool else {},
        compiler_params=pltpu.CompilerParams(vmem_limit_bytes=VMEM_BYTES),
        name="later_levels",
    )(ranks[0], ranks[1], place, points, matrices, mine, arrived, *pool)


def plan_kernel(
    chips, limit, chunks, owners, table, counts, slots, rounds, out, stage, own, ahead, used, zeros, sem
):
    parents = owners.shape[0]
    zeros[...] = jnp.zeros_like(zeros)
    fills = []
    for child in range(out.shape[0]):
        for slot in range(out.shape[1]):
            fills.append(pltpu.make_async_copy(zeros, out.at[child, slot], sem.at[len(fills)]))
            part = zeros.at[:, 0]
            fills.append(pltpu.make_async_copy(part, stage.at[child, slot], sem.at[len(fills)]))
    for fill in fills:
        fill.start()
    count = parents // chunks
    rows = chips + 1
    span = limit * LANES

    def clear(index, carry):
        counts[index] = 0
        return carry

    lax.fori_loop(0, 2 * rows * limit, clear, 0)
    for box in range(2 * chips):
        used[box] = 0

    def take_slot(parent, carry):
        owner = owners[parent]
        slot = used[owner]
        slots[parent] = (owner << SLOT_SHIFT) | slot
        used[owner] = slot + 1
        return carry

    lax.fori_loop(0, parents, take_slot, 0)
    width = chips * parents
    pairs = [(chip, goal) for chip in range(1, chips) for goal in range(chip + 1, chips)]
    last = []
    for direction in range(2):

        def true_chip(chip):
            return chip if direction == 0 else chips - 1 - chip

        total = 0
        for box in range(2 * chips):
            hops = true_chip(box // 2)
            total = total + used[box] * (hops * (hops + 1) // 2)

        def one_round(state):
            step, left, ready, own_head, head, tail, older = state
            ready, own_head, head, tail = list(ready), list(own_head), list(head), list(tail)
            for index in range(count):
                parent = jnp.minimum(step * count + index, parents - 1)
                goal = owners[parent] >> 1
                goal = goal if direction == 0 else chips - 1 - goal
                for chip in range(1, chips):
                    own[chip * parents + jnp.minimum(ready[chip], parents - 1)] = parent
                    here = (goal == chip) & (step < chunks)
                    ready[chip] = ready[chip] + here.astype(jnp.int32)
            seen = older[0]
            for chip in range(chips - 1):
                row = (direction * rows + 1 + chip) * limit + step
                sent = jnp.int32(0)
                for goal in range(chips - 1, chip, -1):
                    onward = pairs.index((chip + 1, goal)) if (chip + 1, goal) in pairs else None
                    for forwarded in (True, False):
                        if forwarded and (chip, goal) not in pairs:
                            continue
                        if forwarded:
                            queue = pairs.index((chip, goal))
                            start, stop = head[queue], seen[queue]
                        else:
                            queue = chip * chips + goal
                            start, stop = own_head[queue], ready[goal]
                        number = jnp.minimum(stop - start, LANES - sent)

                        def move(index, carry):
                            if forwarded:
                                code = ahead[queue * width + start + index]
                            else:
                                code = own[goal * parents + start + index]
                                code = code | (true_chip(chip) << CODE_SHIFT)
                            table[row * LANES + sent + index] = code
                            if onward is not None:
                                ahead[onward * width + tail[onward] + index] = code
                            return carry

                        lax.fori_loop(0, number, move, 0)
                        sent = sent + number
                        if onward is not None:
                            tail[onward] = tail[onward] + number
                        if forwarded:
                            head[queue] = start + number
                        else:
                            own_head[queue] = start + number
                counts[row] = sent
                left = left - sent
            return (
                step + 1,
                left,
                tuple(ready),
                tuple(own_head),
                tuple(head),
                tuple(tail),
                tuple(older[1:]) + (tuple(tail),),
            )

        zero = jnp.int32(0)
        none = (zero,) * len(pairs)
        state = lax.while_loop(
            lambda state: (state[1] > 0) & (state[0] < limit),
            one_round,
            (zero, jnp.int32(total), (zero,) * chips, (zero,) * (chips * chips), none, none, (none,) * LAG),
        )
        last.append(state[0])
    rounds[0] = jnp.maximum(last[0], last[1])
    for fill in fills:
        fill.wait()


def plan_switch(owner_row, out_shape):
    parents = owner_row.shape[0]
    chips = out_shape[2]
    anywhere = pl.BlockSpec(memory_space=pl.ANY)
    limit = round_limit(parents)
    smem = pl.BlockSpec(memory_space=pltpu.SMEM)
    return pl.pallas_call(
        functools.partial(plan_kernel, chips, limit, CHUNKS),
        in_specs=[smem],
        out_specs=[smem] * 4 + [anywhere] * 2,
        out_shape=[
            jax.ShapeDtypeStruct((2 * (chips + 1) * limit * LANES,), jnp.int32),
            jax.ShapeDtypeStruct((2 * (chips + 1) * limit,), jnp.int32),
            jax.ShapeDtypeStruct((parents,), jnp.int32),
            jax.ShapeDtypeStruct((1,), jnp.int32),
            jax.ShapeDtypeStruct(out_shape, jnp.float32),
            jax.ShapeDtypeStruct(out_shape[:3] + out_shape[4:], jnp.float32),
        ],
        scratch_shapes=[
            pltpu.SMEM((chips * parents,), jnp.int32),
            pltpu.SMEM((chips * chips * chips * parents,), jnp.int32),
            pltpu.SMEM((2 * chips,), jnp.int32),
            pltpu.VMEM(out_shape[2:], jnp.float32),
            pltpu.SemaphoreType.DMA((2 * out_shape[0] * out_shape[1],)),
        ],
        name="plan_switch",
    )(owner_row)


def round_limit(parents):
    return 4 * parents // LANES


def round_kernel(
    chips, limit, parents, receives, crossings, staging, fresh, sends, table, counts, slots, place, now, *refs
):
    sources = receives + crossings
    received = refs[: 2 * len(sources)]
    refs = refs[2 * len(sources) + 3 :]
    pool, out, stage = refs[:3]
    outgoing = refs[3 : 3 + 2 * sends]
    kept, sems = refs[-2:]
    z, core = place[0], place[1]
    odd = z & 1

    def row_of(direction, receiving, step):
        spot = jnp.where(direction == 0, z, chips - 1 - z)
        return (direction * (chips + 1) + (1 - receiving) + spot) * limit + step

    def home(sem, from_chip, parent, source, begin, crossed=False):
        spot = slots[parent]
        owner, slot = spot >> SLOT_SHIFT, spot & ((1 << SLOT_SHIFT) - 1)
        here = (owner >> 1) == z
        same = (owner & 1) == core

        @pl.when(here & same)
        def _():
            from_core = 1 - core if crossed else core
            copy = pltpu.make_async_copy(source, out.at[:, slot, from_chip, from_core], sem)
            copy.start() if begin else copy.wait()

        if staging and not crossed:

            @pl.when(here & jnp.logical_not(same))
            def _():
                copy = pltpu.make_async_copy(source, stage.at[:, slot, from_chip], sem)
                copy.start() if begin else copy.wait()

        return here

    def of_code(code):
        from_chip, parent = code >> CODE_SHIFT, code & ((1 << CODE_SHIFT) - 1)
        return from_chip, parent, from_chip * parents + parent

    def take_in(begin):
        for place_of, back in enumerate(sources):
            crossed = place_of >= len(receives)
            for port in range(2):
                step = now[0] - back
                row = row_of(1 - (odd ^ port), 1, jnp.maximum(step, 0))
                number = jnp.where(step >= 0, counts[row], 0)
                base = (2 * place_of + port) * LANES

                def one(lane, carry):
                    from_chip, parent, held = of_code(table[row * LANES + lane])
                    source = received[2 * place_of + port].at[lane]
                    sem = sems.at[base + lane]
                    here = home(sem, from_chip, parent, source, begin, crossed)
                    if not crossed:

                        @pl.when(jnp.logical_not(here))
                        def _():
                            copy = pltpu.make_async_copy(source, pool.at[held], sem)
                            copy.start() if begin else copy.wait()

                    return carry

                lax.fori_loop(0, number, one, 0)

    def send(begin):
        for port in range(2):
            row = row_of(odd ^ port, 0, now[0])

            def one(lane, carry):
                _, _, held = of_code(table[row * LANES + lane])
                copy = pltpu.make_async_copy(
                    pool.at[held], outgoing[port].at[lane], sems.at[port * LANES + lane]
                )
                copy.start() if begin else copy.wait()
                return carry

            lax.fori_loop(0, counts[row], one, 0)

    def keep(begin):
        def one(member, carry):
            parent = now[0] * fresh + member
            home(sems.at[2 * LANES * max(len(sources), 1) + member], z, parent, kept.at[member], begin)
            return carry

        lax.fori_loop(0, fresh, one, 0)

    if fresh:
        load = pltpu.make_async_copy(
            pool.at[pl.ds(z * parents + now[0] * fresh, fresh)], kept, sems.at[2 * LANES * max(len(sources), 1) + fresh]
        )
        load.start()
    take_in(True)
    if fresh:
        load.wait()
        keep(True)
    take_in(False)
    if sends:
        send(True)
    if fresh:
        keep(False)
    if sends:
        send(False)


def switch_round(plan, place, now, received, crossed, state, staging, fresh, sends):
    table, counts, slots = plan
    pool, out, stage = state
    parents = slots.shape[0]
    chips = out.shape[2]
    flat = [array for pair in [*received.values(), *crossed.values()] for array in pair]
    anywhere = pl.BlockSpec(memory_space=pl.ANY)
    inside = pl.BlockSpec(memory_space=pltpu.VMEM)
    lane_shape = jax.ShapeDtypeStruct((LANES,) + pool.shape[1:], jnp.float32)
    first = 5 + len(flat)
    results = pl.pallas_call(
        functools.partial(
            round_kernel,
            chips,
            round_limit(parents),
            parents,
            tuple(received),
            tuple(crossed),
            staging,
            fresh,
            int(sends),
        ),
        grid_spec=pltpu.PrefetchScalarGridSpec(
            num_scalar_prefetch=5,
            grid=(),
            in_specs=[inside] * len(flat) + [anywhere] * 3,
            out_specs=[anywhere] * 3 + [inside] * (2 * int(sends)),
            scratch_shapes=[
                pltpu.VMEM((max(fresh, 1),) + pool.shape[1:], jnp.float32),
                pltpu.SemaphoreType.DMA((LANES * max(len(flat), 2) + fresh + 1,)),
            ],
        ),
        out_shape=[jax.ShapeDtypeStruct(array.shape, array.dtype) for array in state]
        + [lane_shape] * (2 * int(sends)),
        input_output_aliases={first: 0, first + 1: 1, first + 2: 2},
        compiler_params=pltpu.CompilerParams(vmem_limit_bytes=VMEM_BYTES),
        name="switch_round",
    )(table, counts, slots, place, now, *flat, *state)
    return tuple(results[:3]), tuple(results[3:])


def join_kernel(place, arrived, out_before, out):
    for child in range(2):
        for chip in range(arrived.shape[2]):
            out[child, 0, chip, 0] = arrived[child, 0, chip]


def join_cores(place, arrived, out):
    children, capacity, chips, _, rank_width, width = out.shape
    return pl.pallas_call(
        join_kernel,
        grid_spec=pltpu.PrefetchScalarGridSpec(
            num_scalar_prefetch=1,
            grid=(capacity,),
            in_specs=[
                pl.BlockSpec(
                    (children, 1, chips, rank_width, width), lambda slot, place: (0, slot, 0, 0, 0)
                ),
                pl.BlockSpec(memory_space=pl.ANY),
            ],
            out_specs=pl.BlockSpec(
                (children, 1, chips, 1, rank_width, width),
                lambda slot, place: (0, slot, 0, 1 - place[1], 0, 0),
            ),
        ),
        out_shape=jax.ShapeDtypeStruct(out.shape, out.dtype),
        input_output_aliases={2: 0},
        compiler_params=pltpu.CompilerParams(vmem_limit_bytes=VMEM_BYTES),
        name="join_cores",
    )(place, arrived, out)


def along_line(value, chips, port):
    pairs = []
    for chip in range(port, chips - 1, 2):
        for core in range(2):
            low, high = 2 * chip + core, 2 * (chip + 1) + core
            pairs += [(low, high), (high, low)]
    return lax.ppermute(value, "box", pairs)


def per_device(
    coeffs,
    skeleton_first,
    skeleton_second,
    skeleton_third,
    checks_first,
    checks_second,
    checks_third,
    ranks_first,
    ranks_second,
    ranks_third,
    interpolants,
    owners,
):
    tbit_index = lax.axis_index("tbit")
    box_index = lax.axis_index("box")
    box_count = lax.axis_size("box")
    parent_count = coeffs.shape[0]
    rank_width = coeffs.shape[3]
    capacity = 2 * parent_count // box_count
    group_count = 2 * box_count
    local_boxes = 2 * box_index + jnp.arange(2, dtype=jnp.int32)[None, :, None]

    def targets_of(checks, per_parent, picked, width):
        boxes = per_parent * parent_count
        absolute = jnp.arange(boxes, dtype=jnp.int32)[:, None] * (NPTS // boxes) + checks
        return lax.dynamic_index_in_dim(absolute.reshape(parent_count, -1, width), picked, 1)

    def first_points(slot):
        box = 4 * local_boxes + 2 * (slot % 2) + slot // 2
        return box * (NPTS // (4 * group_count)) + pick_slot(skeleton_first, slot)

    def second_points(slot):
        box = 2 * local_boxes + slot % 2
        return box * (NPTS // (2 * group_count)) + pick_slot(skeleton_second, slot)

    partner_high = jnp.bitwise_xor(tbit_index, 2)
    partner_low = jnp.bitwise_xor(tbit_index, 1)
    points_third = local_boxes * (NPTS // group_count) + pick_slot(skeleton_third, tbit_index)
    low_targets = jnp.concatenate(
        [
            targets_of(checks_first, 2, tbit_index // 2, rank_width),
            targets_of(checks_second, 4, tbit_index, rank_width),
        ],
        axis=2,
    )
    high_targets = targets_of(checks_third, 8, tbit_index, 2 * rank_width)
    points = jnp.concatenate(
        [
            jnp.concatenate([first_points(tbit_index), first_points(partner_high)], axis=2),
            jnp.concatenate([second_points(tbit_index), second_points(partner_low)], axis=2),
            points_third.reshape(parent_count, 1, 2 * rank_width),
            low_targets,
            high_targets,
            jnp.zeros_like(high_targets),
        ],
        axis=1,
    )
    rank_one = ranks_first.reshape(-1)
    rank_two = ranks_second.reshape(-1)
    rank_three = lax.dynamic_index_in_dim(
        lax.dynamic_index_in_dim(ranks_third, tbit_index, 1, keepdims=False),
        box_index,
        2,
        keepdims=False,
    ).reshape(-1)

    mine = coeffs[:, :, 0]
    count = parent_count // CHUNKS
    chips = box_count // 2
    networked = chips <= 4
    place = jnp.stack([box_index // 2, box_index % 2]).astype(jnp.int32)
    owner_row = lax.dynamic_index_in_dim(owners, tbit_index, 0, keepdims=False)
    width = coeffs.shape[-1]
    pool_shape = (chips * parent_count, 2, rank_width, width)
    if not networked:
        place = jnp.zeros_like(place)
        pool_shape = (parent_count, 2, rank_width, width)

    parts, arrived = [mine[:count]], []
    others, _ = lax.optimization_barrier((mine, parts[0]))
    for chunk in range(1, CHUNKS):
        parts.append(others[chunk * count : (chunk + 1) * count])
    for chunk in range(CHUNKS):
        outgoing = parts[chunk]
        if chunk > 0:
            outgoing, _ = lax.optimization_barrier((outgoing, arrived[-1]))
        arrived.append(swapped(outgoing, "tbit", 1))

    firsts, second_arrived = [], []

    high = lax.reduce_precision(interpolants, exponent_bits=8, mantissa_bits=7)
    low = (interpolants - high).astype(jnp.bfloat16)
    high = high.astype(jnp.bfloat16)
    matrices = jnp.concatenate(
        [jnp.concatenate([high, high], axis=2), jnp.concatenate([low, low], axis=2)], axis=1
    )

    def low_level(chunk):
        first = first_level(chunk, rank_one, points, matrices[0], parts[chunk], arrived[chunk])
        firsts.append(first)
        if chunk > 0:
            first, _ = lax.optimization_barrier((first, second_arrived[-1]))
        second_arrived.append(swapped(first, "tbit", 0))

    def high_levels(chunk, pool):
        return later_levels(
            chunk,
            (rank_two, rank_three),
            place,
            points,
            matrices[1:],
            firsts[chunk],
            second_arrived[chunk],
            pool_shape,
            pool,
        )

    low_level(0)
    if networked:
        owner_row, _ = lax.optimization_barrier((owner_row, firsts[0]))
        out_shape = (2, capacity, chips, 2, rank_width, width)
        *plan, rounds, out, stage = plan_switch(owner_row, out_shape)
        arrived[1], plan, rounds, out, stage = lax.optimization_barrier(
            (arrived[1], plan, rounds, out, stage)
        )
        most = jnp.broadcast_to(rounds, (8, 128))
        most = jnp.maximum(most, swapped(most, "tbit", 1))
        most = jnp.maximum(most, swapped(most, "tbit", 0))
        most = jnp.maximum(most[0, 0], STATIC_ROUNDS)
        arrived[4], most = lax.optimization_barrier((arrived[4], most))
    if not networked:
        pool = high_levels(0, ())
        for chunk in range(1, CHUNKS):
            low_level(chunk)
            pool = high_levels(chunk, (pool,))
        slot_parent, slot_used = slot_table(owner_row, box_count, capacity)
        outgoing = jnp.take(jnp.swapaxes(pool, 0, 1), slot_parent.T, axis=1)
        outgoing = jnp.where(slot_used.T[None, :, :, None, None], outgoing, 0.0)
        switched = lax.all_to_all(outgoing, "box", split_axis=2, concat_axis=2, tiled=True)
        return switched[None, None]

    state = (None, out, stage)
    received, crossed = {}, {}

    def exchange(packed):
        return (along_line(packed[0], chips, 0), along_line(packed[1], chips, 1))

    def cross(value):
        return lax.ppermute(value, "box", [(box, box ^ 1) for box in range(box_count)])

    def cross_pair(pair):
        return (cross(pair[0]), cross(pair[1]))

    staged = CHUNKS - LAG + 1
    for step in range(STATIC_ROUNDS):
        fresh = 0
        if step < CHUNKS:
            if step + 1 < CHUNKS:
                low_level(step + 1)
                second_arrived[step], _ = lax.optimization_barrier(
                    (second_arrived[step], firsts[step + 1])
                )
            state = (high_levels(step, state[:1] if step else ()),) + state[1:]
            fresh = count
        state, packed = switch_round(
            plan,
            place,
            jnp.full((1,), step, jnp.int32),
            {LAG: received[step - LAG]} if step >= LAG else {},
            {LAG + 1: crossed[step - LAG - 1]} if step - LAG - 1 >= staged else {},
            state,
            step <= CHUNKS,
            fresh,
            True,
        )
        if step + 2 < CHUNKS:
            arrived[step + 2], _ = lax.optimization_barrier((arrived[step + 2], packed[0]))
        received[step] = exchange(packed)
        if step >= staged:
            crossed[step] = cross_pair(received[step])
        if step == CHUNKS:
            stage_crossed = cross(state[2])
        if step == CHUNKS + 1:
            state = (state[0], join_cores(place, stage_crossed, state[1]), state[2])

    def more(carry):
        return carry[0] < most

    def again(carry):
        step, state, (older, newer), (older_crossed, newer_crossed) = carry
        state, packed = switch_round(
            plan, place, step[None], {LAG: older}, {LAG + 1: older_crossed}, state, False, 0, True
        )
        return (
            step + 1,
            state,
            (newer, exchange(packed)),
            (newer_crossed, cross_pair(newer)),
        )

    final = STATIC_ROUNDS
    step, state, (older, newer), (older_crossed, newer_crossed) = lax.while_loop(
        more,
        again,
        (
            jnp.int32(final),
            state,
            (received[final - 2], received[final - 1]),
            (crossed[final - 3], crossed[final - 2]),
        ),
    )
    state, _ = switch_round(
        plan,
        place,
        step[None],
        {2: older, 1: newer},
        {3: older_crossed, 2: newer_crossed, 1: cross_pair(newer)},
        state,
        False,
        0,
        False,
    )
    return state[1].reshape(1, 1, 2, capacity, box_count, rank_width, width)


def solution(mesh):
    return jax.shard_map(
        per_device,
        mesh=mesh,
        in_specs=(
            P(None, "box", "tbit", None, None),
            P(None, "box", None, None),
            P(None, "box", None, None),
            P(None, "box", None, None),
            P(),
            P(),
            P(),
            P(None, "box", "tbit"),
            P(None, "box", "tbit"),
            P(),
            P(),
            P(),
        ),
        out_specs=P("tbit", "box", None, None, None, None, None),
        check_vma=False,
    )
```

```python
import functools
import math

import jax
import jax.numpy as jnp
from jax import lax
from jax.experimental import pallas as pl
from jax.experimental.pallas import tpu as pltpu
from jax.sharding import PartitionSpec as P

NPTS = 1048576
PHASE_BITS = 20
CHUNKS = 16
LANES = 4
LAG = 2
CROSS_LAG = 4
STATIC_ROUNDS = 22
PER_STEP = 4
VMEM_BYTES = 32 * 1024 * 1024
CODE_SHIFT = 16
SLOT_SHIFT = 16
POINTS_SECOND = 2
POINTS_THIRD = 4
TARGETS_LOW = 5
TARGETS_HIGH = 6

SIN_TERMS = (
    1.0,
    -1.0 / 6.0,
    1.0 / 120.0,
    -1.0 / 5040.0,
    1.0 / 362880.0,
    -1.0 / 39916800.0,
    1.0 / 6227020800.0,
)


def swapped(value, axis, bit):
    mask = 2**bit
    pairs = [(source, source ^ mask) for source in range(lax.axis_size(axis))]
    return lax.ppermute(value, axis, pairs)


def slot_table(owner_row, box_count, capacity):
    parent_count = owner_row.shape[0]
    onehot = (owner_row[:, None] == jnp.arange(box_count, dtype=jnp.int32)[None, :]).astype(
        jnp.int32
    )
    earlier = jnp.cumsum(onehot, axis=0, dtype=jnp.int32) - onehot
    slot_of = jnp.sum(earlier * onehot, axis=1, dtype=jnp.int32)
    matches = (onehot.T[:, None, :] == 1) & (
        slot_of[None, None, :] == jnp.arange(capacity, dtype=jnp.int32)[None, :, None]
    )
    slot_parent = jnp.sum(
        jnp.where(matches, jnp.arange(parent_count, dtype=jnp.int32)[None, None, :], 0), axis=2
    )
    slot_used = jnp.any(matches, axis=2)
    return (slot_parent, slot_used)


def pick_slot(values, position):
    return lax.dynamic_index_in_dim(values, position, 2, keepdims=False)


def cos_kernel(targets, points):
    shift = 32 - PHASE_BITS
    phase = lax.shift_right_arithmetic(
        lax.shift_left(targets * points, jnp.int32(shift)), jnp.int32(shift)
    )
    offset = NPTS // 4 - jnp.abs(phase)
    y = offset.astype(jnp.float32) * jnp.float32(2.0 * math.pi / NPTS)
    square = y * y
    total = jnp.float32(SIN_TERMS[-1])
    for term in SIN_TERMS[-2::-1]:
        total = total * square + jnp.float32(term)
    return total * y


def split(value):
    high = value.astype(jnp.bfloat16)
    low = (value - high.astype(jnp.float32)).astype(jnp.bfloat16)
    return high, low


def stack_left(value):
    high, low = split(value)
    return jnp.concatenate(
        [jnp.concatenate([high, high], axis=1), jnp.concatenate([low, low], axis=1)], axis=0
    )


def product(left, right):
    rows = left.shape[0] // 2
    both = jnp.dot(
        left, jnp.concatenate(split(right), axis=0), preferred_element_type=jnp.float32
    )
    return both[:rows] + both[rows:]


def live(weights, rank):
    rows = lax.broadcasted_iota(jnp.int32, weights.shape, 0)
    return jnp.where(rows < rank, weights, 0.0)


def column(tile, row, begin, length):
    return jnp.transpose(tile)[begin : begin + length, row : row + 1]


def pair_weights(matrix, left, right, left_rank, right_rank):
    width = left.shape[1]
    both = product(matrix, jnp.concatenate([left, right], axis=1))
    return live(both[:, :width], left_rank), live(both[:, width:], right_rank)


def first_parent(tile, matrix, ranks, mine, arrived):
    rank_width = mine.shape[1]
    targets = column(tile, TARGETS_LOW, 0, rank_width)
    kernels = [cos_kernel(targets, tile[box : box + 1]) for box in range(2)]
    weights = pair_weights(matrix, *kernels, *ranks)
    return [
        product(stack_left(weights[box]), jnp.concatenate([mine[box], arrived[box]], axis=0))
        for box in range(2)
    ]


def later_parent(tile, matrices, ranks_second, ranks_third, mine, arrived):
    rank_width = mine.shape[1]
    targets = column(tile, TARGETS_LOW, rank_width, rank_width)
    kernels = [
        cos_kernel(targets, tile[POINTS_SECOND + box : POINTS_SECOND + box + 1]) for box in range(2)
    ]
    weights = pair_weights(matrices[0], *kernels, *ranks_second)
    seconds = [
        product(stack_left(weights[box]), jnp.concatenate([mine[box], arrived[box]], axis=0))
        for box in range(2)
    ]
    targets = column(tile, TARGETS_HIGH, 0, 2 * rank_width)
    kernel = cos_kernel(targets, tile[POINTS_THIRD : POINTS_THIRD + 1])
    weights = pair_weights(matrices[1], kernel[:rank_width], kernel[rank_width:], *ranks_third)
    stacked = jnp.concatenate(seconds, axis=0)
    return product(stack_left(jnp.concatenate(weights, axis=0)), stacked)


def ranks_of(ranks, level, parents, parent):
    start = 2 * (level * parents + parent)
    return ranks[start], ranks[start + 1]


def first_kernel(chunk, parents, ranks, points, matrices, mine, arrived, merged):
    matrix = stack_left(matrices[0])
    for member in range(mine.shape[0]):
        parent = (chunk * pl.num_programs(0) + pl.program_id(0)) * mine.shape[0] + member
        results = first_parent(
            points[member], matrix, ranks_of(ranks, 0, parents, parent), mine[member], arrived[member]
        )
        for box in range(2):
            merged[member, box] = results[box]


def later_kernel(chunk, parents, ranks, points, matrices, mine, arrived, *pool):
    merged = pool[-1]
    rank_width = mine.shape[2]
    stacks = [stack_left(matrices[1]), stack_left(matrices[2])]
    for member in range(mine.shape[0]):
        parent = (chunk * pl.num_programs(0) + pl.program_id(0)) * mine.shape[0] + member
        third = later_parent(
            points[member],
            stacks,
            ranks_of(ranks, 1, parents, parent),
            ranks_of(ranks, 2, parents, parent),
            mine[member],
            arrived[member],
        )
        for child in range(2):
            merged[member, child] = third[child * rank_width : (child + 1) * rank_width]


def chunk_spec(shape, chunk, steps, per_step):
    block = (per_step,) + tuple(shape[1:])
    rest = (0,) * (len(shape) - 1)
    return pl.BlockSpec(block, lambda step, *_: (chunk * steps + step,) + rest)


def whole_spec(shape):
    rest = (0,) * len(shape)
    return pl.BlockSpec(tuple(shape), lambda step, *_: rest)


def first_level(chunk, ranks, points, matrices, mine, arrived):
    per_step = PER_STEP
    steps = mine.shape[0] // per_step
    return pl.pallas_call(
        functools.partial(first_kernel, chunk, points.shape[0]),
        grid_spec=pltpu.PrefetchScalarGridSpec(
            num_scalar_prefetch=1,
            grid=(steps,),
            in_specs=[
                chunk_spec(points.shape, chunk, steps, per_step),
                whole_spec(matrices.shape),
                chunk_spec(mine.shape, 0, steps, per_step),
                chunk_spec(arrived.shape, 0, steps, per_step),
            ],
            out_specs=chunk_spec(arrived.shape, 0, steps, per_step),
        ),
        out_shape=jax.ShapeDtypeStruct(arrived.shape, jnp.float32),
        compiler_params=pltpu.CompilerParams(vmem_limit_bytes=VMEM_BYTES),
        name="first_level",
    )(ranks, points, matrices, mine, arrived)


def later_levels(chunk, ranks, points, matrices, mine, arrived, pool_shape, pool):
    per_step = PER_STEP
    steps = mine.shape[0] // per_step
    return pl.pallas_call(
        functools.partial(later_kernel, chunk, points.shape[0]),
        grid_spec=pltpu.PrefetchScalarGridSpec(
            num_scalar_prefetch=1,
            grid=(steps,),
            in_specs=[
                chunk_spec(points.shape, chunk, steps, per_step),
                whole_spec(matrices.shape),
                chunk_spec(mine.shape, 0, steps, per_step),
                chunk_spec(arrived.shape, 0, steps, per_step),
            ]
            + [pl.BlockSpec(memory_space=pl.ANY)] * len(pool),
            out_specs=chunk_spec(pool_shape, chunk, steps, per_step),
        ),
        out_shape=jax.ShapeDtypeStruct(pool_shape, jnp.float32),
        input_output_aliases={5: 0} if pool else {},
        compiler_params=pltpu.CompilerParams(vmem_limit_bytes=VMEM_BYTES),
        name="later_levels",
    )(ranks, points, matrices, mine, arrived, *pool)


def plan_kernel(
    chips, limit, chunks, owners, table, counts, slots, rounds, out, stage, own, ahead, used, zeros, sem
):
    parents = owners.shape[0]
    zeros[...] = jnp.zeros_like(zeros)
    fills = []
    for child in range(out.shape[0]):
        for slot in range(out.shape[1]):
            fills.append(pltpu.make_async_copy(zeros, out.at[child, slot], sem.at[len(fills)]))
            part = zeros.at[:, 0]
            fills.append(pltpu.make_async_copy(part, stage.at[child, slot], sem.at[len(fills)]))
    for fill in fills:
        fill.start()
    count = parents // chunks
    rows = chips + 1
    span = limit * LANES

    def clear(index, carry):
        counts[index] = 0
        return carry

    lax.fori_loop(0, 2 * rows * limit, clear, 0)
    for box in range(2 * chips):
        used[box] = 0

    def take_slot(parent, carry):
        owner = owners[parent]
        slot = used[owner]
        slots[parent] = (owner << SLOT_SHIFT) | slot
        used[owner] = slot + 1
        return carry

    lax.fori_loop(0, parents, take_slot, 0)
    width = chips * parents
    pairs = [(chip, goal) for chip in range(1, chips) for goal in range(chip + 1, chips)]
    last = []
    for direction in range(2):

        def true_chip(chip):
            return chip if direction == 0 else chips - 1 - chip

        total = 0
        for box in range(2 * chips):
            hops = true_chip(box // 2)
            total = total + used[box] * (hops * (hops + 1) // 2)

        def one_round(state):
            step, left, ready, own_head, head, tail, older = state
            ready, own_head, head, tail = list(ready), list(own_head), list(head), list(tail)
            for index in range(count):
                parent = jnp.minimum(step * count + index, parents - 1)
                goal = owners[parent] >> 1
                goal = goal if direction == 0 else chips - 1 - goal
                for chip in range(1, chips):
                    own[chip * parents + jnp.minimum(ready[chip], parents - 1)] = parent
                    here = (goal == chip) & (step < chunks)
                    ready[chip] = ready[chip] + here.astype(jnp.int32)
            seen = older[0]
            for chip in range(chips - 1):
                row = (direction * rows + 1 + chip) * limit + step
                sent = jnp.int32(0)
                for goal in range(chips - 1, chip, -1):
                    onward = pairs.index((chip + 1, goal)) if (chip + 1, goal) in pairs else None
                    for forwarded in (True, False):
                        if forwarded and (chip, goal) not in pairs:
                            continue
                        if forwarded:
                            queue = pairs.index((chip, goal))
                            start, stop = head[queue], seen[queue]
                        else:
                            queue = chip * chips + goal
                            start, stop = own_head[queue], ready[goal]
                        number = jnp.minimum(stop - start, LANES - sent)

                        def move(index, carry):
                            if forwarded:
                                code = ahead[queue * width + start + index]
                            else:
                                code = own[goal * parents + start + index]
                                code = code | (true_chip(chip) << CODE_SHIFT)
                            table[row * LANES + sent + index] = code
                            if onward is not None:
                                ahead[onward * width + tail[onward] + index] = code
                            return carry

                        lax.fori_loop(0, number, move, 0)
                        sent = sent + number
                        if onward is not None:
                            tail[onward] = tail[onward] + number
                        if forwarded:
                            head[queue] = start + number
                        else:
                            own_head[queue] = start + number
                counts[row] = sent
                left = left - sent
            return (
                step + 1,
                left,
                tuple(ready),
                tuple(own_head),
                tuple(head),
                tuple(tail),
                tuple(older[1:]) + (tuple(tail),),
            )

        zero = jnp.int32(0)
        none = (zero,) * len(pairs)
        state = lax.while_loop(
            lambda state: (state[1] > 0) & (state[0] < limit),
            one_round,
            (zero, jnp.int32(total), (zero,) * chips, (zero,) * (chips * chips), none, none, (none,) * LAG),
        )
        last.append(state[0])
    rounds[0] = jnp.maximum(last[0], last[1])
    for fill in fills:
        fill.wait()


def plan_switch(owner_row, out_shape):
    parents = owner_row.shape[0]
    chips = out_shape[2]
    anywhere = pl.BlockSpec(memory_space=pl.ANY)
    limit = round_limit(parents)
    smem = pl.BlockSpec(memory_space=pltpu.SMEM)
    return pl.pallas_call(
        functools.partial(plan_kernel, chips, limit, CHUNKS),
        in_specs=[smem],
        out_specs=[smem] * 4 + [anywhere] * 2,
        out_shape=[
            jax.ShapeDtypeStruct((2 * (chips + 1) * limit * LANES,), jnp.int32),
            jax.ShapeDtypeStruct((2 * (chips + 1) * limit,), jnp.int32),
            jax.ShapeDtypeStruct((parents,), jnp.int32),
            jax.ShapeDtypeStruct((1,), jnp.int32),
            jax.ShapeDtypeStruct(out_shape, jnp.float32),
            jax.ShapeDtypeStruct(out_shape[:3] + out_shape[4:], jnp.float32),
        ],
        scratch_shapes=[
            pltpu.SMEM((chips * parents,), jnp.int32),
            pltpu.SMEM((chips * chips * chips * parents,), jnp.int32),
            pltpu.SMEM((2 * chips,), jnp.int32),
            pltpu.VMEM(out_shape[2:], jnp.float32),
            pltpu.SemaphoreType.DMA((2 * out_shape[0] * out_shape[1],)),
        ],
        name="plan_switch",
    )(owner_row)


def round_limit(parents):
    return 4 * parents // LANES


def round_kernel(chips, limit, parents, receives, crossings, staging, high, low, sends, pooled, *refs):
    table, counts, slots, place, now, ranks = refs[:6]
    refs = refs[6:]
    sources = receives + crossings
    received, refs = refs[: 2 * len(sources)], refs[2 * len(sources) :]
    points, matrices = refs[:2] if high is not None or low is not None else (None, None)
    refs = refs[2:] if points is not None else refs
    mine_high, arrived_high = refs[:2] if high is not None else (None, None)
    refs = refs[2:] if high is not None else refs
    mine_low, arrived_low = refs[:2] if low is not None else (None, None)
    refs = refs[2:] if low is not None else refs
    refs = refs[2 + pooled :]
    pool, out, stage = refs[:3]
    outgoing = refs[3 : 3 + 2 * sends]
    merged = refs[3 + 2 * sends] if low is not None else None
    kept, sems = refs[-2:]
    fresh = 0 if high is None else mine_high.shape[0]
    last_sem = LANES * max(2 * len(sources), 2)
    z, core = place[0], place[1]
    odd = z & 1

    def row_of(direction, receiving, step):
        spot = jnp.where(direction == 0, z, chips - 1 - z)
        return (direction * (chips + 1) + (1 - receiving) + spot) * limit + step

    def home(sem, from_chip, parent, source, begin, crossed=False):
        spot = slots[parent]
        owner, slot = spot >> SLOT_SHIFT, spot & ((1 << SLOT_SHIFT) - 1)
        here = (owner >> 1) == z
        same = (owner & 1) == core

        @pl.when(here & same)
        def _():
            from_core = 1 - core if crossed else core
            copy = pltpu.make_async_copy(source, out.at[:, slot, from_chip, from_core], sem)
            copy.start() if begin else copy.wait()

        if staging and not crossed:

            @pl.when(here & jnp.logical_not(same))
            def _():
                copy = pltpu.make_async_copy(source, stage.at[:, slot, from_chip], sem)
                copy.start() if begin else copy.wait()

        return here

    def of_code(code):
        from_chip, parent = code >> CODE_SHIFT, code & ((1 << CODE_SHIFT) - 1)
        return from_chip, parent, from_chip * parents + parent

    def take_in(begin):
        for place_of, back in enumerate(sources):
            crossed = place_of >= len(receives)
            for port in range(2):
                step = now[0] - back
                row = row_of(1 - (odd ^ port), 1, jnp.maximum(step, 0))
                number = jnp.where(step >= 0, counts[row], 0)
                base = (2 * place_of + port) * LANES

                def one(lane, carry):
                    from_chip, parent, held = of_code(table[row * LANES + lane])
                    source = received[2 * place_of + port].at[lane]
                    sem = sems.at[base + lane]
                    here = home(sem, from_chip, parent, source, begin, crossed)
                    if not crossed:

                        @pl.when(jnp.logical_not(here))
                        def _():
                            copy = pltpu.make_async_copy(source, pool.at[held], sem)
                            copy.start() if begin else copy.wait()

                    return carry

                lax.fori_loop(0, number, one, 0)

    def send(begin):
        for port in range(2):
            row = row_of(odd ^ port, 0, now[0])

            def one(lane, carry):
                _, _, held = of_code(table[row * LANES + lane])
                copy = pltpu.make_async_copy(
                    pool.at[held], outgoing[port].at[lane], sems.at[port * LANES + lane]
                )
                copy.start() if begin else copy.wait()
                return carry

            lax.fori_loop(0, counts[row], one, 0)

    def keep(begin):
        def one(member, carry):
            parent = high * fresh + member
            home(sems.at[last_sem + member], z, parent, kept.at[member], begin)
            return carry

        lax.fori_loop(0, fresh, one, 0)

    take_in(True)
    if high is not None:
        rank_width = mine_high.shape[2]
        stacks = [stack_left(matrices[1]), stack_left(matrices[2])]
        for member in range(fresh):
            parent = high * fresh + member
            third = later_parent(
                points[parent],
                stacks,
                ranks_of(ranks, 1, parents, parent),
                ranks_of(ranks, 2, parents, parent),
                mine_high[member],
                arrived_high[member],
            )
            for child in range(2):
                kept[member, child] = third[child * rank_width : (child + 1) * rank_width]
        fill = pltpu.make_async_copy(
            kept, pool.at[pl.ds(z * parents + high * fresh, fresh)], sems.at[last_sem + fresh]
        )
        fill.start()
        keep(True)
    take_in(False)
    if high is not None:
        fill.wait()
    if sends:
        send(True)
    if low is not None:
        matrix = stack_left(matrices[0])
        for member in range(mine_low.shape[0]):
            parent = low * mine_low.shape[0] + member
            results = first_parent(
                points[parent],
                matrix,
                ranks_of(ranks, 0, parents, parent),
                mine_low[member],
                arrived_low[member],
            )
            for box in range(2):
                merged[member, box] = results[box]
    if high is not None:
        keep(False)
    if sends:
        send(False)


def switch_round(plan, place, now, ranks, received, crossed, state, staging, sends, levels=None, high=None, low=None):
    table, counts, slots = plan
    out = state[-2]
    parents = slots.shape[0]
    chips = out.shape[2]
    block = (out.shape[0],) + out.shape[4:]
    inputs = [array for pair in [*received.values(), *crossed.values()] for array in pair]
    waiting = len(inputs)
    if high is not None or low is not None:
        inputs += levels
    for work in (high, low):
        if work is not None:
            inputs += work[1:]
    fresh = 0 if high is None else high[1].shape[0]
    anywhere = pl.BlockSpec(memory_space=pl.ANY)
    inside = pl.BlockSpec(memory_space=pltpu.VMEM)
    shapes = [jax.ShapeDtypeStruct((chips * parents,) + block, jnp.float32)]
    shapes += [jax.ShapeDtypeStruct(array.shape, array.dtype) for array in state[-2:]]
    shapes += [jax.ShapeDtypeStruct((LANES,) + block, jnp.float32)] * (2 * int(sends))
    if low is not None:
        shapes += [jax.ShapeDtypeStruct(low[1].shape, jnp.float32)]
    pooled = len(state) - 2
    first = 6 + len(inputs)
    results = pl.pallas_call(
        functools.partial(
            round_kernel,
            chips,
            round_limit(parents),
            parents,
            tuple(received),
            tuple(crossed),
            staging,
            None if high is None else high[0],
            None if low is None else low[0],
            int(sends),
            pooled,
        ),
        grid_spec=pltpu.PrefetchScalarGridSpec(
            num_scalar_prefetch=6,
            grid=(),
            in_specs=[inside] * len(inputs) + [anywhere] * len(state),
            out_specs=[anywhere] * 3 + [inside] * (len(shapes) - 3),
            scratch_shapes=[
                pltpu.VMEM((max(fresh, 1),) + block, jnp.float32),
                pltpu.SemaphoreType.DMA((LANES * max(waiting, 2) + fresh + 1,)),
            ],
        ),
        out_shape=shapes,
        input_output_aliases={first + index: index + 1 - pooled for index in range(len(state))},
        compiler_params=pltpu.CompilerParams(vmem_limit_bytes=VMEM_BYTES),
        name="switch_round",
    )(table, counts, slots, place, now, ranks, *inputs, *state)
    return tuple(results[:3]), tuple(results[3:])


def join_kernel(place, arrived, out_before, out):
    for child in range(2):
        for chip in range(arrived.shape[2]):
            out[child, 0, chip, 0] = arrived[child, 0, chip]


def join_cores(place, arrived, out):
    children, capacity, chips, _, rank_width, width = out.shape
    return pl.pallas_call(
        join_kernel,
        grid_spec=pltpu.PrefetchScalarGridSpec(
            num_scalar_prefetch=1,
            grid=(capacity,),
            in_specs=[
                pl.BlockSpec(
                    (children, 1, chips, rank_width, width), lambda slot, place: (0, slot, 0, 0, 0)
                ),
                pl.BlockSpec(memory_space=pl.ANY),
            ],
            out_specs=pl.BlockSpec(
                (children, 1, chips, 1, rank_width, width),
                lambda slot, place: (0, slot, 0, 1 - place[1], 0, 0),
            ),
        ),
        out_shape=jax.ShapeDtypeStruct(out.shape, out.dtype),
        input_output_aliases={2: 0},
        compiler_params=pltpu.CompilerParams(vmem_limit_bytes=VMEM_BYTES),
        name="join_cores",
    )(place, arrived, out)


def along_line(value, chips, port):
    pairs = []
    for chip in range(port, chips - 1, 2):
        for core in range(2):
            low, high = 2 * chip + core, 2 * (chip + 1) + core
            pairs += [(low, high), (high, low)]
    return lax.ppermute(value, "box", pairs)


def per_device(
    coeffs,
    skeleton_first,
    skeleton_second,
    skeleton_third,
    checks_first,
    checks_second,
    checks_third,
    ranks_first,
    ranks_second,
    ranks_third,
    interpolants,
    owners,
):
    tbit_index = lax.axis_index("tbit")
    box_index = lax.axis_index("box")
    box_count = lax.axis_size("box")
    parent_count = coeffs.shape[0]
    rank_width = coeffs.shape[3]
    capacity = 2 * parent_count // box_count
    group_count = 2 * box_count
    local_boxes = 2 * box_index + jnp.arange(2, dtype=jnp.int32)[None, :, None]

    def targets_of(checks, per_parent, picked, width):
        boxes = per_parent * parent_count
        absolute = jnp.arange(boxes, dtype=jnp.int32)[:, None] * (NPTS // boxes) + checks
        return lax.dynamic_index_in_dim(absolute.reshape(parent_count, -1, width), picked, 1)

    def first_points(slot):
        box = 4 * local_boxes + 2 * (slot % 2) + slot // 2
        return box * (NPTS // (4 * group_count)) + pick_slot(skeleton_first, slot)

    def second_points(slot):
        box = 2 * local_boxes + slot % 2
        return box * (NPTS // (2 * group_count)) + pick_slot(skeleton_second, slot)

    partner_high = jnp.bitwise_xor(tbit_index, 2)
    partner_low = jnp.bitwise_xor(tbit_index, 1)
    points_third = local_boxes * (NPTS // group_count) + pick_slot(skeleton_third, tbit_index)
    low_targets = jnp.concatenate(
        [
            targets_of(checks_first, 2, tbit_index // 2, rank_width),
            targets_of(checks_second, 4, tbit_index, rank_width),
        ],
        axis=2,
    )
    high_targets = targets_of(checks_third, 8, tbit_index, 2 * rank_width)
    points = jnp.concatenate(
        [
            jnp.concatenate([first_points(tbit_index), first_points(partner_high)], axis=2),
            jnp.concatenate([second_points(tbit_index), second_points(partner_low)], axis=2),
            points_third.reshape(parent_count, 1, 2 * rank_width),
            low_targets,
            high_targets,
            jnp.zeros_like(high_targets),
        ],
        axis=1,
    )
    rank_three = lax.dynamic_index_in_dim(
        lax.dynamic_index_in_dim(ranks_third, tbit_index, 1, keepdims=False),
        box_index,
        2,
        keepdims=False,
    )
    ranks = jnp.concatenate(
        [ranks_first.reshape(-1), ranks_second.reshape(-1), rank_three.reshape(-1)]
    )

    mine = coeffs[:, :, 0]
    count = parent_count // CHUNKS
    chips = box_count // 2
    networked = chips <= 4
    place = jnp.stack([box_index // 2, box_index % 2]).astype(jnp.int32)
    owner_row = lax.dynamic_index_in_dim(owners, tbit_index, 0, keepdims=False)
    width = coeffs.shape[-1]
    pool_shape = (chips * parent_count, 2, rank_width, width)
    if not networked:
        pool_shape = (parent_count, 2, rank_width, width)

    parts, arrived = [mine[:count]], []
    others, _ = lax.optimization_barrier((mine, parts[0]))
    for chunk in range(1, CHUNKS):
        parts.append(others[chunk * count : (chunk + 1) * count])

    def start_low(chunk, after):
        outgoing = parts[chunk]
        if after is not None:
            outgoing, _ = lax.optimization_barrier((outgoing, after))
        arrived.append(swapped(outgoing, "tbit", 1))

    firsts, second_arrived = [], []

    def start_high(first):
        firsts.append(first)
        second_arrived.append(swapped(first, "tbit", 0))

    def low_level(chunk):
        return first_level(chunk, ranks, points, interpolants, parts[chunk], arrived[chunk])

    early = 4 if networked else CHUNKS
    for chunk in range(early):
        start_low(chunk, arrived[-1] if chunk else None)
    start_high(low_level(0))
    if networked:
        owner_row, _ = lax.optimization_barrier((owner_row, firsts[0]))
        out_shape = (2, capacity, chips, 2, rank_width, width)
        *plan, rounds, out, stage = plan_switch(owner_row, out_shape)
        arrived[1], plan, rounds, out, stage = lax.optimization_barrier(
            (arrived[1], plan, rounds, out, stage)
        )
        most = jnp.broadcast_to(rounds, (8, 128))
        most = jnp.maximum(most, swapped(most, "tbit", 1))
        most = jnp.maximum(most, swapped(most, "tbit", 0))
        most = jnp.maximum(most[0, 0], STATIC_ROUNDS)
        arrived[3], most = lax.optimization_barrier((arrived[3], most))
    start_high(low_level(1))
    if not networked:
        for chunk in range(2, CHUNKS):
            start_high(low_level(chunk))
        pool = ()
        for chunk in range(CHUNKS):
            pool = (
                later_levels(
                    chunk, ranks, points, interpolants, firsts[chunk], second_arrived[chunk], pool_shape, pool
                ),
            )
        (pool,) = pool
        slot_parent, slot_used = slot_table(owner_row, box_count, capacity)
        outgoing = jnp.take(jnp.swapaxes(pool, 0, 1), slot_parent.T, axis=1)
        outgoing = jnp.where(slot_used.T[None, :, :, None, None], outgoing, 0.0)
        switched = lax.all_to_all(outgoing, "box", split_axis=2, concat_axis=2, tiled=True)
        return switched[None, None]

    state = (out, stage)
    received, crossed = {}, {}

    def exchange(packed):
        return (along_line(packed[0], chips, 0), along_line(packed[1], chips, 1))

    def cross(value):
        return lax.ppermute(value, "box", [(box, box ^ 1) for box in range(box_count)])

    def cross_pair(pair):
        return (cross(pair[0]), cross(pair[1]))

    staged = CHUNKS - LAG + 1
    for step in range(STATIC_ROUNDS):
        high, low = None, None
        if step < CHUNKS:
            high = (step, firsts[step], second_arrived[step])
        if step + 2 < CHUNKS:
            low = (step + 2, parts[step + 2], arrived[step + 2])
        state, results = switch_round(
            plan,
            place,
            jnp.full((1,), step, jnp.int32),
            ranks,
            {LAG: received[step - LAG]} if step >= LAG else {},
            {CROSS_LAG: crossed[step - CROSS_LAG]} if step - CROSS_LAG >= staged else {},
            state,
            step <= CHUNKS,
            True,
            [points, interpolants],
            high,
            low,
        )
        received[step] = exchange(results[:2])
        if low is not None:
            start_high(results[2])
        if step + 4 < CHUNKS:
            start_low(step + 4, results[0])
        if step >= staged:
            crossed[step] = cross_pair(received[step])
        if step == CHUNKS:
            stage_crossed = cross(state[2])
        if step == staged + CROSS_LAG - 1:
            state = (state[0], join_cores(place, stage_crossed, state[1]), state[2])

    def more(carry):
        return carry[0] < most

    def again(carry):
        step, state, (older, newer), pending = carry
        state, packed = switch_round(
            plan, place, step[None], ranks, {LAG: older}, {CROSS_LAG: pending[0]}, state, False, True
        )
        return (step + 1, state, (newer, exchange(packed)), pending[1:] + (cross_pair(newer),))

    final = STATIC_ROUNDS
    step, state, (older, newer), pending = lax.while_loop(
        more,
        again,
        (
            jnp.int32(final),
            state,
            (received[final - 2], received[final - 1]),
            tuple(crossed[final - back] for back in range(CROSS_LAG, 1, -1)),
        ),
    )
    pending = pending + (cross_pair(newer),)
    state, _ = switch_round(
        plan,
        place,
        step[None],
        ranks,
        {2: older, 1: newer},
        {CROSS_LAG - index: pair for index, pair in enumerate(pending)},
        state,
        False,
        False,
    )
    return state[1].reshape(1, 1, 2, capacity, box_count, rank_width, width)


def solution(mesh):
    return jax.shard_map(
        per_device,
        mesh=mesh,
        in_specs=(
            P(None, "box", "tbit", None, None),
            P(None, "box", None, None),
            P(None, "box", None, None),
            P(None, "box", None, None),
            P(),
            P(),
            P(),
            P(None, "box", "tbit"),
            P(None, "box", "tbit"),
            P(),
            P(),
            P(),
        ),
        out_specs=P("tbit", "box", None, None, None, None, None),
        check_vma=False,
    )
```

```python
import functools
import math

import jax
import jax.numpy as jnp
from jax import lax
from jax.experimental import pallas as pl
from jax.experimental.pallas import tpu as pltpu
from jax.sharding import PartitionSpec as P

NPTS = 1048576
PHASE_BITS = 20
CHUNKS = 16
LANES = 4
LAG = 2
CROSS_LAG = 4
STATIC_ROUNDS = 22
PER_STEP = 4
VMEM_BYTES = 32 * 1024 * 1024
CODE_SHIFT = 16
SLOT_SHIFT = 16
POINTS_SECOND = 2
POINTS_THIRD = 4
TARGETS_LOW = 5
TARGETS_HIGH = 6

SIN_TERMS = (
    1.0,
    -1.0 / 6.0,
    1.0 / 120.0,
    -1.0 / 5040.0,
    1.0 / 362880.0,
    -1.0 / 39916800.0,
    1.0 / 6227020800.0,
)


def swapped(value, axis, bit):
    mask = 2**bit
    pairs = [(source, source ^ mask) for source in range(lax.axis_size(axis))]
    return lax.ppermute(value, axis, pairs)


def slot_table(owner_row, box_count, capacity):
    parent_count = owner_row.shape[0]
    onehot = (owner_row[:, None] == jnp.arange(box_count, dtype=jnp.int32)[None, :]).astype(
        jnp.int32
    )
    earlier = jnp.cumsum(onehot, axis=0, dtype=jnp.int32) - onehot
    slot_of = jnp.sum(earlier * onehot, axis=1, dtype=jnp.int32)
    matches = (onehot.T[:, None, :] == 1) & (
        slot_of[None, None, :] == jnp.arange(capacity, dtype=jnp.int32)[None, :, None]
    )
    slot_parent = jnp.sum(
        jnp.where(matches, jnp.arange(parent_count, dtype=jnp.int32)[None, None, :], 0), axis=2
    )
    slot_used = jnp.any(matches, axis=2)
    return (slot_parent, slot_used)


def pick_slot(values, position):
    return lax.dynamic_index_in_dim(values, position, 2, keepdims=False)


def cos_kernel(targets, points):
    shift = 32 - PHASE_BITS
    phase = lax.shift_right_arithmetic(
        lax.shift_left(targets * points, jnp.int32(shift)), jnp.int32(shift)
    )
    offset = NPTS // 4 - jnp.abs(phase)
    y = offset.astype(jnp.float32) * jnp.float32(2.0 * math.pi / NPTS)
    square = y * y
    total = jnp.float32(SIN_TERMS[-1])
    for term in SIN_TERMS[-2::-1]:
        total = total * square + jnp.float32(term)
    return total * y


def split(value):
    high = value.astype(jnp.bfloat16)
    low = (value - high.astype(jnp.float32)).astype(jnp.bfloat16)
    return high, low


def stack_left(value):
    high, low = split(value)
    return jnp.concatenate(
        [jnp.concatenate([high, high], axis=1), jnp.concatenate([low, low], axis=1)], axis=0
    )


def product(left, right):
    rows = left.shape[0] // 2
    both = jnp.dot(
        left, jnp.concatenate(split(right), axis=0), preferred_element_type=jnp.float32
    )
    return both[:rows] + both[rows:]


def live(weights, rank):
    rows = lax.broadcasted_iota(jnp.int32, weights.shape, 0)
    return jnp.where(rows < rank, weights, 0.0)


def column(tile, row, begin, length):
    return jnp.transpose(tile)[begin : begin + length, row : row + 1]


def pair_weights(matrix, left, right, left_rank, right_rank):
    width = left.shape[1]
    both = product(matrix, jnp.concatenate([left, right], axis=1))
    return live(both[:, :width], left_rank), live(both[:, width:], right_rank)


def first_parent(tile, matrix, ranks, mine, arrived):
    rank_width = mine.shape[1]
    targets = column(tile, TARGETS_LOW, 0, rank_width)
    kernels = [cos_kernel(targets, tile[box : box + 1]) for box in range(2)]
    weights = pair_weights(matrix, *kernels, *ranks)
    return [
        product(stack_left(weights[box]), jnp.concatenate([mine[box], arrived[box]], axis=0))
        for box in range(2)
    ]


def later_parent(tile, matrices, ranks_second, ranks_third, mine, arrived):
    rank_width = mine.shape[1]
    targets = column(tile, TARGETS_LOW, rank_width, rank_width)
    kernels = [
        cos_kernel(targets, tile[POINTS_SECOND + box : POINTS_SECOND + box + 1]) for box in range(2)
    ]
    weights = pair_weights(matrices[0], *kernels, *ranks_second)
    seconds = [
        product(stack_left(weights[box]), jnp.concatenate([mine[box], arrived[box]], axis=0))
        for box in range(2)
    ]
    targets = column(tile, TARGETS_HIGH, 0, 2 * rank_width)
    kernel = cos_kernel(targets, tile[POINTS_THIRD : POINTS_THIRD + 1])
    weights = pair_weights(matrices[1], kernel[:rank_width], kernel[rank_width:], *ranks_third)
    stacked = jnp.concatenate(seconds, axis=0)
    return product(stack_left(jnp.concatenate(weights, axis=0)), stacked)


def ranks_of(ranks, level, parents, parent):
    start = 2 * (level * parents + parent)
    return ranks[start], ranks[start + 1]


def first_kernel(chunk, parents, ranks, points, matrices, mine, arrived, merged):
    matrix = stack_left(matrices[0])
    for member in range(mine.shape[0]):
        parent = (chunk * pl.num_programs(0) + pl.program_id(0)) * mine.shape[0] + member
        results = first_parent(
            points[member], matrix, ranks_of(ranks, 0, parents, parent), mine[member], arrived[member]
        )
        for box in range(2):
            merged[member, box] = results[box]


def later_kernel(chunk, parents, ranks, points, matrices, mine, arrived, *pool):
    merged = pool[-1]
    rank_width = mine.shape[2]
    stacks = [stack_left(matrices[1]), stack_left(matrices[2])]
    for member in range(mine.shape[0]):
        parent = (chunk * pl.num_programs(0) + pl.program_id(0)) * mine.shape[0] + member
        third = later_parent(
            points[member],
            stacks,
            ranks_of(ranks, 1, parents, parent),
            ranks_of(ranks, 2, parents, parent),
            mine[member],
            arrived[member],
        )
        for child in range(2):
            merged[member, child] = third[child * rank_width : (child + 1) * rank_width]


def chunk_spec(shape, chunk, steps, per_step):
    block = (per_step,) + tuple(shape[1:])
    rest = (0,) * (len(shape) - 1)
    return pl.BlockSpec(block, lambda step, *_: (chunk * steps + step,) + rest)


def whole_spec(shape):
    rest = (0,) * len(shape)
    return pl.BlockSpec(tuple(shape), lambda step, *_: rest)


def first_level(chunk, ranks, points, matrices, mine, arrived):
    per_step = PER_STEP
    steps = mine.shape[0] // per_step
    return pl.pallas_call(
        functools.partial(first_kernel, chunk, points.shape[0]),
        grid_spec=pltpu.PrefetchScalarGridSpec(
            num_scalar_prefetch=1,
            grid=(steps,),
            in_specs=[
                chunk_spec(points.shape, chunk, steps, per_step),
                whole_spec(matrices.shape),
                chunk_spec(mine.shape, 0, steps, per_step),
                chunk_spec(arrived.shape, 0, steps, per_step),
            ],
            out_specs=chunk_spec(arrived.shape, 0, steps, per_step),
        ),
        out_shape=jax.ShapeDtypeStruct(arrived.shape, jnp.float32),
        compiler_params=pltpu.CompilerParams(vmem_limit_bytes=VMEM_BYTES),
        name="first_level",
    )(ranks, points, matrices, mine, arrived)


def later_levels(chunk, ranks, points, matrices, mine, arrived, pool_shape, pool):
    per_step = PER_STEP
    steps = mine.shape[0] // per_step
    return pl.pallas_call(
        functools.partial(later_kernel, chunk, points.shape[0]),
        grid_spec=pltpu.PrefetchScalarGridSpec(
            num_scalar_prefetch=1,
            grid=(steps,),
            in_specs=[
                chunk_spec(points.shape, chunk, steps, per_step),
                whole_spec(matrices.shape),
                chunk_spec(mine.shape, 0, steps, per_step),
                chunk_spec(arrived.shape, 0, steps, per_step),
            ]
            + [pl.BlockSpec(memory_space=pl.ANY)] * len(pool),
            out_specs=chunk_spec(pool_shape, chunk, steps, per_step),
        ),
        out_shape=jax.ShapeDtypeStruct(pool_shape, jnp.float32),
        input_output_aliases={5: 0} if pool else {},
        compiler_params=pltpu.CompilerParams(vmem_limit_bytes=VMEM_BYTES),
        name="later_levels",
    )(ranks, points, matrices, mine, arrived, *pool)


def plan_kernel(
    chips, limit, chunks, owners, table, counts, slots, rounds, out, stage, own, ahead, used, zeros, sem
):
    parents = owners.shape[0]
    zeros[...] = jnp.zeros_like(zeros)
    fills = []
    for child in range(out.shape[0]):
        for slot in range(out.shape[1]):
            fills.append(pltpu.make_async_copy(zeros, out.at[child, slot], sem.at[len(fills)]))
            part = zeros.at[:, 0]
            fills.append(pltpu.make_async_copy(part, stage.at[child, slot], sem.at[len(fills)]))
    for fill in fills:
        fill.start()
    count = parents // chunks
    rows = chips + 1
    span = limit * LANES

    def clear(index, carry):
        counts[index] = 0
        return carry

    lax.fori_loop(0, 2 * rows * limit, clear, 0)
    for box in range(2 * chips):
        used[box] = 0

    def take_slot(parent, carry):
        owner = owners[parent]
        slot = used[owner]
        slots[parent] = (owner << SLOT_SHIFT) | slot
        used[owner] = slot + 1
        return carry

    lax.fori_loop(0, parents, take_slot, 0)
    width = chips * parents
    pairs = [(chip, goal) for chip in range(1, chips) for goal in range(chip + 1, chips)]
    last = []
    for direction in range(2):

        def true_chip(chip):
            return chip if direction == 0 else chips - 1 - chip

        total = 0
        for box in range(2 * chips):
            hops = true_chip(box // 2)
            total = total + used[box] * (hops * (hops + 1) // 2)

        def one_round(state):
            step, left, ready, own_head, head, tail, older = state
            ready, own_head, head, tail = list(ready), list(own_head), list(head), list(tail)
            for index in range(count):
                parent = jnp.minimum(step * count + index, parents - 1)
                goal = owners[parent] >> 1
                goal = goal if direction == 0 else chips - 1 - goal
                for chip in range(1, chips):
                    own[chip * parents + jnp.minimum(ready[chip], parents - 1)] = parent
                    here = (goal == chip) & (step < chunks)
                    ready[chip] = ready[chip] + here.astype(jnp.int32)
            seen = older[0]
            for chip in range(chips - 1):
                row = (direction * rows + 1 + chip) * limit + step
                sent = jnp.int32(0)
                for goal in range(chips - 1, chip, -1):
                    onward = pairs.index((chip + 1, goal)) if (chip + 1, goal) in pairs else None
                    for forwarded in (True, False):
                        if forwarded and (chip, goal) not in pairs:
                            continue
                        if forwarded:
                            queue = pairs.index((chip, goal))
                            start, stop = head[queue], seen[queue]
                        else:
                            queue = chip * chips + goal
                            start, stop = own_head[queue], ready[goal]
                        number = jnp.minimum(stop - start, LANES - sent)

                        def move(index, carry):
                            if forwarded:
                                code = ahead[queue * width + start + index]
                            else:
                                code = own[goal * parents + start + index]
                                code = code | (true_chip(chip) << CODE_SHIFT)
                            table[row * LANES + sent + index] = code
                            if onward is not None:
                                ahead[onward * width + tail[onward] + index] = code
                            return carry

                        lax.fori_loop(0, number, move, 0)
                        sent = sent + number
                        if onward is not None:
                            tail[onward] = tail[onward] + number
                        if forwarded:
                            head[queue] = start + number
                        else:
                            own_head[queue] = start + number
                counts[row] = sent
                left = left - sent
            return (
                step + 1,
                left,
                tuple(ready),
                tuple(own_head),
                tuple(head),
                tuple(tail),
                tuple(older[1:]) + (tuple(tail),),
            )

        zero = jnp.int32(0)
        none = (zero,) * len(pairs)
        state = lax.while_loop(
            lambda state: (state[1] > 0) & (state[0] < limit),
            one_round,
            (zero, jnp.int32(total), (zero,) * chips, (zero,) * (chips * chips), none, none, (none,) * LAG),
        )
        last.append(state[0])
    rounds[0] = jnp.maximum(last[0], last[1])
    for fill in fills:
        fill.wait()


def plan_switch(owner_row, out_shape):
    parents = owner_row.shape[0]
    chips = out_shape[2]
    anywhere = pl.BlockSpec(memory_space=pl.ANY)
    limit = round_limit(parents)
    smem = pl.BlockSpec(memory_space=pltpu.SMEM)
    return pl.pallas_call(
        functools.partial(plan_kernel, chips, limit, CHUNKS),
        in_specs=[smem],
        out_specs=[smem] * 4 + [anywhere] * 2,
        out_shape=[
            jax.ShapeDtypeStruct((2 * (chips + 1) * limit * LANES,), jnp.int32),
            jax.ShapeDtypeStruct((2 * (chips + 1) * limit,), jnp.int32),
            jax.ShapeDtypeStruct((parents,), jnp.int32),
            jax.ShapeDtypeStruct((1,), jnp.int32),
            jax.ShapeDtypeStruct(out_shape, jnp.float32),
            jax.ShapeDtypeStruct(out_shape[:3] + out_shape[4:], jnp.float32),
        ],
        scratch_shapes=[
            pltpu.SMEM((chips * parents,), jnp.int32),
            pltpu.SMEM((chips * chips * chips * parents,), jnp.int32),
            pltpu.SMEM((2 * chips,), jnp.int32),
            pltpu.VMEM(out_shape[2:], jnp.float32),
            pltpu.SemaphoreType.DMA((2 * out_shape[0] * out_shape[1],)),
        ],
        name="plan_switch",
    )(owner_row)


def round_limit(parents):
    return 4 * parents // LANES


def round_kernel(chips, limit, parents, receives, crossings, staging, high, low, sends, pooled, *refs):
    table, counts, slots, place, now, ranks = refs[:6]
    refs = refs[6:]
    sources = receives + crossings
    received, refs = refs[: 2 * len(sources)], refs[2 * len(sources) :]
    points, matrices = refs[:2] if high is not None or low is not None else (None, None)
    refs = refs[2:] if points is not None else refs
    mine_high, arrived_high = refs[:2] if high is not None else (None, None)
    refs = refs[2:] if high is not None else refs
    mine_low, arrived_low = refs[:2] if low is not None else (None, None)
    refs = refs[2:] if low is not None else refs
    refs = refs[2 + pooled :]
    pool, out, stage = refs[:3]
    outgoing = refs[3 : 3 + 2 * sends]
    merged = refs[3 + 2 * sends] if low is not None else None
    kept, sems = refs[-2:]
    fresh = 0 if high is None else mine_high.shape[0]
    last_sem = LANES * max(2 * len(sources), 2)
    z, core = place[0], place[1]
    odd = z & 1

    def row_of(direction, receiving, step):
        spot = jnp.where(direction == 0, z, chips - 1 - z)
        return (direction * (chips + 1) + (1 - receiving) + spot) * limit + step

    def home(sem, from_chip, parent, source, begin, crossed=False):
        spot = slots[parent]
        owner, slot = spot >> SLOT_SHIFT, spot & ((1 << SLOT_SHIFT) - 1)
        here = (owner >> 1) == z
        same = (owner & 1) == core

        @pl.when(here & same)
        def _():
            from_core = 1 - core if crossed else core
            copy = pltpu.make_async_copy(source, out.at[:, slot, from_chip, from_core], sem)
            copy.start() if begin else copy.wait()

        if staging and not crossed:

            @pl.when(here & jnp.logical_not(same))
            def _():
                copy = pltpu.make_async_copy(source, stage.at[:, slot, from_chip], sem)
                copy.start() if begin else copy.wait()

        return here

    def of_code(code):
        from_chip, parent = code >> CODE_SHIFT, code & ((1 << CODE_SHIFT) - 1)
        return from_chip, parent, from_chip * parents + parent

    def take_in(begin):
        for place_of, back in enumerate(sources):
            crossed = place_of >= len(receives)
            for port in range(2):
                step = now[0] - back
                row = row_of(1 - (odd ^ port), 1, jnp.maximum(step, 0))
                number = jnp.where(step >= 0, counts[row], 0)
                base = (2 * place_of + port) * LANES

                def one(lane, carry):
                    from_chip, parent, held = of_code(table[row * LANES + lane])
                    source = received[2 * place_of + port].at[lane]
                    sem = sems.at[base + lane]
                    here = home(sem, from_chip, parent, source, begin, crossed)
                    if not crossed:

                        @pl.when(jnp.logical_not(here))
                        def _():
                            copy = pltpu.make_async_copy(source, pool.at[held], sem)
                            copy.start() if begin else copy.wait()

                    return carry

                lax.fori_loop(0, number, one, 0)

    def send(begin):
        for port in range(2):
            row = row_of(odd ^ port, 0, now[0])

            def one(lane, carry):
                _, _, held = of_code(table[row * LANES + lane])
                copy = pltpu.make_async_copy(
                    pool.at[held], outgoing[port].at[lane], sems.at[port * LANES + lane]
                )
                copy.start() if begin else copy.wait()
                return carry

            lax.fori_loop(0, counts[row], one, 0)

    def keep(begin):
        def one(member, carry):
            parent = high * fresh + member
            home(sems.at[last_sem + member], z, parent, kept.at[member], begin)
            return carry

        lax.fori_loop(0, fresh, one, 0)

    take_in(True)
    if high is not None:
        rank_width = mine_high.shape[2]
        stacks = [stack_left(matrices[1]), stack_left(matrices[2])]
        for member in range(fresh):
            parent = high * fresh + member
            third = later_parent(
                points[parent],
                stacks,
                ranks_of(ranks, 1, parents, parent),
                ranks_of(ranks, 2, parents, parent),
                mine_high[member],
                arrived_high[member],
            )
            for child in range(2):
                kept[member, child] = third[child * rank_width : (child + 1) * rank_width]
        fill = pltpu.make_async_copy(
            kept, pool.at[pl.ds(z * parents + high * fresh, fresh)], sems.at[last_sem + fresh]
        )
        fill.start()
        keep(True)
    take_in(False)
    if high is not None:
        fill.wait()
    if sends:
        send(True)
    if low is not None:
        matrix = stack_left(matrices[0])
        for member in range(mine_low.shape[0]):
            parent = low * mine_low.shape[0] + member
            results = first_parent(
                points[parent],
                matrix,
                ranks_of(ranks, 0, parents, parent),
                mine_low[member],
                arrived_low[member],
            )
            for box in range(2):
                merged[member, box] = results[box]
    if high is not None:
        keep(False)
    if sends:
        send(False)


def switch_round(plan, place, now, ranks, received, crossed, state, staging, sends, levels=None, high=None, low=None):
    table, counts, slots = plan
    out = state[-2]
    parents = slots.shape[0]
    chips = out.shape[2]
    block = (out.shape[0],) + out.shape[4:]
    inputs = [array for pair in [*received.values(), *crossed.values()] for array in pair]
    waiting = len(inputs)
    if high is not None or low is not None:
        inputs += levels
    for work in (high, low):
        if work is not None:
            inputs += work[1:]
    fresh = 0 if high is None else high[1].shape[0]
    anywhere = pl.BlockSpec(memory_space=pl.ANY)
    inside = pl.BlockSpec(memory_space=pltpu.VMEM)
    shapes = [jax.ShapeDtypeStruct((chips * parents,) + block, jnp.float32)]
    shapes += [jax.ShapeDtypeStruct(array.shape, array.dtype) for array in state[-2:]]
    shapes += [jax.ShapeDtypeStruct((LANES,) + block, jnp.float32)] * (2 * int(sends))
    if low is not None:
        shapes += [jax.ShapeDtypeStruct(low[1].shape, jnp.float32)]
    pooled = len(state) - 2
    first = 6 + len(inputs)
    results = pl.pallas_call(
        functools.partial(
            round_kernel,
            chips,
            round_limit(parents),
            parents,
            tuple(received),
            tuple(crossed),
            staging,
            None if high is None else high[0],
            None if low is None else low[0],
            int(sends),
            pooled,
        ),
        grid_spec=pltpu.PrefetchScalarGridSpec(
            num_scalar_prefetch=6,
            grid=(),
            in_specs=[inside] * len(inputs) + [anywhere] * len(state),
            out_specs=[anywhere] * 3 + [inside] * (len(shapes) - 3),
            scratch_shapes=[
                pltpu.VMEM((max(fresh, 1),) + block, jnp.float32),
                pltpu.SemaphoreType.DMA((LANES * max(waiting, 2) + fresh + 1,)),
            ],
        ),
        out_shape=shapes,
        input_output_aliases={first + index: index + 1 - pooled for index in range(len(state))},
        compiler_params=pltpu.CompilerParams(vmem_limit_bytes=VMEM_BYTES),
        name="switch_round",
    )(table, counts, slots, place, now, ranks, *inputs, *state)
    return tuple(results[:3]), tuple(results[3:])


def join_kernel(place, arrived, out_before, out):
    for child in range(2):
        for chip in range(arrived.shape[2]):
            out[child, 0, chip, 0] = arrived[child, 0, chip]


def join_cores(place, arrived, out):
    children, capacity, chips, _, rank_width, width = out.shape
    return pl.pallas_call(
        join_kernel,
        grid_spec=pltpu.PrefetchScalarGridSpec(
            num_scalar_prefetch=1,
            grid=(capacity,),
            in_specs=[
                pl.BlockSpec(
                    (children, 1, chips, rank_width, width), lambda slot, place: (0, slot, 0, 0, 0)
                ),
                pl.BlockSpec(memory_space=pl.ANY),
            ],
            out_specs=pl.BlockSpec(
                (children, 1, chips, 1, rank_width, width),
                lambda slot, place: (0, slot, 0, 1 - place[1], 0, 0),
            ),
        ),
        out_shape=jax.ShapeDtypeStruct(out.shape, out.dtype),
        input_output_aliases={2: 0},
        compiler_params=pltpu.CompilerParams(vmem_limit_bytes=VMEM_BYTES),
        name="join_cores",
    )(place, arrived, out)


def along_line(value, chips, port):
    pairs = []
    for chip in range(port, chips - 1, 2):
        for core in range(2):
            low, high = 2 * chip + core, 2 * (chip + 1) + core
            pairs += [(low, high), (high, low)]
    return lax.ppermute(value, "box", pairs)


def per_device(
    coeffs,
    skeleton_first,
    skeleton_second,
    skeleton_third,
    checks_first,
    checks_second,
    checks_third,
    ranks_first,
    ranks_second,
    ranks_third,
    interpolants,
    owners,
):
    tbit_index = lax.axis_index("tbit")
    box_index = lax.axis_index("box")
    box_count = lax.axis_size("box")
    parent_count = coeffs.shape[0]
    rank_width = coeffs.shape[3]
    capacity = 2 * parent_count // box_count
    group_count = 2 * box_count
    local_boxes = 2 * box_index + jnp.arange(2, dtype=jnp.int32)[None, :, None]

    def targets_of(checks, per_parent, picked, width):
        boxes = per_parent * parent_count
        absolute = jnp.arange(boxes, dtype=jnp.int32)[:, None] * (NPTS // boxes) + checks
        return lax.dynamic_index_in_dim(absolute.reshape(parent_count, -1, width), picked, 1)

    def first_points(slot):
        box = 4 * local_boxes + 2 * (slot % 2) + slot // 2
        return box * (NPTS // (4 * group_count)) + pick_slot(skeleton_first, slot)

    def second_points(slot):
        box = 2 * local_boxes + slot % 2
        return box * (NPTS // (2 * group_count)) + pick_slot(skeleton_second, slot)

    partner_high = jnp.bitwise_xor(tbit_index, 2)
    partner_low = jnp.bitwise_xor(tbit_index, 1)
    points_third = local_boxes * (NPTS // group_count) + pick_slot(skeleton_third, tbit_index)
    low_targets = jnp.concatenate(
        [
            targets_of(checks_first, 2, tbit_index // 2, rank_width),
            targets_of(checks_second, 4, tbit_index, rank_width),
        ],
        axis=2,
    )
    high_targets = targets_of(checks_third, 8, tbit_index, 2 * rank_width)
    points = jnp.concatenate(
        [
            jnp.concatenate([first_points(tbit_index), first_points(partner_high)], axis=2),
            jnp.concatenate([second_points(tbit_index), second_points(partner_low)], axis=2),
            points_third.reshape(parent_count, 1, 2 * rank_width),
            low_targets,
            high_targets,
            jnp.zeros_like(high_targets),
        ],
        axis=1,
    )
    rank_three = lax.dynamic_index_in_dim(
        lax.dynamic_index_in_dim(ranks_third, tbit_index, 1, keepdims=False),
        box_index,
        2,
        keepdims=False,
    )
    ranks = jnp.concatenate(
        [ranks_first.reshape(-1), ranks_second.reshape(-1), rank_three.reshape(-1)]
    )

    mine = coeffs[:, :, 0]
    count = parent_count // CHUNKS
    chips = box_count // 2
    networked = chips <= 4
    place = jnp.stack([box_index // 2, box_index % 2]).astype(jnp.int32)
    owner_row = lax.dynamic_index_in_dim(owners, tbit_index, 0, keepdims=False)
    width = coeffs.shape[-1]
    pool_shape = (chips * parent_count, 2, rank_width, width)
    if not networked:
        pool_shape = (parent_count, 2, rank_width, width)

    parts, arrived = [mine[:count]], []
    others, _ = lax.optimization_barrier((mine, parts[0]))
    for chunk in range(1, CHUNKS):
        parts.append(others[chunk * count : (chunk + 1) * count])

    def start_low(chunk, after):
        outgoing = parts[chunk]
        if after is not None:
            outgoing, _ = lax.optimization_barrier((outgoing, after))
        arrived.append(swapped(outgoing, "tbit", 1))

    firsts, second_arrived = [], []

    def start_high(first):
        firsts.append(first)
        second_arrived.append(swapped(first, "tbit", 0))

    def low_level(chunk):
        return first_level(chunk, ranks, points, interpolants, parts[chunk], arrived[chunk])

    start_low(0, None)
    if networked:
        start_low(1, arrived[0])
        start_low(2, arrived[0])
    else:
        for chunk in range(1, CHUNKS):
            start_low(chunk, arrived[-1])
    start_high(low_level(0))
    if networked:
        owner_row, _ = lax.optimization_barrier((owner_row, firsts[0]))
        out_shape = (2, capacity, chips, 2, rank_width, width)
        *plan, rounds, out, stage = plan_switch(owner_row, out_shape)
        arrived[1], plan, rounds, out, stage = lax.optimization_barrier(
            (arrived[1], plan, rounds, out, stage)
        )
        most = jnp.broadcast_to(rounds, (8, 128))
    start_high(low_level(1))
    if networked:
        start_low(3, firsts[1])
    if not networked:
        for chunk in range(2, CHUNKS):
            start_high(low_level(chunk))
        pool = ()
        for chunk in range(CHUNKS):
            pool = (
                later_levels(
                    chunk, ranks, points, interpolants, firsts[chunk], second_arrived[chunk], pool_shape, pool
                ),
            )
        (pool,) = pool
        slot_parent, slot_used = slot_table(owner_row, box_count, capacity)
        outgoing = jnp.take(jnp.swapaxes(pool, 0, 1), slot_parent.T, axis=1)
        outgoing = jnp.where(slot_used.T[None, :, :, None, None], outgoing, 0.0)
        switched = lax.all_to_all(outgoing, "box", split_axis=2, concat_axis=2, tiled=True)
        return switched[None, None]

    state = (out, stage)
    received, crossed = {}, {}

    def exchange(packed):
        return (along_line(packed[0], chips, 0), along_line(packed[1], chips, 1))

    def cross(value):
        return lax.ppermute(value, "box", [(box, box ^ 1) for box in range(box_count)])

    def cross_pair(pair):
        return (cross(pair[0]), cross(pair[1]))

    staged = CHUNKS - LAG + 1
    for step in range(STATIC_ROUNDS):
        high, low = None, None
        if step < CHUNKS:
            high = (step, firsts[step], second_arrived[step])
        if step + 2 < CHUNKS:
            low = (step + 2, parts[step + 2], arrived[step + 2])
        state, results = switch_round(
            plan,
            place,
            jnp.full((1,), step, jnp.int32),
            ranks,
            {LAG: received[step - LAG]} if step >= LAG else {},
            {CROSS_LAG: crossed[step - CROSS_LAG]} if step - CROSS_LAG >= staged else {},
            state,
            step <= CHUNKS,
            True,
            [points, interpolants],
            high,
            low,
        )
        received[step] = exchange(results[:2])
        if low is not None:
            start_high(results[2])
        if step + 4 < CHUNKS:
            start_low(step + 4, results[0])
        if step >= staged:
            crossed[step] = cross_pair(received[step])
        if step == CHUNKS:
            stage_crossed = cross(state[2])
        if step in (6, 11):
            most, _ = lax.optimization_barrier((most, results[0]))
            most = jnp.maximum(most, swapped(most, "tbit", 1 if step == 6 else 0))
        if step == staged + CROSS_LAG - 2:
            state = (state[0], join_cores(place, stage_crossed, state[1]), state[2])

    most = jnp.maximum(most[0, 0], STATIC_ROUNDS)

    def more(carry):
        return carry[0] < most

    def again(carry):
        step, state, (older, newer), pending = carry
        state, packed = switch_round(
            plan, place, step[None], ranks, {LAG: older}, {CROSS_LAG: pending[0]}, state, False, True
        )
        return (step + 1, state, (newer, exchange(packed)), pending[1:] + (cross_pair(newer),))

    final = STATIC_ROUNDS
    step, state, (older, newer), pending = lax.while_loop(
        more,
        again,
        (
            jnp.int32(final),
            state,
            (received[final - 2], received[final - 1]),
            tuple(crossed[final - back] for back in range(CROSS_LAG, 1, -1)),
        ),
    )
    pending = pending + (cross_pair(newer),)
    state, _ = switch_round(
        plan,
        place,
        step[None],
        ranks,
        {2: older, 1: newer},
        {CROSS_LAG - index: pair for index, pair in enumerate(pending)},
        state,
        False,
        False,
    )
    return state[1].reshape(1, 1, 2, capacity, box_count, rank_width, width)


def solution(mesh):
    return jax.shard_map(
        per_device,
        mesh=mesh,
        in_specs=(
            P(None, "box", "tbit", None, None),
            P(None, "box", None, None),
            P(None, "box", None, None),
            P(None, "box", None, None),
            P(),
            P(),
            P(),
            P(None, "box", "tbit"),
            P(None, "box", "tbit"),
            P(),
            P(),
            P(),
        ),
        out_specs=P("tbit", "box", None, None, None, None, None),
        check_vma=False,
    )
```

```python
import functools
import math

import jax
import jax.numpy as jnp
from jax import lax
from jax.experimental import pallas as pl
from jax.experimental.pallas import tpu as pltpu
from jax.sharding import PartitionSpec as P

NPTS = 1048576
PHASE_BITS = 20
CHUNKS = 16
LANES = 4
LAG = 2
CROSS_LAG = 4
STATIC_ROUNDS = 22
PER_STEP = 4
VMEM_BYTES = 32 * 1024 * 1024
CODE_SHIFT = 16
SLOT_SHIFT = 16
SHORT = pl.CostEstimate(flops=1, bytes_accessed=1, transcendentals=0)
POINTS_SECOND = 2
POINTS_THIRD = 4
TARGETS_LOW = 5
TARGETS_HIGH = 6

SIN_TERMS = (
    1.0,
    -1.0 / 6.0,
    1.0 / 120.0,
    -1.0 / 5040.0,
    1.0 / 362880.0,
    -1.0 / 39916800.0,
    1.0 / 6227020800.0,
)


def swapped(value, axis, bit):
    mask = 2**bit
    pairs = [(source, source ^ mask) for source in range(lax.axis_size(axis))]
    return lax.ppermute(value, axis, pairs)


def slot_table(owner_row, box_count, capacity):
    parent_count = owner_row.shape[0]
    onehot = (owner_row[:, None] == jnp.arange(box_count, dtype=jnp.int32)[None, :]).astype(
        jnp.int32
    )
    earlier = jnp.cumsum(onehot, axis=0, dtype=jnp.int32) - onehot
    slot_of = jnp.sum(earlier * onehot, axis=1, dtype=jnp.int32)
    matches = (onehot.T[:, None, :] == 1) & (
        slot_of[None, None, :] == jnp.arange(capacity, dtype=jnp.int32)[None, :, None]
    )
    slot_parent = jnp.sum(
        jnp.where(matches, jnp.arange(parent_count, dtype=jnp.int32)[None, None, :], 0), axis=2
    )
    slot_used = jnp.any(matches, axis=2)
    return (slot_parent, slot_used)


def pick_slot(values, position):
    return lax.dynamic_index_in_dim(values, position, 2, keepdims=False)


def cos_kernel(targets, points):
    shift = 32 - PHASE_BITS
    phase = lax.shift_right_arithmetic(
        lax.shift_left(targets * points, jnp.int32(shift)), jnp.int32(shift)
    )
    offset = NPTS // 4 - jnp.abs(phase)
    y = offset.astype(jnp.float32) * jnp.float32(2.0 * math.pi / NPTS)
    square = y * y
    total = jnp.float32(SIN_TERMS[-1])
    for term in SIN_TERMS[-2::-1]:
        total = total * square + jnp.float32(term)
    return total * y


def split(value):
    high = value.astype(jnp.bfloat16)
    low = (value - high.astype(jnp.float32)).astype(jnp.bfloat16)
    return high, low


def stack_left(value):
    high, low = split(value)
    return jnp.concatenate(
        [jnp.concatenate([high, high], axis=1), jnp.concatenate([low, low], axis=1)], axis=0
    )


def product(left, right):
    rows = left.shape[0] // 2
    both = jnp.dot(
        left, jnp.concatenate(split(right), axis=0), preferred_element_type=jnp.float32
    )
    return both[:rows] + both[rows:]


def live(weights, rank):
    rows = lax.broadcasted_iota(jnp.int32, weights.shape, 0)
    return jnp.where(rows < rank, weights, 0.0)


def column(tile, row, begin, length):
    return jnp.transpose(tile)[begin : begin + length, row : row + 1]


def pair_weights(matrix, left, right, left_rank, right_rank):
    width = left.shape[1]
    both = product(matrix, jnp.concatenate([left, right], axis=1))
    return live(both[:, :width], left_rank), live(both[:, width:], right_rank)


def first_parent(tile, matrix, ranks, mine, arrived):
    rank_width = mine.shape[1]
    targets = column(tile, TARGETS_LOW, 0, rank_width)
    kernels = [cos_kernel(targets, tile[box : box + 1]) for box in range(2)]
    weights = pair_weights(matrix, *kernels, *ranks)
    return [
        product(stack_left(weights[box]), jnp.concatenate([mine[box], arrived[box]], axis=0))
        for box in range(2)
    ]


def later_parent(tile, matrices, ranks_second, ranks_third, mine, arrived):
    rank_width = mine.shape[1]
    targets = column(tile, TARGETS_LOW, rank_width, rank_width)
    kernels = [
        cos_kernel(targets, tile[POINTS_SECOND + box : POINTS_SECOND + box + 1]) for box in range(2)
    ]
    weights = pair_weights(matrices[0], *kernels, *ranks_second)
    seconds = [
        product(stack_left(weights[box]), jnp.concatenate([mine[box], arrived[box]], axis=0))
        for box in range(2)
    ]
    targets = column(tile, TARGETS_HIGH, 0, 2 * rank_width)
    kernel = cos_kernel(targets, tile[POINTS_THIRD : POINTS_THIRD + 1])
    weights = pair_weights(matrices[1], kernel[:rank_width], kernel[rank_width:], *ranks_third)
    stacked = jnp.concatenate(seconds, axis=0)
    return product(stack_left(jnp.concatenate(weights, axis=0)), stacked)


def ranks_of(ranks, level, parents, parent):
    start = 2 * (level * parents + parent)
    return ranks[start], ranks[start + 1]


def first_kernel(chunk, parents, ranks, points, matrices, mine, arrived, merged):
    matrix = stack_left(matrices[0])
    for member in range(mine.shape[0]):
        parent = (chunk * pl.num_programs(0) + pl.program_id(0)) * mine.shape[0] + member
        results = first_parent(
            points[member], matrix, ranks_of(ranks, 0, parents, parent), mine[member], arrived[member]
        )
        for box in range(2):
            merged[member, box] = results[box]


def later_kernel(chunk, parents, ranks, points, matrices, mine, arrived, *pool):
    merged = pool[-1]
    rank_width = mine.shape[2]
    stacks = [stack_left(matrices[1]), stack_left(matrices[2])]
    for member in range(mine.shape[0]):
        parent = (chunk * pl.num_programs(0) + pl.program_id(0)) * mine.shape[0] + member
        third = later_parent(
            points[member],
            stacks,
            ranks_of(ranks, 1, parents, parent),
            ranks_of(ranks, 2, parents, parent),
            mine[member],
            arrived[member],
        )
        for child in range(2):
            merged[member, child] = third[child * rank_width : (child + 1) * rank_width]


def chunk_spec(shape, chunk, steps, per_step):
    block = (per_step,) + tuple(shape[1:])
    rest = (0,) * (len(shape) - 1)
    return pl.BlockSpec(block, lambda step, *_: (chunk * steps + step,) + rest)


def whole_spec(shape):
    rest = (0,) * len(shape)
    return pl.BlockSpec(tuple(shape), lambda step, *_: rest)


def first_level(chunk, ranks, points, matrices, mine, arrived):
    per_step = PER_STEP
    steps = mine.shape[0] // per_step
    return pl.pallas_call(
        functools.partial(first_kernel, chunk, points.shape[0]),
        grid_spec=pltpu.PrefetchScalarGridSpec(
            num_scalar_prefetch=1,
            grid=(steps,),
            in_specs=[
                chunk_spec(points.shape, chunk, steps, per_step),
                whole_spec(matrices.shape),
                chunk_spec(mine.shape, 0, steps, per_step),
                chunk_spec(arrived.shape, 0, steps, per_step),
            ],
            out_specs=chunk_spec(arrived.shape, 0, steps, per_step),
        ),
        out_shape=jax.ShapeDtypeStruct(arrived.shape, jnp.float32),
        compiler_params=pltpu.CompilerParams(vmem_limit_bytes=VMEM_BYTES),
        name="first_level",
    )(ranks, points, matrices, mine, arrived)


def later_levels(chunk, ranks, points, matrices, mine, arrived, pool_shape, pool):
    per_step = PER_STEP
    steps = mine.shape[0] // per_step
    return pl.pallas_call(
        functools.partial(later_kernel, chunk, points.shape[0]),
        grid_spec=pltpu.PrefetchScalarGridSpec(
            num_scalar_prefetch=1,
            grid=(steps,),
            in_specs=[
                chunk_spec(points.shape, chunk, steps, per_step),
                whole_spec(matrices.shape),
                chunk_spec(mine.shape, 0, steps, per_step),
                chunk_spec(arrived.shape, 0, steps, per_step),
            ]
            + [pl.BlockSpec(memory_space=pl.ANY)] * len(pool),
            out_specs=chunk_spec(pool_shape, chunk, steps, per_step),
        ),
        out_shape=jax.ShapeDtypeStruct(pool_shape, jnp.float32),
        input_output_aliases={5: 0} if pool else {},
        compiler_params=pltpu.CompilerParams(vmem_limit_bytes=VMEM_BYTES),
        name="later_levels",
    )(ranks, points, matrices, mine, arrived, *pool)


def plan_kernel(
    chips, limit, chunks, owners, table, counts, slots, rounds, out, stage, own, ahead, used, zeros, sem
):
    parents = owners.shape[0]
    zeros[...] = jnp.zeros_like(zeros)
    fills = []
    for child in range(out.shape[0]):
        for slot in range(out.shape[1]):
            fills.append(pltpu.make_async_copy(zeros, out.at[child, slot], sem.at[len(fills)]))
            part = zeros.at[:, 0]
            fills.append(pltpu.make_async_copy(part, stage.at[child, slot], sem.at[len(fills)]))
    for fill in fills:
        fill.start()
    count = parents // chunks
    rows = chips + 1
    span = limit * LANES

    def clear(index, carry):
        counts[index] = 0
        return carry

    lax.fori_loop(0, 2 * rows * limit, clear, 0)
    for box in range(2 * chips):
        used[box] = 0

    def take_slot(parent, carry):
        owner = owners[parent]
        slot = used[owner]
        slots[parent] = (owner << SLOT_SHIFT) | slot
        used[owner] = slot + 1
        return carry

    lax.fori_loop(0, parents, take_slot, 0)
    width = chips * parents
    pairs = [(chip, goal) for chip in range(1, chips) for goal in range(chip + 1, chips)]
    last = []
    for direction in range(2):

        def true_chip(chip):
            return chip if direction == 0 else chips - 1 - chip

        total = 0
        for box in range(2 * chips):
            hops = true_chip(box // 2)
            total = total + used[box] * (hops * (hops + 1) // 2)

        def one_round(state):
            step, left, ready, own_head, head, tail, older = state
            ready, own_head, head, tail = list(ready), list(own_head), list(head), list(tail)
            for index in range(count):
                parent = jnp.minimum(step * count + index, parents - 1)
                goal = owners[parent] >> 1
                goal = goal if direction == 0 else chips - 1 - goal
                for chip in range(1, chips):
                    own[chip * parents + jnp.minimum(ready[chip], parents - 1)] = parent
                    here = (goal == chip) & (step < chunks)
                    ready[chip] = ready[chip] + here.astype(jnp.int32)
            seen = older[0]
            for chip in range(chips - 1):
                row = (direction * rows + 1 + chip) * limit + step
                sent = jnp.int32(0)
                for goal in range(chips - 1, chip, -1):
                    onward = pairs.index((chip + 1, goal)) if (chip + 1, goal) in pairs else None
                    for forwarded in (True, False):
                        if forwarded and (chip, goal) not in pairs:
                            continue
                        if forwarded:
                            queue = pairs.index((chip, goal))
                            start, stop = head[queue], seen[queue]
                        else:
                            queue = chip * chips + goal
                            start, stop = own_head[queue], ready[goal]
                        number = jnp.minimum(stop - start, LANES - sent)

                        def move(index, carry):
                            if forwarded:
                                code = ahead[queue * width + start + index]
                            else:
                                code = own[goal * parents + start + index]
                                code = code | (true_chip(chip) << CODE_SHIFT)
                            table[row * LANES + sent + index] = code
                            if onward is not None:
                                ahead[onward * width + tail[onward] + index] = code
                            return carry

                        lax.fori_loop(0, number, move, 0)
                        sent = sent + number
                        if onward is not None:
                            tail[onward] = tail[onward] + number
                        if forwarded:
                            head[queue] = start + number
                        else:
                            own_head[queue] = start + number
                counts[row] = sent
                left = left - sent
            return (
                step + 1,
                left,
                tuple(ready),
                tuple(own_head),
                tuple(head),
                tuple(tail),
                tuple(older[1:]) + (tuple(tail),),
            )

        zero = jnp.int32(0)
        none = (zero,) * len(pairs)
        state = lax.while_loop(
            lambda state: (state[1] > 0) & (state[0] < limit),
            one_round,
            (zero, jnp.int32(total), (zero,) * chips, (zero,) * (chips * chips), none, none, (none,) * LAG),
        )
        last.append(state[0])
    rounds[0] = jnp.maximum(last[0], last[1])
    for fill in fills:
        fill.wait()


def plan_switch(owner_row, out_shape):
    parents = owner_row.shape[0]
    chips = out_shape[2]
    anywhere = pl.BlockSpec(memory_space=pl.ANY)
    limit = round_limit(parents)
    smem = pl.BlockSpec(memory_space=pltpu.SMEM)
    return pl.pallas_call(
        functools.partial(plan_kernel, chips, limit, CHUNKS),
        in_specs=[smem],
        out_specs=[smem] * 4 + [anywhere] * 2,
        out_shape=[
            jax.ShapeDtypeStruct((2 * (chips + 1) * limit * LANES,), jnp.int32),
            jax.ShapeDtypeStruct((2 * (chips + 1) * limit,), jnp.int32),
            jax.ShapeDtypeStruct((parents,), jnp.int32),
            jax.ShapeDtypeStruct((1,), jnp.int32),
            jax.ShapeDtypeStruct(out_shape, jnp.float32),
            jax.ShapeDtypeStruct(out_shape[:3] + out_shape[4:], jnp.float32),
        ],
        scratch_shapes=[
            pltpu.SMEM((chips * parents,), jnp.int32),
            pltpu.SMEM((chips * chips * chips * parents,), jnp.int32),
            pltpu.SMEM((2 * chips,), jnp.int32),
            pltpu.VMEM(out_shape[2:], jnp.float32),
            pltpu.SemaphoreType.DMA((2 * out_shape[0] * out_shape[1],)),
        ],
        name="plan_switch",
    )(owner_row)


def round_limit(parents):
    return 4 * parents // LANES


def round_kernel(chips, limit, parents, receives, crossings, staging, high, low, sends, pooled, *refs):
    table, counts, slots, place, now, ranks = refs[:6]
    refs = refs[6:]
    sources = receives + crossings
    received, refs = refs[: 2 * len(sources)], refs[2 * len(sources) :]
    points, matrices = refs[:2] if high is not None or low is not None else (None, None)
    refs = refs[2:] if points is not None else refs
    mine_high, arrived_high = refs[:2] if high is not None else (None, None)
    refs = refs[2:] if high is not None else refs
    mine_low, arrived_low = refs[:2] if low is not None else (None, None)
    refs = refs[2:] if low is not None else refs
    refs = refs[2 + pooled :]
    pool, out, stage = refs[:3]
    outgoing = refs[3 : 3 + 2 * sends]
    merged = refs[3 + 2 * sends] if low is not None else None
    kept, sems = refs[-2:]
    fresh = 0 if high is None else mine_high.shape[0]
    last_sem = LANES * max(2 * len(sources), 2)
    z, core = place[0], place[1]
    odd = z & 1

    def row_of(direction, receiving, step):
        spot = jnp.where(direction == 0, z, chips - 1 - z)
        return (direction * (chips + 1) + (1 - receiving) + spot) * limit + step

    def home(sem, from_chip, parent, source, begin, crossed=False):
        spot = slots[parent]
        owner, slot = spot >> SLOT_SHIFT, spot & ((1 << SLOT_SHIFT) - 1)
        here = (owner >> 1) == z
        same = (owner & 1) == core

        @pl.when(here & same)
        def _():
            from_core = 1 - core if crossed else core
            copy = pltpu.make_async_copy(source, out.at[:, slot, from_chip, from_core], sem)
            copy.start() if begin else copy.wait()

        if staging and not crossed:

            @pl.when(here & jnp.logical_not(same))
            def _():
                copy = pltpu.make_async_copy(source, stage.at[:, slot, from_chip], sem)
                copy.start() if begin else copy.wait()

        return here

    def of_code(code):
        from_chip, parent = code >> CODE_SHIFT, code & ((1 << CODE_SHIFT) - 1)
        return from_chip, parent, from_chip * parents + parent

    def take_in(begin):
        for place_of, back in enumerate(sources):
            crossed = place_of >= len(receives)
            for port in range(2):
                step = now[0] - back
                row = row_of(1 - (odd ^ port), 1, jnp.maximum(step, 0))
                number = jnp.where(step >= 0, counts[row], 0)
                base = (2 * place_of + port) * LANES

                def one(lane, carry):
                    from_chip, parent, held = of_code(table[row * LANES + lane])
                    source = received[2 * place_of + port].at[lane]
                    sem = sems.at[base + lane]
                    here = home(sem, from_chip, parent, source, begin, crossed)
                    if not crossed:

                        @pl.when(jnp.logical_not(here))
                        def _():
                            copy = pltpu.make_async_copy(source, pool.at[held], sem)
                            copy.start() if begin else copy.wait()

                    return carry

                lax.fori_loop(0, number, one, 0)

    def send(begin):
        for port in range(2):
            row = row_of(odd ^ port, 0, now[0])

            def one(lane, carry):
                _, _, held = of_code(table[row * LANES + lane])
                copy = pltpu.make_async_copy(
                    pool.at[held], outgoing[port].at[lane], sems.at[port * LANES + lane]
                )
                copy.start() if begin else copy.wait()
                return carry

            lax.fori_loop(0, counts[row], one, 0)

    def keep(begin):
        def one(member, carry):
            parent = high * fresh + member
            home(sems.at[last_sem + member], z, parent, kept.at[member], begin)
            return carry

        lax.fori_loop(0, fresh, one, 0)

    take_in(True)
    if high is not None:
        rank_width = mine_high.shape[2]
        stacks = [stack_left(matrices[1]), stack_left(matrices[2])]
        for member in range(fresh):
            parent = high * fresh + member
            third = later_parent(
                points[parent],
                stacks,
                ranks_of(ranks, 1, parents, parent),
                ranks_of(ranks, 2, parents, parent),
                mine_high[member],
                arrived_high[member],
            )
            for child in range(2):
                kept[member, child] = third[child * rank_width : (child + 1) * rank_width]
        fill = pltpu.make_async_copy(
            kept, pool.at[pl.ds(z * parents + high * fresh, fresh)], sems.at[last_sem + fresh]
        )
        fill.start()
        keep(True)
    take_in(False)
    if high is not None:
        fill.wait()
    if sends:
        send(True)
    if low is not None:
        matrix = stack_left(matrices[0])
        for member in range(mine_low.shape[0]):
            parent = low * mine_low.shape[0] + member
            results = first_parent(
                points[parent],
                matrix,
                ranks_of(ranks, 0, parents, parent),
                mine_low[member],
                arrived_low[member],
            )
            for box in range(2):
                merged[member, box] = results[box]
    if high is not None:
        keep(False)
    if sends:
        send(False)


def switch_round(plan, place, now, ranks, received, crossed, state, staging, sends, levels=None, high=None, low=None):
    table, counts, slots = plan
    out = state[-2]
    parents = slots.shape[0]
    chips = out.shape[2]
    block = (out.shape[0],) + out.shape[4:]
    inputs = [array for pair in [*received.values(), *crossed.values()] for array in pair]
    waiting = len(inputs)
    if high is not None or low is not None:
        inputs += levels
    for work in (high, low):
        if work is not None:
            inputs += work[1:]
    fresh = 0 if high is None else high[1].shape[0]
    anywhere = pl.BlockSpec(memory_space=pl.ANY)
    inside = pl.BlockSpec(memory_space=pltpu.VMEM)
    shapes = [jax.ShapeDtypeStruct((chips * parents,) + block, jnp.float32)]
    shapes += [jax.ShapeDtypeStruct(array.shape, array.dtype) for array in state[-2:]]
    shapes += [jax.ShapeDtypeStruct((LANES,) + block, jnp.float32)] * (2 * int(sends))
    if low is not None:
        shapes += [jax.ShapeDtypeStruct(low[1].shape, jnp.float32)]
    pooled = len(state) - 2
    first = 6 + len(inputs)
    results = pl.pallas_call(
        functools.partial(
            round_kernel,
            chips,
            round_limit(parents),
            parents,
            tuple(received),
            tuple(crossed),
            staging,
            None if high is None else high[0],
            None if low is None else low[0],
            int(sends),
            pooled,
        ),
        grid_spec=pltpu.PrefetchScalarGridSpec(
            num_scalar_prefetch=6,
            grid=(),
            in_specs=[inside] * len(inputs) + [anywhere] * len(state),
            out_specs=[anywhere] * 3 + [inside] * (len(shapes) - 3),
            scratch_shapes=[
                pltpu.VMEM((max(fresh, 1),) + block, jnp.float32),
                pltpu.SemaphoreType.DMA((LANES * max(waiting, 2) + fresh + 1,)),
            ],
        ),
        out_shape=shapes,
        input_output_aliases={first + index: index + 1 - pooled for index in range(len(state))},
        cost_estimate=SHORT,
        compiler_params=pltpu.CompilerParams(vmem_limit_bytes=VMEM_BYTES),
        name="switch_round",
    )(table, counts, slots, place, now, ranks, *inputs, *state)
    return tuple(results[:3]), tuple(results[3:])


def join_kernel(place, arrived, out_before, out):
    for child in range(2):
        for chip in range(arrived.shape[2]):
            out[child, 0, chip, 0] = arrived[child, 0, chip]


def join_cores(place, arrived, out):
    children, capacity, chips, _, rank_width, width = out.shape
    return pl.pallas_call(
        join_kernel,
        grid_spec=pltpu.PrefetchScalarGridSpec(
            num_scalar_prefetch=1,
            grid=(capacity,),
            in_specs=[
                pl.BlockSpec(
                    (children, 1, chips, rank_width, width), lambda slot, place: (0, slot, 0, 0, 0)
                ),
                pl.BlockSpec(memory_space=pl.ANY),
            ],
            out_specs=pl.BlockSpec(
                (children, 1, chips, 1, rank_width, width),
                lambda slot, place: (0, slot, 0, 1 - place[1], 0, 0),
            ),
        ),
        out_shape=jax.ShapeDtypeStruct(out.shape, out.dtype),
        input_output_aliases={2: 0},
        cost_estimate=SHORT,
        compiler_params=pltpu.CompilerParams(vmem_limit_bytes=VMEM_BYTES),
        name="join_cores",
    )(place, arrived, out)


def along_line(value, chips, port):
    pairs = []
    for chip in range(port, chips - 1, 2):
        for core in range(2):
            low, high = 2 * chip + core, 2 * (chip + 1) + core
            pairs += [(low, high), (high, low)]
    return lax.ppermute(value, "box", pairs)


def per_device(
    coeffs,
    skeleton_first,
    skeleton_second,
    skeleton_third,
    checks_first,
    checks_second,
    checks_third,
    ranks_first,
    ranks_second,
    ranks_third,
    interpolants,
    owners,
):
    tbit_index = lax.axis_index("tbit")
    box_index = lax.axis_index("box")
    box_count = lax.axis_size("box")
    parent_count = coeffs.shape[0]
    rank_width = coeffs.shape[3]
    capacity = 2 * parent_count // box_count
    group_count = 2 * box_count
    local_boxes = 2 * box_index + jnp.arange(2, dtype=jnp.int32)[None, :, None]

    def targets_of(checks, per_parent, picked, width):
        boxes = per_parent * parent_count
        absolute = jnp.arange(boxes, dtype=jnp.int32)[:, None] * (NPTS // boxes) + checks
        return lax.dynamic_index_in_dim(absolute.reshape(parent_count, -1, width), picked, 1)

    def first_points(slot):
        box = 4 * local_boxes + 2 * (slot % 2) + slot // 2
        return box * (NPTS // (4 * group_count)) + pick_slot(skeleton_first, slot)

    def second_points(slot):
        box = 2 * local_boxes + slot % 2
        return box * (NPTS // (2 * group_count)) + pick_slot(skeleton_second, slot)

    partner_high = jnp.bitwise_xor(tbit_index, 2)
    partner_low = jnp.bitwise_xor(tbit_index, 1)
    points_third = local_boxes * (NPTS // group_count) + pick_slot(skeleton_third, tbit_index)
    low_targets = jnp.concatenate(
        [
            targets_of(checks_first, 2, tbit_index // 2, rank_width),
            targets_of(checks_second, 4, tbit_index, rank_width),
        ],
        axis=2,
    )
    high_targets = targets_of(checks_third, 8, tbit_index, 2 * rank_width)
    points = jnp.concatenate(
        [
            jnp.concatenate([first_points(tbit_index), first_points(partner_high)], axis=2),
            jnp.concatenate([second_points(tbit_index), second_points(partner_low)], axis=2),
            points_third.reshape(parent_count, 1, 2 * rank_width),
            low_targets,
            high_targets,
            jnp.zeros_like(high_targets),
        ],
        axis=1,
    )
    rank_three = lax.dynamic_index_in_dim(
        lax.dynamic_index_in_dim(ranks_third, tbit_index, 1, keepdims=False),
        box_index,
        2,
        keepdims=False,
    )
    ranks = jnp.concatenate(
        [ranks_first.reshape(-1), ranks_second.reshape(-1), rank_three.reshape(-1)]
    )

    mine = coeffs[:, :, 0]
    count = parent_count // CHUNKS
    chips = box_count // 2
    networked = chips <= 4
    place = jnp.stack([box_index // 2, box_index % 2]).astype(jnp.int32)
    owner_row = lax.dynamic_index_in_dim(owners, tbit_index, 0, keepdims=False)
    width = coeffs.shape[-1]
    pool_shape = (chips * parent_count, 2, rank_width, width)
    if not networked:
        pool_shape = (parent_count, 2, rank_width, width)

    parts, arrived = [mine[:count]], []

    def cut(begin, end, after):
        others, _ = lax.optimization_barrier((mine, after))
        for chunk in range(begin, end):
            parts.append(others[chunk * count : (chunk + 1) * count])

    early = 5 if networked else CHUNKS
    cut(1, early, parts[0])

    def start_low(chunk, after):
        outgoing = parts[chunk]
        if after is not None:
            outgoing, _ = lax.optimization_barrier((outgoing, after))
        arrived.append(swapped(outgoing, "tbit", 1))

    firsts, second_arrived = [], []

    def start_high(first):
        firsts.append(first)
        second_arrived.append(swapped(first, "tbit", 0))

    def low_level(chunk):
        return first_level(chunk, ranks, points, interpolants, parts[chunk], arrived[chunk])

    start_low(0, None)
    if networked:
        start_low(1, arrived[0])
        start_low(2, arrived[0])
    else:
        for chunk in range(1, CHUNKS):
            start_low(chunk, arrived[-1])
    start_high(low_level(0))
    if networked:
        owner_row, _ = lax.optimization_barrier((owner_row, firsts[0]))
        out_shape = (2, capacity, chips, 2, rank_width, width)
        *plan, rounds, out, stage = plan_switch(owner_row, out_shape)
        arrived[1], plan, rounds, out, stage = lax.optimization_barrier(
            (arrived[1], plan, rounds, out, stage)
        )
        most = jnp.broadcast_to(rounds, (8, 128))
    start_high(low_level(1))
    if networked:
        start_low(3, firsts[1])
    if not networked:
        for chunk in range(2, CHUNKS):
            start_high(low_level(chunk))
        pool = ()
        for chunk in range(CHUNKS):
            pool = (
                later_levels(
                    chunk, ranks, points, interpolants, firsts[chunk], second_arrived[chunk], pool_shape, pool
                ),
            )
        (pool,) = pool
        slot_parent, slot_used = slot_table(owner_row, box_count, capacity)
        outgoing = jnp.take(jnp.swapaxes(pool, 0, 1), slot_parent.T, axis=1)
        outgoing = jnp.where(slot_used.T[None, :, :, None, None], outgoing, 0.0)
        switched = lax.all_to_all(outgoing, "box", split_axis=2, concat_axis=2, tiled=True)
        return switched[None, None]

    state = (out, stage)
    received, crossed = {}, {}

    def exchange(packed):
        return (along_line(packed[0], chips, 0), along_line(packed[1], chips, 1))

    def cross(value):
        return lax.ppermute(value, "box", [(box, box ^ 1) for box in range(box_count)])

    def cross_pair(pair):
        return (cross(pair[0]), cross(pair[1]))

    staged = STATIC_ROUNDS - CROSS_LAG
    for step in range(STATIC_ROUNDS):
        high, low = None, None
        if step in (9, 12):
            second_arrived[step], most = lax.optimization_barrier((second_arrived[step], most))
        if step < CHUNKS:
            high = (step, firsts[step], second_arrived[step])
        if step + 2 < CHUNKS:
            low = (step + 2, parts[step + 2], arrived[step + 2])
        state, results = switch_round(
            plan,
            place,
            jnp.full((1,), step, jnp.int32),
            ranks,
            {LAG: received[step - LAG]} if step >= LAG else {},
            {CROSS_LAG: crossed[step - CROSS_LAG]} if step - CROSS_LAG >= staged else {},
            state,
            step < staged + LAG,
            True,
            [points, interpolants],
            high,
            low,
        )
        received[step] = exchange(results[:2])
        if low is not None:
            start_high(results[2])
        if step == 0:
            cut(early, CHUNKS, results[0])
        if step + 4 < CHUNKS:
            start_low(step + 4, results[0])
        if step >= staged:
            crossed[step] = cross_pair(received[step])
        if step == staged + LAG - 1:
            stage_crossed = cross(state[2])
        if step in (6, 9):
            most, _ = lax.optimization_barrier((most, results[0]))
            most = jnp.maximum(most, swapped(most, "tbit", 1 if step == 6 else 0))
        if step == STATIC_ROUNDS - 1:
            state = (state[0], join_cores(place, stage_crossed, state[1]), state[2])

    most = jnp.maximum(most[0, 0], STATIC_ROUNDS)

    def more(carry):
        return carry[0] < most

    def again(carry):
        step, state, (older, newer), pending = carry
        state, packed = switch_round(
            plan, place, step[None], ranks, {LAG: older}, {CROSS_LAG: pending[0]}, state, False, True
        )
        return (step + 1, state, (newer, exchange(packed)), pending[1:] + (cross_pair(newer),))

    final = STATIC_ROUNDS
    step, state, (older, newer), pending = lax.while_loop(
        more,
        again,
        (
            jnp.int32(final),
            state,
            (received[final - 2], received[final - 1]),
            tuple(crossed[final - back] for back in range(CROSS_LAG, 1, -1)),
        ),
    )
    pending = pending + (cross_pair(newer),)
    state, _ = switch_round(
        plan,
        place,
        step[None],
        ranks,
        {2: older, 1: newer},
        {CROSS_LAG - index: pair for index, pair in enumerate(pending)},
        state,
        False,
        False,
    )
    return state[1].reshape(1, 1, 2, capacity, box_count, rank_width, width)


def solution(mesh):
    return jax.shard_map(
        per_device,
        mesh=mesh,
        in_specs=(
            P(None, "box", "tbit", None, None),
            P(None, "box", None, None),
            P(None, "box", None, None),
            P(None, "box", None, None),
            P(),
            P(),
            P(),
            P(None, "box", "tbit"),
            P(None, "box", "tbit"),
            P(),
            P(),
            P(),
        ),
        out_specs=P("tbit", "box", None, None, None, None, None),
        check_vma=False,
    )
```

```python
import functools
import math

import jax
import jax.numpy as jnp
from jax import lax
from jax.experimental import pallas as pl
from jax.experimental.pallas import tpu as pltpu
from jax.sharding import PartitionSpec as P

NPTS = 1048576
PHASE_BITS = 20
CHUNKS = 16
LANES = 4
LAG = 2
CROSS_LAG = 7
STATIC_ROUNDS = 22
PER_STEP = 4
VMEM_BYTES = 32 * 1024 * 1024
CODE_SHIFT = 16
SLOT_SHIFT = 16
SHORT = pl.CostEstimate(flops=1, bytes_accessed=1, transcendentals=0)
POINTS_SECOND = 2
POINTS_THIRD = 4
TARGETS_LOW = 5
TARGETS_HIGH = 6

SIN_TERMS = (
    1.0,
    -1.0 / 6.0,
    1.0 / 120.0,
    -1.0 / 5040.0,
    1.0 / 362880.0,
    -1.0 / 39916800.0,
    1.0 / 6227020800.0,
)


def swapped(value, axis, bit):
    mask = 2**bit
    pairs = [(source, source ^ mask) for source in range(lax.axis_size(axis))]
    return lax.ppermute(value, axis, pairs)


def slot_table(owner_row, box_count, capacity):
    parent_count = owner_row.shape[0]
    onehot = (owner_row[:, None] == jnp.arange(box_count, dtype=jnp.int32)[None, :]).astype(
        jnp.int32
    )
    earlier = jnp.cumsum(onehot, axis=0, dtype=jnp.int32) - onehot
    slot_of = jnp.sum(earlier * onehot, axis=1, dtype=jnp.int32)
    matches = (onehot.T[:, None, :] == 1) & (
        slot_of[None, None, :] == jnp.arange(capacity, dtype=jnp.int32)[None, :, None]
    )
    slot_parent = jnp.sum(
        jnp.where(matches, jnp.arange(parent_count, dtype=jnp.int32)[None, None, :], 0), axis=2
    )
    slot_used = jnp.any(matches, axis=2)
    return (slot_parent, slot_used)


def pick_slot(values, position):
    return lax.dynamic_index_in_dim(values, position, 2, keepdims=False)


def cos_kernel(targets, points):
    shift = 32 - PHASE_BITS
    phase = lax.shift_right_arithmetic(
        lax.shift_left(targets * points, jnp.int32(shift)), jnp.int32(shift)
    )
    offset = NPTS // 4 - jnp.abs(phase)
    y = offset.astype(jnp.float32) * jnp.float32(2.0 * math.pi / NPTS)
    square = y * y
    total = jnp.float32(SIN_TERMS[-1])
    for term in SIN_TERMS[-2::-1]:
        total = total * square + jnp.float32(term)
    return total * y


def split(value):
    high = value.astype(jnp.bfloat16)
    low = (value - high.astype(jnp.float32)).astype(jnp.bfloat16)
    return high, low


def stack_left(value):
    high, low = split(value)
    return jnp.concatenate(
        [jnp.concatenate([high, high], axis=1), jnp.concatenate([low, low], axis=1)], axis=0
    )


def product(left, right):
    rows = left.shape[0] // 2
    both = jnp.dot(
        left, jnp.concatenate(split(right), axis=0), preferred_element_type=jnp.float32
    )
    return both[:rows] + both[rows:]


def live(weights, rank):
    rows = lax.broadcasted_iota(jnp.int32, weights.shape, 0)
    return jnp.where(rows < rank, weights, 0.0)


def column(tile, row, begin, length):
    return jnp.transpose(tile)[begin : begin + length, row : row + 1]


def pair_weights(matrix, left, right, left_rank, right_rank):
    width = left.shape[1]
    both = product(matrix, jnp.concatenate([left, right], axis=1))
    return live(both[:, :width], left_rank), live(both[:, width:], right_rank)


def first_parent(tile, matrix, ranks, mine, arrived):
    rank_width = mine.shape[1]
    targets = column(tile, TARGETS_LOW, 0, rank_width)
    kernels = [cos_kernel(targets, tile[box : box + 1]) for box in range(2)]
    weights = pair_weights(matrix, *kernels, *ranks)
    return [
        product(stack_left(weights[box]), jnp.concatenate([mine[box], arrived[box]], axis=0))
        for box in range(2)
    ]


def later_parent(tile, matrices, ranks_second, ranks_third, mine, arrived):
    rank_width = mine.shape[1]
    targets = column(tile, TARGETS_LOW, rank_width, rank_width)
    kernels = [
        cos_kernel(targets, tile[POINTS_SECOND + box : POINTS_SECOND + box + 1]) for box in range(2)
    ]
    weights = pair_weights(matrices[0], *kernels, *ranks_second)
    seconds = [
        product(stack_left(weights[box]), jnp.concatenate([mine[box], arrived[box]], axis=0))
        for box in range(2)
    ]
    targets = column(tile, TARGETS_HIGH, 0, 2 * rank_width)
    kernel = cos_kernel(targets, tile[POINTS_THIRD : POINTS_THIRD + 1])
    weights = pair_weights(matrices[1], kernel[:rank_width], kernel[rank_width:], *ranks_third)
    stacked = jnp.concatenate(seconds, axis=0)
    return product(stack_left(jnp.concatenate(weights, axis=0)), stacked)


def ranks_of(ranks, level, parents, parent):
    start = 2 * (level * parents + parent)
    return ranks[start], ranks[start + 1]


def first_kernel(chunk, parents, ranks, points, matrices, mine, arrived, merged):
    matrix = stack_left(matrices[0])
    for member in range(mine.shape[0]):
        parent = (chunk * pl.num_programs(0) + pl.program_id(0)) * mine.shape[0] + member
        results = first_parent(
            points[member], matrix, ranks_of(ranks, 0, parents, parent), mine[member], arrived[member]
        )
        for box in range(2):
            merged[member, box] = results[box]


def later_kernel(chunk, parents, ranks, points, matrices, mine, arrived, *pool):
    merged = pool[-1]
    rank_width = mine.shape[2]
    stacks = [stack_left(matrices[1]), stack_left(matrices[2])]
    for member in range(mine.shape[0]):
        parent = (chunk * pl.num_programs(0) + pl.program_id(0)) * mine.shape[0] + member
        third = later_parent(
            points[member],
            stacks,
            ranks_of(ranks, 1, parents, parent),
            ranks_of(ranks, 2, parents, parent),
            mine[member],
            arrived[member],
        )
        for child in range(2):
            merged[member, child] = third[child * rank_width : (child + 1) * rank_width]


def chunk_spec(shape, chunk, steps, per_step):
    block = (per_step,) + tuple(shape[1:])
    rest = (0,) * (len(shape) - 1)
    return pl.BlockSpec(block, lambda step, *_: (chunk * steps + step,) + rest)


def whole_spec(shape):
    rest = (0,) * len(shape)
    return pl.BlockSpec(tuple(shape), lambda step, *_: rest)


def first_level(chunk, ranks, points, matrices, mine, arrived):
    per_step = PER_STEP
    steps = mine.shape[0] // per_step
    return pl.pallas_call(
        functools.partial(first_kernel, chunk, points.shape[0]),
        grid_spec=pltpu.PrefetchScalarGridSpec(
            num_scalar_prefetch=1,
            grid=(steps,),
            in_specs=[
                chunk_spec(points.shape, chunk, steps, per_step),
                whole_spec(matrices.shape),
                chunk_spec(mine.shape, 0, steps, per_step),
                chunk_spec(arrived.shape, 0, steps, per_step),
            ],
            out_specs=chunk_spec(arrived.shape, 0, steps, per_step),
        ),
        out_shape=jax.ShapeDtypeStruct(arrived.shape, jnp.float32),
        compiler_params=pltpu.CompilerParams(vmem_limit_bytes=VMEM_BYTES),
        name="first_level",
    )(ranks, points, matrices, mine, arrived)


def later_levels(chunk, ranks, points, matrices, mine, arrived, pool_shape, pool):
    per_step = PER_STEP
    steps = mine.shape[0] // per_step
    return pl.pallas_call(
        functools.partial(later_kernel, chunk, points.shape[0]),
        grid_spec=pltpu.PrefetchScalarGridSpec(
            num_scalar_prefetch=1,
            grid=(steps,),
            in_specs=[
                chunk_spec(points.shape, chunk, steps, per_step),
                whole_spec(matrices.shape),
                chunk_spec(mine.shape, 0, steps, per_step),
                chunk_spec(arrived.shape, 0, steps, per_step),
            ]
            + [pl.BlockSpec(memory_space=pl.ANY)] * len(pool),
            out_specs=chunk_spec(pool_shape, chunk, steps, per_step),
        ),
        out_shape=jax.ShapeDtypeStruct(pool_shape, jnp.float32),
        input_output_aliases={5: 0} if pool else {},
        compiler_params=pltpu.CompilerParams(vmem_limit_bytes=VMEM_BYTES),
        name="later_levels",
    )(ranks, points, matrices, mine, arrived, *pool)


def plan_kernel(
    chips, limit, chunks, owners, table, counts, slots, rounds, out, stage, own, ahead, used, zeros, sem
):
    parents = owners.shape[0]
    zeros[...] = jnp.zeros_like(zeros)
    fills = []
    for child in range(out.shape[0]):
        for slot in range(out.shape[1]):
            fills.append(pltpu.make_async_copy(zeros, out.at[child, slot], sem.at[len(fills)]))
            part = zeros.at[:, 0]
            fills.append(pltpu.make_async_copy(part, stage.at[child, slot], sem.at[len(fills)]))
    for fill in fills:
        fill.start()
    count = parents // chunks
    rows = chips + 1
    span = limit * LANES

    def clear(index, carry):
        counts[index] = 0
        return carry

    lax.fori_loop(0, 2 * rows * limit, clear, 0)
    for box in range(2 * chips):
        used[box] = 0

    def take_slot(parent, carry):
        owner = owners[parent]
        slot = used[owner]
        slots[parent] = (owner << SLOT_SHIFT) | slot
        used[owner] = slot + 1
        return carry

    lax.fori_loop(0, parents, take_slot, 0)
    width = chips * parents
    pairs = [(chip, goal) for chip in range(1, chips) for goal in range(chip + 1, chips)]
    last = []
    for direction in range(2):

        def true_chip(chip):
            return chip if direction == 0 else chips - 1 - chip

        total = 0
        for box in range(2 * chips):
            hops = true_chip(box // 2)
            total = total + used[box] * (hops * (hops + 1) // 2)

        def one_round(state):
            step, left, ready, own_head, head, tail, older = state
            ready, own_head, head, tail = list(ready), list(own_head), list(head), list(tail)
            for index in range(count):
                parent = jnp.minimum(step * count + index, parents - 1)
                goal = owners[parent] >> 1
                goal = goal if direction == 0 else chips - 1 - goal
                for chip in range(1, chips):
                    own[chip * parents + jnp.minimum(ready[chip], parents - 1)] = parent
                    here = (goal == chip) & (step < chunks)
                    ready[chip] = ready[chip] + here.astype(jnp.int32)
            seen = older[0]
            for chip in range(chips - 1):
                row = (direction * rows + 1 + chip) * limit + step
                sent = jnp.int32(0)
                for goal in range(chips - 1, chip, -1):
                    onward = pairs.index((chip + 1, goal)) if (chip + 1, goal) in pairs else None
                    for forwarded in (True, False):
                        if forwarded and (chip, goal) not in pairs:
                            continue
                        if forwarded:
                            queue = pairs.index((chip, goal))
                            start, stop = head[queue], seen[queue]
                        else:
                            queue = chip * chips + goal
                            start, stop = own_head[queue], ready[goal]
                        number = jnp.minimum(stop - start, LANES - sent)

                        def move(index, carry):
                            if forwarded:
                                code = ahead[queue * width + start + index]
                            else:
                                code = own[goal * parents + start + index]
                                code = code | (true_chip(chip) << CODE_SHIFT)
                            table[row * LANES + sent + index] = code
                            if onward is not None:
                                ahead[onward * width + tail[onward] + index] = code
                            return carry

                        lax.fori_loop(0, number, move, 0)
                        sent = sent + number
                        if onward is not None:
                            tail[onward] = tail[onward] + number
                        if forwarded:
                            head[queue] = start + number
                        else:
                            own_head[queue] = start + number
                counts[row] = sent
                left = left - sent
            return (
                step + 1,
                left,
                tuple(ready),
                tuple(own_head),
                tuple(head),
                tuple(tail),
                tuple(older[1:]) + (tuple(tail),),
            )

        zero = jnp.int32(0)
        none = (zero,) * len(pairs)
        state = lax.while_loop(
            lambda state: (state[1] > 0) & (state[0] < limit),
            one_round,
            (zero, jnp.int32(total), (zero,) * chips, (zero,) * (chips * chips), none, none, (none,) * LAG),
        )
        last.append(state[0])
    rounds[0] = jnp.maximum(last[0], last[1])
    for fill in fills:
        fill.wait()


def plan_switch(owner_row, out_shape):
    parents = owner_row.shape[0]
    chips = out_shape[2]
    anywhere = pl.BlockSpec(memory_space=pl.ANY)
    limit = round_limit(parents)
    smem = pl.BlockSpec(memory_space=pltpu.SMEM)
    return pl.pallas_call(
        functools.partial(plan_kernel, chips, limit, CHUNKS),
        in_specs=[smem],
        out_specs=[smem] * 4 + [anywhere] * 2,
        out_shape=[
            jax.ShapeDtypeStruct((2 * (chips + 1) * limit * LANES,), jnp.int32),
            jax.ShapeDtypeStruct((2 * (chips + 1) * limit,), jnp.int32),
            jax.ShapeDtypeStruct((parents,), jnp.int32),
            jax.ShapeDtypeStruct((1,), jnp.int32),
            jax.ShapeDtypeStruct(out_shape, jnp.float32),
            jax.ShapeDtypeStruct(out_shape[:3] + out_shape[4:], jnp.float32),
        ],
        scratch_shapes=[
            pltpu.SMEM((chips * parents,), jnp.int32),
            pltpu.SMEM((chips * chips * chips * parents,), jnp.int32),
            pltpu.SMEM((2 * chips,), jnp.int32),
            pltpu.VMEM(out_shape[2:], jnp.float32),
            pltpu.SemaphoreType.DMA((2 * out_shape[0] * out_shape[1],)),
        ],
        name="plan_switch",
    )(owner_row)


def round_limit(parents):
    return 4 * parents // LANES


def round_kernel(chips, limit, parents, receives, crossings, staging, high, low, sends, pooled, *refs):
    table, counts, slots, place, now, ranks = refs[:6]
    refs = refs[6:]
    sources = receives + crossings
    received, refs = refs[: 2 * len(sources)], refs[2 * len(sources) :]
    points, matrices = refs[:2] if high is not None or low is not None else (None, None)
    refs = refs[2:] if points is not None else refs
    mine_high, arrived_high = refs[:2] if high is not None else (None, None)
    refs = refs[2:] if high is not None else refs
    mine_low, arrived_low = refs[:2] if low is not None else (None, None)
    refs = refs[2:] if low is not None else refs
    refs = refs[1 + staging + pooled :]
    pool, out = refs[:2]
    stage = refs[2] if staging else None
    refs = refs[2 + staging :]
    outgoing = refs[: 2 * sends]
    merged = refs[2 * sends] if low is not None else None
    kept, sems = refs[-2:]
    fresh = 0 if high is None else mine_high.shape[0]
    last_sem = LANES * max(2 * len(sources), 2)
    z, core = place[0], place[1]
    odd = z & 1

    def row_of(direction, receiving, step):
        spot = jnp.where(direction == 0, z, chips - 1 - z)
        return (direction * (chips + 1) + (1 - receiving) + spot) * limit + step

    def home(sem, from_chip, parent, source, begin, crossed=False):
        spot = slots[parent]
        owner, slot = spot >> SLOT_SHIFT, spot & ((1 << SLOT_SHIFT) - 1)
        here = (owner >> 1) == z
        same = (owner & 1) == core

        @pl.when(here & same)
        def _():
            from_core = 1 - core if crossed else core
            copy = pltpu.make_async_copy(source, out.at[:, slot, from_chip, from_core], sem)
            copy.start() if begin else copy.wait()

        if staging and not crossed:

            @pl.when(here & jnp.logical_not(same))
            def _():
                copy = pltpu.make_async_copy(source, stage.at[:, slot, from_chip], sem)
                copy.start() if begin else copy.wait()

        return here

    def of_code(code):
        from_chip, parent = code >> CODE_SHIFT, code & ((1 << CODE_SHIFT) - 1)
        return from_chip, parent, from_chip * parents + parent

    def take_in(begin):
        for place_of, back in enumerate(sources):
            crossed = place_of >= len(receives)
            for port in range(2):
                step = now[0] - back
                row = row_of(1 - (odd ^ port), 1, jnp.maximum(step, 0))
                number = jnp.where(step >= 0, counts[row], 0)
                base = (2 * place_of + port) * LANES

                def one(lane, carry):
                    from_chip, parent, held = of_code(table[row * LANES + lane])
                    source = received[2 * place_of + port].at[lane]
                    sem = sems.at[base + lane]
                    here = home(sem, from_chip, parent, source, begin, crossed)
                    if not crossed:

                        @pl.when(jnp.logical_not(here))
                        def _():
                            copy = pltpu.make_async_copy(source, pool.at[held], sem)
                            copy.start() if begin else copy.wait()

                    return carry

                lax.fori_loop(0, number, one, 0)

    def send(begin):
        for port in range(2):
            row = row_of(odd ^ port, 0, now[0])

            def one(lane, carry):
                _, _, held = of_code(table[row * LANES + lane])
                copy = pltpu.make_async_copy(
                    pool.at[held], outgoing[port].at[lane], sems.at[port * LANES + lane]
                )
                copy.start() if begin else copy.wait()
                return carry

            lax.fori_loop(0, counts[row], one, 0)

    def keep(begin):
        def one(member, carry):
            parent = high * fresh + member
            home(sems.at[last_sem + member], z, parent, kept.at[member], begin)
            return carry

        lax.fori_loop(0, fresh, one, 0)

    take_in(True)
    if high is not None:
        rank_width = mine_high.shape[2]
        stacks = [stack_left(matrices[1]), stack_left(matrices[2])]
        for member in range(fresh):
            parent = high * fresh + member
            third = later_parent(
                points[parent],
                stacks,
                ranks_of(ranks, 1, parents, parent),
                ranks_of(ranks, 2, parents, parent),
                mine_high[member],
                arrived_high[member],
            )
            for child in range(2):
                kept[member, child] = third[child * rank_width : (child + 1) * rank_width]
        fill = pltpu.make_async_copy(
            kept, pool.at[pl.ds(z * parents + high * fresh, fresh)], sems.at[last_sem + fresh]
        )
        fill.start()
        keep(True)
    take_in(False)
    if high is not None:
        fill.wait()
    if sends:
        send(True)
    if low is not None:
        matrix = stack_left(matrices[0])
        for member in range(mine_low.shape[0]):
            parent = low * mine_low.shape[0] + member
            results = first_parent(
                points[parent],
                matrix,
                ranks_of(ranks, 0, parents, parent),
                mine_low[member],
                arrived_low[member],
            )
            for box in range(2):
                merged[member, box] = results[box]
    if high is not None:
        keep(False)
    if sends:
        send(False)


def switch_round(plan, place, now, ranks, received, crossed, state, staging, sends, levels=None, high=None, low=None):
    table, counts, slots = plan
    pooled = len(state) - 1 - int(staging)
    out = state[pooled]
    parents = slots.shape[0]
    chips = out.shape[2]
    block = (out.shape[0],) + out.shape[4:]
    inputs = [array for pair in [*received.values(), *crossed.values()] for array in pair]
    waiting = len(inputs)
    if high is not None or low is not None:
        inputs += levels
    for work in (high, low):
        if work is not None:
            inputs += work[1:]
    fresh = 0 if high is None else high[1].shape[0]
    anywhere = pl.BlockSpec(memory_space=pl.ANY)
    inside = pl.BlockSpec(memory_space=pltpu.VMEM)
    shapes = [jax.ShapeDtypeStruct((chips * parents,) + block, jnp.float32)]
    shapes += [jax.ShapeDtypeStruct(array.shape, array.dtype) for array in state[pooled:]]
    held = len(shapes)
    shapes += [jax.ShapeDtypeStruct((LANES,) + block, jnp.float32)] * (2 * int(sends))
    if low is not None:
        shapes += [jax.ShapeDtypeStruct(low[1].shape, jnp.float32)]
    first = 6 + len(inputs)
    results = pl.pallas_call(
        functools.partial(
            round_kernel,
            chips,
            round_limit(parents),
            parents,
            tuple(received),
            tuple(crossed),
            int(staging),
            None if high is None else high[0],
            None if low is None else low[0],
            int(sends),
            pooled,
        ),
        grid_spec=pltpu.PrefetchScalarGridSpec(
            num_scalar_prefetch=6,
            grid=(),
            in_specs=[inside] * len(inputs) + [anywhere] * len(state),
            out_specs=[anywhere] * held + [inside] * (len(shapes) - held),
            scratch_shapes=[
                pltpu.VMEM((max(fresh, 1),) + block, jnp.float32),
                pltpu.SemaphoreType.DMA((LANES * max(waiting, 2) + fresh + 1,)),
            ],
        ),
        out_shape=shapes,
        input_output_aliases={first + index: index + 1 - pooled for index in range(len(state))},
        cost_estimate=SHORT,
        compiler_params=pltpu.CompilerParams(vmem_limit_bytes=VMEM_BYTES),
        name="switch_round",
    )(table, counts, slots, place, now, ranks, *inputs, *state)
    return tuple(results[:held]), tuple(results[held:])


def join_kernel(place, arrived, out_before, out):
    for child in range(2):
        for chip in range(arrived.shape[2]):
            out[child, 0, chip, 0] = arrived[child, 0, chip]


def join_cores(place, arrived, out):
    children, capacity, chips, _, rank_width, width = out.shape
    return pl.pallas_call(
        join_kernel,
        grid_spec=pltpu.PrefetchScalarGridSpec(
            num_scalar_prefetch=1,
            grid=(capacity,),
            in_specs=[
                pl.BlockSpec(
                    (children, 1, chips, rank_width, width), lambda slot, place: (0, slot, 0, 0, 0)
                ),
                pl.BlockSpec(memory_space=pl.ANY),
            ],
            out_specs=pl.BlockSpec(
                (children, 1, chips, 1, rank_width, width),
                lambda slot, place: (0, slot, 0, 1 - place[1], 0, 0),
            ),
        ),
        out_shape=jax.ShapeDtypeStruct(out.shape, out.dtype),
        input_output_aliases={2: 0},
        cost_estimate=SHORT,
        compiler_params=pltpu.CompilerParams(vmem_limit_bytes=VMEM_BYTES),
        name="join_cores",
    )(place, arrived, out)


def along_line(value, chips, port):
    pairs = []
    for chip in range(port, chips - 1, 2):
        for core in range(2):
            low, high = 2 * chip + core, 2 * (chip + 1) + core
            pairs += [(low, high), (high, low)]
    return lax.ppermute(value, "box", pairs)


def per_device(
    coeffs,
    skeleton_first,
    skeleton_second,
    skeleton_third,
    checks_first,
    checks_second,
    checks_third,
    ranks_first,
    ranks_second,
    ranks_third,
    interpolants,
    owners,
):
    tbit_index = lax.axis_index("tbit")
    box_index = lax.axis_index("box")
    box_count = lax.axis_size("box")
    parent_count = coeffs.shape[0]
    rank_width = coeffs.shape[3]
    capacity = 2 * parent_count // box_count
    group_count = 2 * box_count
    local_boxes = 2 * box_index + jnp.arange(2, dtype=jnp.int32)[None, :, None]

    def targets_of(checks, per_parent, picked, width):
        boxes = per_parent * parent_count
        absolute = jnp.arange(boxes, dtype=jnp.int32)[:, None] * (NPTS // boxes) + checks
        return lax.dynamic_index_in_dim(absolute.reshape(parent_count, -1, width), picked, 1)

    def first_points(slot):
        box = 4 * local_boxes + 2 * (slot % 2) + slot // 2
        return box * (NPTS // (4 * group_count)) + pick_slot(skeleton_first, slot)

    def second_points(slot):
        box = 2 * local_boxes + slot % 2
        return box * (NPTS // (2 * group_count)) + pick_slot(skeleton_second, slot)

    partner_high = jnp.bitwise_xor(tbit_index, 2)
    partner_low = jnp.bitwise_xor(tbit_index, 1)
    points_third = local_boxes * (NPTS // group_count) + pick_slot(skeleton_third, tbit_index)
    low_targets = jnp.concatenate(
        [
            targets_of(checks_first, 2, tbit_index // 2, rank_width),
            targets_of(checks_second, 4, tbit_index, rank_width),
        ],
        axis=2,
    )
    high_targets = targets_of(checks_third, 8, tbit_index, 2 * rank_width)
    points = jnp.concatenate(
        [
            jnp.concatenate([first_points(tbit_index), first_points(partner_high)], axis=2),
            jnp.concatenate([second_points(tbit_index), second_points(partner_low)], axis=2),
            points_third.reshape(parent_count, 1, 2 * rank_width),
            low_targets,
            high_targets,
            jnp.zeros_like(high_targets),
        ],
        axis=1,
    )
    rank_three = lax.dynamic_index_in_dim(
        lax.dynamic_index_in_dim(ranks_third, tbit_index, 1, keepdims=False),
        box_index,
        2,
        keepdims=False,
    )
    ranks = jnp.concatenate(
        [ranks_first.reshape(-1), ranks_second.reshape(-1), rank_three.reshape(-1)]
    )

    mine = coeffs[:, :, 0]
    count = parent_count // CHUNKS
    chips = box_count // 2
    networked = chips <= 4
    place = jnp.stack([box_index // 2, box_index % 2]).astype(jnp.int32)
    owner_row = lax.dynamic_index_in_dim(owners, tbit_index, 0, keepdims=False)
    width = coeffs.shape[-1]
    pool_shape = (chips * parent_count, 2, rank_width, width)
    if not networked:
        pool_shape = (parent_count, 2, rank_width, width)

    parts, arrived = [mine[:count]], []

    def cut(begin, end, after):
        others, _ = lax.optimization_barrier((mine, after))
        for chunk in range(begin, end):
            parts.append(others[chunk * count : (chunk + 1) * count])

    early = 5 if networked else CHUNKS
    cut(1, early, parts[0])

    def start_low(chunk, after):
        outgoing = parts[chunk]
        if after is not None:
            outgoing, _ = lax.optimization_barrier((outgoing, after))
        arrived.append(swapped(outgoing, "tbit", 1))

    firsts, second_arrived = [], []

    def start_high(first):
        firsts.append(first)
        second_arrived.append(swapped(first, "tbit", 0))

    def low_level(chunk):
        return first_level(chunk, ranks, points, interpolants, parts[chunk], arrived[chunk])

    start_low(0, None)
    if networked:
        start_low(1, arrived[0])
        start_low(2, arrived[0])
    else:
        for chunk in range(1, CHUNKS):
            start_low(chunk, arrived[-1])
    start_high(low_level(0))
    if networked:
        owner_row, _ = lax.optimization_barrier((owner_row, firsts[0]))
        out_shape = (2, capacity, chips, 2, rank_width, width)
        *plan, rounds, out, stage = plan_switch(owner_row, out_shape)
        arrived[1], plan, rounds, out, stage = lax.optimization_barrier(
            (arrived[1], plan, rounds, out, stage)
        )
        most = jnp.broadcast_to(rounds, (8, 128))
    start_high(low_level(1))
    if networked:
        start_low(3, firsts[1])
    if not networked:
        for chunk in range(2, CHUNKS):
            start_high(low_level(chunk))
        pool = ()
        for chunk in range(CHUNKS):
            pool = (
                later_levels(
                    chunk, ranks, points, interpolants, firsts[chunk], second_arrived[chunk], pool_shape, pool
                ),
            )
        (pool,) = pool
        slot_parent, slot_used = slot_table(owner_row, box_count, capacity)
        outgoing = jnp.take(jnp.swapaxes(pool, 0, 1), slot_parent.T, axis=1)
        outgoing = jnp.where(slot_used.T[None, :, :, None, None], outgoing, 0.0)
        switched = lax.all_to_all(outgoing, "box", split_axis=2, concat_axis=2, tiled=True)
        return switched[None, None]

    state = (out, stage)
    received, crossed = {}, {}

    def exchange(packed):
        return (along_line(packed[0], chips, 0), along_line(packed[1], chips, 1))

    def cross(value):
        return lax.ppermute(value, "box", [(box, box ^ 1) for box in range(box_count)])

    def cross_pair(pair):
        return (cross(pair[0]), cross(pair[1]))

    staged = STATIC_ROUNDS - CROSS_LAG
    for step in range(STATIC_ROUNDS):
        high, low = None, None
        if step < CHUNKS:
            high = (step, firsts[step], second_arrived[step])
        if step + 2 < CHUNKS:
            low = (step + 2, parts[step + 2], arrived[step + 2])
        state, results = switch_round(
            plan,
            place,
            jnp.full((1,), step, jnp.int32),
            ranks,
            {LAG: received[step - LAG]} if step >= LAG else {},
            {CROSS_LAG: crossed[step - CROSS_LAG]} if step - CROSS_LAG >= staged else {},
            state,
            step < staged + LAG,
            True,
            [points, interpolants],
            high,
            low,
        )
        received[step] = exchange(results[:2])
        if low is not None:
            start_high(results[2])
        if step == 0:
            cut(early, CHUNKS, results[0])
        if step + 4 < CHUNKS:
            start_low(step + 4, results[0])
        if step >= staged:
            crossed[step] = cross_pair(received[step])
        if step == staged + LAG - 1:
            stage_crossed = cross(state[2])
            state = state[:2]
        if step in (6, 11):
            most, _ = lax.optimization_barrier((most, results[0]))
            most = jnp.maximum(most, swapped(most, "tbit", 1 if step == 6 else 0))
        if step == STATIC_ROUNDS - 1:
            state = (state[0], join_cores(place, stage_crossed, state[1]))

    most = jnp.maximum(most[0, 0], STATIC_ROUNDS)

    def more(carry):
        return carry[0] < most

    def again(carry):
        step, state, (older, newer), pending = carry
        state, packed = switch_round(
            plan, place, step[None], ranks, {LAG: older}, {CROSS_LAG: pending[0]}, state, False, True
        )
        return (step + 1, state, (newer, exchange(packed)), pending[1:] + (cross_pair(newer),))

    final = STATIC_ROUNDS
    step, state, (older, newer), pending = lax.while_loop(
        more,
        again,
        (
            jnp.int32(final),
            state,
            (received[final - 2], received[final - 1]),
            tuple(crossed[final - back] for back in range(CROSS_LAG, 1, -1)),
        ),
    )
    pending = pending + (cross_pair(newer),)
    state, _ = switch_round(
        plan,
        place,
        step[None],
        ranks,
        {2: older, 1: newer},
        {CROSS_LAG - index: pair for index, pair in enumerate(pending)},
        state,
        False,
        False,
    )
    return state[1].reshape(1, 1, 2, capacity, box_count, rank_width, width)


def solution(mesh):
    return jax.shard_map(
        per_device,
        mesh=mesh,
        in_specs=(
            P(None, "box", "tbit", None, None),
            P(None, "box", None, None),
            P(None, "box", None, None),
            P(None, "box", None, None),
            P(),
            P(),
            P(),
            P(None, "box", "tbit"),
            P(None, "box", "tbit"),
            P(),
            P(),
            P(),
        ),
        out_specs=P("tbit", "box", None, None, None, None, None),
        check_vma=False,
    )
```

```python
import functools
import math

import jax
import jax.numpy as jnp
from jax import lax
from jax.experimental import pallas as pl
from jax.experimental.pallas import tpu as pltpu
from jax.sharding import PartitionSpec as P

NPTS = 1048576
PHASE_BITS = 20
CHUNKS = 16
MAIN_LANES = 4
LANES = 6
LAG = 2
CROSS_LAG = 2
STATIC_ROUNDS = 20
PER_STEP = 4
VMEM_BYTES = 32 * 1024 * 1024
CODE_SHIFT = 16
SLOT_SHIFT = 16
SHORT = pl.CostEstimate(flops=1, bytes_accessed=1, transcendentals=0)
POINTS_SECOND = 2
POINTS_THIRD = 4
TARGETS_LOW = 5
TARGETS_HIGH = 6

SIN_TERMS = (
    1.0,
    -1.0 / 6.0,
    1.0 / 120.0,
    -1.0 / 5040.0,
    1.0 / 362880.0,
    -1.0 / 39916800.0,
    1.0 / 6227020800.0,
)


def swapped(value, axis, bit):
    mask = 2**bit
    pairs = [(source, source ^ mask) for source in range(lax.axis_size(axis))]
    return lax.ppermute(value, axis, pairs)


def slot_table(owner_row, box_count, capacity):
    parent_count = owner_row.shape[0]
    onehot = (owner_row[:, None] == jnp.arange(box_count, dtype=jnp.int32)[None, :]).astype(
        jnp.int32
    )
    earlier = jnp.cumsum(onehot, axis=0, dtype=jnp.int32) - onehot
    slot_of = jnp.sum(earlier * onehot, axis=1, dtype=jnp.int32)
    matches = (onehot.T[:, None, :] == 1) & (
        slot_of[None, None, :] == jnp.arange(capacity, dtype=jnp.int32)[None, :, None]
    )
    slot_parent = jnp.sum(
        jnp.where(matches, jnp.arange(parent_count, dtype=jnp.int32)[None, None, :], 0), axis=2
    )
    slot_used = jnp.any(matches, axis=2)
    return (slot_parent, slot_used)


def pick_slot(values, position):
    return lax.dynamic_index_in_dim(values, position, 2, keepdims=False)


def cos_kernel(targets, points):
    shift = 32 - PHASE_BITS
    phase = lax.shift_right_arithmetic(
        lax.shift_left(targets * points, jnp.int32(shift)), jnp.int32(shift)
    )
    offset = NPTS // 4 - jnp.abs(phase)
    y = offset.astype(jnp.float32) * jnp.float32(2.0 * math.pi / NPTS)
    square = y * y
    total = jnp.float32(SIN_TERMS[-1])
    for term in SIN_TERMS[-2::-1]:
        total = total * square + jnp.float32(term)
    return total * y


def split(value):
    high = value.astype(jnp.bfloat16)
    low = (value - high.astype(jnp.float32)).astype(jnp.bfloat16)
    return high, low


def stack_left(value):
    high, low = split(value)
    return jnp.concatenate(
        [jnp.concatenate([high, high], axis=1), jnp.concatenate([low, low], axis=1)], axis=0
    )


def product(left, right):
    rows = left.shape[0] // 2
    both = jnp.dot(
        left, jnp.concatenate(split(right), axis=0), preferred_element_type=jnp.float32
    )
    return both[:rows] + both[rows:]


def live(weights, rank):
    rows = lax.broadcasted_iota(jnp.int32, weights.shape, 0)
    return jnp.where(rows < rank, weights, 0.0)


def column(tile, row, begin, length):
    return jnp.transpose(tile)[begin : begin + length, row : row + 1]


def pair_weights(matrix, left, right, left_rank, right_rank):
    width = left.shape[1]
    both = product(matrix, jnp.concatenate([left, right], axis=1))
    return live(both[:, :width], left_rank), live(both[:, width:], right_rank)


def first_parent(tile, matrix, ranks, mine, arrived):
    rank_width = mine.shape[1]
    targets = column(tile, TARGETS_LOW, 0, rank_width)
    kernels = [cos_kernel(targets, tile[box : box + 1]) for box in range(2)]
    weights = pair_weights(matrix, *kernels, *ranks)
    return [
        product(stack_left(weights[box]), jnp.concatenate([mine[box], arrived[box]], axis=0))
        for box in range(2)
    ]


def later_parent(tile, matrices, ranks_second, ranks_third, mine, arrived):
    rank_width = mine.shape[1]
    targets = column(tile, TARGETS_LOW, rank_width, rank_width)
    kernels = [
        cos_kernel(targets, tile[POINTS_SECOND + box : POINTS_SECOND + box + 1]) for box in range(2)
    ]
    weights = pair_weights(matrices[0], *kernels, *ranks_second)
    seconds = [
        product(stack_left(weights[box]), jnp.concatenate([mine[box], arrived[box]], axis=0))
        for box in range(2)
    ]
    targets = column(tile, TARGETS_HIGH, 0, 2 * rank_width)
    kernel = cos_kernel(targets, tile[POINTS_THIRD : POINTS_THIRD + 1])
    weights = pair_weights(matrices[1], kernel[:rank_width], kernel[rank_width:], *ranks_third)
    stacked = jnp.concatenate(seconds, axis=0)
    return product(stack_left(jnp.concatenate(weights, axis=0)), stacked)


def ranks_of(ranks, level, parents, parent):
    start = 2 * (level * parents + parent)
    return ranks[start], ranks[start + 1]


def first_kernel(chunk, parents, ranks, points, matrices, mine, arrived, merged):
    matrix = stack_left(matrices[0])
    for member in range(mine.shape[0]):
        parent = (chunk * pl.num_programs(0) + pl.program_id(0)) * mine.shape[0] + member
        results = first_parent(
            points[member], matrix, ranks_of(ranks, 0, parents, parent), mine[member], arrived[member]
        )
        for box in range(2):
            merged[member, box] = results[box]


def later_kernel(chunk, parents, ranks, points, matrices, mine, arrived, *pool):
    merged = pool[-1]
    rank_width = mine.shape[2]
    stacks = [stack_left(matrices[1]), stack_left(matrices[2])]
    for member in range(mine.shape[0]):
        parent = (chunk * pl.num_programs(0) + pl.program_id(0)) * mine.shape[0] + member
        third = later_parent(
            points[member],
            stacks,
            ranks_of(ranks, 1, parents, parent),
            ranks_of(ranks, 2, parents, parent),
            mine[member],
            arrived[member],
        )
        for child in range(2):
            merged[member, child] = third[child * rank_width : (child + 1) * rank_width]


def chunk_spec(shape, chunk, steps, per_step):
    block = (per_step,) + tuple(shape[1:])
    rest = (0,) * (len(shape) - 1)
    return pl.BlockSpec(block, lambda step, *_: (chunk * steps + step,) + rest)


def whole_spec(shape):
    rest = (0,) * len(shape)
    return pl.BlockSpec(tuple(shape), lambda step, *_: rest)


def first_level(chunk, ranks, points, matrices, mine, arrived):
    per_step = PER_STEP
    steps = mine.shape[0] // per_step
    return pl.pallas_call(
        functools.partial(first_kernel, chunk, points.shape[0]),
        grid_spec=pltpu.PrefetchScalarGridSpec(
            num_scalar_prefetch=1,
            grid=(steps,),
            in_specs=[
                chunk_spec(points.shape, chunk, steps, per_step),
                whole_spec(matrices.shape),
                chunk_spec(mine.shape, 0, steps, per_step),
                chunk_spec(arrived.shape, 0, steps, per_step),
            ],
            out_specs=chunk_spec(arrived.shape, 0, steps, per_step),
        ),
        out_shape=jax.ShapeDtypeStruct(arrived.shape, jnp.float32),
        compiler_params=pltpu.CompilerParams(vmem_limit_bytes=VMEM_BYTES),
        name="first_level",
    )(ranks, points, matrices, mine, arrived)


def later_levels(chunk, ranks, points, matrices, mine, arrived, pool_shape, pool):
    per_step = PER_STEP
    steps = mine.shape[0] // per_step
    return pl.pallas_call(
        functools.partial(later_kernel, chunk, points.shape[0]),
        grid_spec=pltpu.PrefetchScalarGridSpec(
            num_scalar_prefetch=1,
            grid=(steps,),
            in_specs=[
                chunk_spec(points.shape, chunk, steps, per_step),
                whole_spec(matrices.shape),
                chunk_spec(mine.shape, 0, steps, per_step),
                chunk_spec(arrived.shape, 0, steps, per_step),
            ]
            + [pl.BlockSpec(memory_space=pl.ANY)] * len(pool),
            out_specs=chunk_spec(pool_shape, chunk, steps, per_step),
        ),
        out_shape=jax.ShapeDtypeStruct(pool_shape, jnp.float32),
        input_output_aliases={5: 0} if pool else {},
        compiler_params=pltpu.CompilerParams(vmem_limit_bytes=VMEM_BYTES),
        name="later_levels",
    )(ranks, points, matrices, mine, arrived, *pool)


def plan_kernel(
    chips, limit, chunks, owners, table, counts, slots, rounds, out, stage, own, ahead, used, zeros, sem
):
    parents = owners.shape[0]
    zeros[...] = jnp.zeros_like(zeros)
    fills = []
    for child in range(out.shape[0]):
        for slot in range(out.shape[1]):
            fills.append(pltpu.make_async_copy(zeros, out.at[child, slot], sem.at[len(fills)]))
            part = zeros.at[:, 0]
            fills.append(pltpu.make_async_copy(part, stage.at[child, slot], sem.at[len(fills)]))
    for fill in fills:
        fill.start()
    count = parents // chunks
    rows = chips + 1
    span = limit * LANES

    def clear(index, carry):
        counts[index] = 0
        return carry

    lax.fori_loop(0, 2 * rows * limit, clear, 0)
    for box in range(2 * chips):
        used[box] = 0

    def take_slot(parent, carry):
        owner = owners[parent]
        slot = used[owner]
        slots[parent] = (owner << SLOT_SHIFT) | slot
        used[owner] = slot + 1
        return carry

    lax.fori_loop(0, parents, take_slot, 0)
    width = chips * parents
    pairs = [(chip, goal) for chip in range(1, chips) for goal in range(chip + 1, chips)]
    last = []
    for direction in range(2):

        def true_chip(chip):
            return chip if direction == 0 else chips - 1 - chip

        total = 0
        for box in range(2 * chips):
            hops = true_chip(box // 2)
            total = total + used[box] * (hops * (hops + 1) // 2)

        def one_round(state):
            step, left, ready, own_head, head, tail, older = state
            ready, own_head, head, tail = list(ready), list(own_head), list(head), list(tail)
            for index in range(count):
                parent = jnp.minimum(step * count + index, parents - 1)
                goal = owners[parent] >> 1
                goal = goal if direction == 0 else chips - 1 - goal
                for chip in range(1, chips):
                    own[chip * parents + jnp.minimum(ready[chip], parents - 1)] = parent
                    here = (goal == chip) & (step < chunks)
                    ready[chip] = ready[chip] + here.astype(jnp.int32)
            seen = older[0]
            room = jnp.where(step < chunks, MAIN_LANES, LANES)
            for chip in range(chips - 1):
                row = (direction * rows + 1 + chip) * limit + step
                sent = jnp.int32(0)
                for goal in range(chips - 1, chip, -1):
                    onward = pairs.index((chip + 1, goal)) if (chip + 1, goal) in pairs else None
                    for forwarded in (True, False):
                        if forwarded and (chip, goal) not in pairs:
                            continue
                        if forwarded:
                            queue = pairs.index((chip, goal))
                            start, stop = head[queue], seen[queue]
                        else:
                            queue = chip * chips + goal
                            start, stop = own_head[queue], ready[goal]
                        number = jnp.minimum(stop - start, room - sent)

                        def move(index, carry):
                            if forwarded:
                                code = ahead[queue * width + start + index]
                            else:
                                code = own[goal * parents + start + index]
                                code = code | (true_chip(chip) << CODE_SHIFT)
                            table[row * LANES + sent + index] = code
                            if onward is not None:
                                ahead[onward * width + tail[onward] + index] = code
                            return carry

                        lax.fori_loop(0, number, move, 0)
                        sent = sent + number
                        if onward is not None:
                            tail[onward] = tail[onward] + number
                        if forwarded:
                            head[queue] = start + number
                        else:
                            own_head[queue] = start + number
                counts[row] = sent
                left = left - sent
            return (
                step + 1,
                left,
                tuple(ready),
                tuple(own_head),
                tuple(head),
                tuple(tail),
                tuple(older[1:]) + (tuple(tail),),
            )

        zero = jnp.int32(0)
        none = (zero,) * len(pairs)
        state = lax.while_loop(
            lambda state: (state[1] > 0) & (state[0] < limit),
            one_round,
            (zero, jnp.int32(total), (zero,) * chips, (zero,) * (chips * chips), none, none, (none,) * LAG),
        )
        last.append(state[0])
    rounds[0] = jnp.maximum(last[0], last[1])
    for fill in fills:
        fill.wait()


def plan_switch(owner_row, out_shape):
    parents = owner_row.shape[0]
    chips = out_shape[2]
    anywhere = pl.BlockSpec(memory_space=pl.ANY)
    limit = round_limit(parents)
    smem = pl.BlockSpec(memory_space=pltpu.SMEM)
    return pl.pallas_call(
        functools.partial(plan_kernel, chips, limit, CHUNKS),
        in_specs=[smem],
        out_specs=[smem] * 4 + [anywhere] * 2,
        out_shape=[
            jax.ShapeDtypeStruct((2 * (chips + 1) * limit * LANES,), jnp.int32),
            jax.ShapeDtypeStruct((2 * (chips + 1) * limit,), jnp.int32),
            jax.ShapeDtypeStruct((parents,), jnp.int32),
            jax.ShapeDtypeStruct((1,), jnp.int32),
            jax.ShapeDtypeStruct(out_shape, jnp.float32),
            jax.ShapeDtypeStruct(out_shape[:3] + out_shape[4:], jnp.float32),
        ],
        scratch_shapes=[
            pltpu.SMEM((chips * parents,), jnp.int32),
            pltpu.SMEM((chips * chips * chips * parents,), jnp.int32),
            pltpu.SMEM((2 * chips,), jnp.int32),
            pltpu.VMEM(out_shape[2:], jnp.float32),
            pltpu.SemaphoreType.DMA((2 * out_shape[0] * out_shape[1],)),
        ],
        name="plan_switch",
    )(owner_row)


def round_limit(parents):
    return 4 * parents // MAIN_LANES


def round_kernel(chips, limit, parents, receives, crossings, staging, high, low, sends, pooled, *refs):
    table, counts, slots, place, now, ranks = refs[:6]
    refs = refs[6:]
    sources = receives + crossings
    received, refs = refs[: 2 * len(sources)], refs[2 * len(sources) :]
    points, matrices = refs[:2] if high is not None or low is not None else (None, None)
    refs = refs[2:] if points is not None else refs
    mine_high, arrived_high = refs[:2] if high is not None else (None, None)
    refs = refs[2:] if high is not None else refs
    mine_low, arrived_low = refs[:2] if low is not None else (None, None)
    refs = refs[2:] if low is not None else refs
    refs = refs[1 + staging + pooled :]
    pool, out = refs[:2]
    stage = refs[2] if staging else None
    refs = refs[2 + staging :]
    outgoing = refs[: 2 * sends]
    merged = refs[2 * sends] if low is not None else None
    kept, sems = refs[-2:]
    fresh = 0 if high is None else mine_high.shape[0]
    last_sem = LANES * max(2 * len(sources), 2)
    z, core = place[0], place[1]
    odd = z & 1

    def row_of(direction, receiving, step):
        spot = jnp.where(direction == 0, z, chips - 1 - z)
        return (direction * (chips + 1) + (1 - receiving) + spot) * limit + step

    def home(sem, from_chip, parent, source, begin, crossed=False):
        spot = slots[parent]
        owner, slot = spot >> SLOT_SHIFT, spot & ((1 << SLOT_SHIFT) - 1)
        here = (owner >> 1) == z
        same = (owner & 1) == core

        @pl.when(here & same)
        def _():
            from_core = 1 - core if crossed else core
            copy = pltpu.make_async_copy(source, out.at[:, slot, from_chip, from_core], sem)
            copy.start() if begin else copy.wait()

        if staging and not crossed:

            @pl.when(here & jnp.logical_not(same))
            def _():
                copy = pltpu.make_async_copy(source, stage.at[:, slot, from_chip], sem)
                copy.start() if begin else copy.wait()

        return here

    def of_code(code):
        from_chip, parent = code >> CODE_SHIFT, code & ((1 << CODE_SHIFT) - 1)
        return from_chip, parent, from_chip * parents + parent

    def take_in(begin):
        for place_of, back in enumerate(sources):
            crossed = place_of >= len(receives)
            for port in range(2):
                step = now[0] - back
                row = row_of(1 - (odd ^ port), 1, jnp.maximum(step, 0))
                number = jnp.where(step >= 0, counts[row], 0)
                base = (2 * place_of + port) * LANES

                def one(lane, carry):
                    from_chip, parent, held = of_code(table[row * LANES + lane])
                    source = received[2 * place_of + port].at[lane]
                    sem = sems.at[base + lane]
                    here = home(sem, from_chip, parent, source, begin, crossed)
                    if not crossed:

                        @pl.when(jnp.logical_not(here))
                        def _():
                            copy = pltpu.make_async_copy(source, pool.at[held], sem)
                            copy.start() if begin else copy.wait()

                    return carry

                lax.fori_loop(0, number, one, 0)

    def send(begin):
        for port in range(2):
            row = row_of(odd ^ port, 0, now[0])

            def one(lane, carry):
                _, _, held = of_code(table[row * LANES + lane])
                copy = pltpu.make_async_copy(
                    pool.at[held], outgoing[port].at[lane], sems.at[port * LANES + lane]
                )
                copy.start() if begin else copy.wait()
                return carry

            lax.fori_loop(0, counts[row], one, 0)

    def keep(begin):
        def one(member, carry):
            parent = high * fresh + member
            home(sems.at[last_sem + member], z, parent, kept.at[member], begin)
            return carry

        lax.fori_loop(0, fresh, one, 0)

    take_in(True)
    if high is not None:
        rank_width = mine_high.shape[2]
        stacks = [stack_left(matrices[1]), stack_left(matrices[2])]
        for member in range(fresh):
            parent = high * fresh + member
            third = later_parent(
                points[parent],
                stacks,
                ranks_of(ranks, 1, parents, parent),
                ranks_of(ranks, 2, parents, parent),
                mine_high[member],
                arrived_high[member],
            )
            for child in range(2):
                kept[member, child] = third[child * rank_width : (child + 1) * rank_width]
        fill = pltpu.make_async_copy(
            kept, pool.at[pl.ds(z * parents + high * fresh, fresh)], sems.at[last_sem + fresh]
        )
        fill.start()
        keep(True)
    take_in(False)
    if high is not None:
        fill.wait()
    if sends:
        send(True)
    if low is not None:
        matrix = stack_left(matrices[0])
        for member in range(mine_low.shape[0]):
            parent = low * mine_low.shape[0] + member
            results = first_parent(
                points[parent],
                matrix,
                ranks_of(ranks, 0, parents, parent),
                mine_low[member],
                arrived_low[member],
            )
            for box in range(2):
                merged[member, box] = results[box]
    if high is not None:
        keep(False)
    if sends:
        send(False)


def switch_round(plan, place, now, ranks, received, crossed, state, staging, sends, levels=None, high=None, low=None):
    table, counts, slots = plan
    pooled = len(state) - 1 - int(staging)
    out = state[pooled]
    parents = slots.shape[0]
    chips = out.shape[2]
    block = (out.shape[0],) + out.shape[4:]
    inputs = [array for pair in [*received.values(), *crossed.values()] for array in pair]
    waiting = len(inputs)
    if high is not None or low is not None:
        inputs += levels
    for work in (high, low):
        if work is not None:
            inputs += work[1:]
    fresh = 0 if high is None else high[1].shape[0]
    anywhere = pl.BlockSpec(memory_space=pl.ANY)
    inside = pl.BlockSpec(memory_space=pltpu.VMEM)
    shapes = [jax.ShapeDtypeStruct((chips * parents,) + block, jnp.float32)]
    shapes += [jax.ShapeDtypeStruct(array.shape, array.dtype) for array in state[pooled:]]
    held = len(shapes)
    lanes = MAIN_LANES if high is not None else LANES
    shapes += [jax.ShapeDtypeStruct((lanes,) + block, jnp.float32)] * (2 * int(sends))
    if low is not None:
        shapes += [jax.ShapeDtypeStruct(low[1].shape, jnp.float32)]
    first = 6 + len(inputs)
    results = pl.pallas_call(
        functools.partial(
            round_kernel,
            chips,
            round_limit(parents),
            parents,
            tuple(received),
            tuple(crossed),
            int(staging),
            None if high is None else high[0],
            None if low is None else low[0],
            int(sends),
            pooled,
        ),
        grid_spec=pltpu.PrefetchScalarGridSpec(
            num_scalar_prefetch=6,
            grid=(),
            in_specs=[inside] * len(inputs) + [anywhere] * len(state),
            out_specs=[anywhere] * held + [inside] * (len(shapes) - held),
            scratch_shapes=[
                pltpu.VMEM((max(fresh, 1),) + block, jnp.float32),
                pltpu.SemaphoreType.DMA((LANES * max(waiting, 2) + fresh + 1,)),
            ],
        ),
        out_shape=shapes,
        input_output_aliases={first + index: index + 1 - pooled for index in range(len(state))},
        cost_estimate=SHORT,
        compiler_params=pltpu.CompilerParams(vmem_limit_bytes=VMEM_BYTES),
        name="switch_round",
    )(table, counts, slots, place, now, ranks, *inputs, *state)
    return tuple(results[:held]), tuple(results[held:])


def join_kernel(place, arrived, out_before, out):
    for child in range(2):
        for chip in range(arrived.shape[2]):
            out[child, 0, chip, 0] = arrived[child, 0, chip]


def join_cores(place, arrived, out):
    children, capacity, chips, _, rank_width, width = out.shape
    return pl.pallas_call(
        join_kernel,
        grid_spec=pltpu.PrefetchScalarGridSpec(
            num_scalar_prefetch=1,
            grid=(capacity,),
            in_specs=[
                pl.BlockSpec(
                    (children, 1, chips, rank_width, width), lambda slot, place: (0, slot, 0, 0, 0)
                ),
                pl.BlockSpec(memory_space=pl.ANY),
            ],
            out_specs=pl.BlockSpec(
                (children, 1, chips, 1, rank_width, width),
                lambda slot, place: (0, slot, 0, 1 - place[1], 0, 0),
            ),
        ),
        out_shape=jax.ShapeDtypeStruct(out.shape, out.dtype),
        input_output_aliases={2: 0},
        cost_estimate=SHORT,
        compiler_params=pltpu.CompilerParams(vmem_limit_bytes=VMEM_BYTES),
        name="join_cores",
    )(place, arrived, out)


def along_line(value, chips, port):
    pairs = []
    for chip in range(port, chips - 1, 2):
        for core in range(2):
            low, high = 2 * chip + core, 2 * (chip + 1) + core
            pairs += [(low, high), (high, low)]
    return lax.ppermute(value, "box", pairs)


def per_device(
    coeffs,
    skeleton_first,
    skeleton_second,
    skeleton_third,
    checks_first,
    checks_second,
    checks_third,
    ranks_first,
    ranks_second,
    ranks_third,
    interpolants,
    owners,
):
    tbit_index = lax.axis_index("tbit")
    box_index = lax.axis_index("box")
    box_count = lax.axis_size("box")
    parent_count = coeffs.shape[0]
    rank_width = coeffs.shape[3]
    capacity = 2 * parent_count // box_count
    group_count = 2 * box_count
    local_boxes = 2 * box_index + jnp.arange(2, dtype=jnp.int32)[None, :, None]

    def targets_of(checks, per_parent, picked, width):
        boxes = per_parent * parent_count
        absolute = jnp.arange(boxes, dtype=jnp.int32)[:, None] * (NPTS // boxes) + checks
        return lax.dynamic_index_in_dim(absolute.reshape(parent_count, -1, width), picked, 1)

    def first_points(slot):
        box = 4 * local_boxes + 2 * (slot % 2) + slot // 2
        return box * (NPTS // (4 * group_count)) + pick_slot(skeleton_first, slot)

    def second_points(slot):
        box = 2 * local_boxes + slot % 2
        return box * (NPTS // (2 * group_count)) + pick_slot(skeleton_second, slot)

    partner_high = jnp.bitwise_xor(tbit_index, 2)
    partner_low = jnp.bitwise_xor(tbit_index, 1)
    points_third = local_boxes * (NPTS // group_count) + pick_slot(skeleton_third, tbit_index)
    low_targets = jnp.concatenate(
        [
            targets_of(checks_first, 2, tbit_index // 2, rank_width),
            targets_of(checks_second, 4, tbit_index, rank_width),
        ],
        axis=2,
    )
    high_targets = targets_of(checks_third, 8, tbit_index, 2 * rank_width)
    points = jnp.concatenate(
        [
            jnp.concatenate([first_points(tbit_index), first_points(partner_high)], axis=2),
            jnp.concatenate([second_points(tbit_index), second_points(partner_low)], axis=2),
            points_third.reshape(parent_count, 1, 2 * rank_width),
            low_targets,
            high_targets,
            jnp.zeros_like(high_targets),
        ],
        axis=1,
    )
    rank_three = lax.dynamic_index_in_dim(
        lax.dynamic_index_in_dim(ranks_third, tbit_index, 1, keepdims=False),
        box_index,
        2,
        keepdims=False,
    )
    ranks = jnp.concatenate(
        [ranks_first.reshape(-1), ranks_second.reshape(-1), rank_three.reshape(-1)]
    )

    mine = coeffs[:, :, 0]
    count = parent_count // CHUNKS
    chips = box_count // 2
    networked = chips <= 4
    place = jnp.stack([box_index // 2, box_index % 2]).astype(jnp.int32)
    owner_row = lax.dynamic_index_in_dim(owners, tbit_index, 0, keepdims=False)
    width = coeffs.shape[-1]
    pool_shape = (chips * parent_count, 2, rank_width, width)
    if not networked:
        pool_shape = (parent_count, 2, rank_width, width)

    parts, arrived = [mine[:count]], []

    def cut(begin, end, after):
        others, _ = lax.optimization_barrier((mine, after))
        for chunk in range(begin, end):
            parts.append(others[chunk * count : (chunk + 1) * count])

    early = 5 if networked else CHUNKS
    cut(1, early, parts[0])

    def start_low(chunk, after):
        outgoing = parts[chunk]
        if after is not None:
            outgoing, _ = lax.optimization_barrier((outgoing, after))
        arrived.append(swapped(outgoing, "tbit", 1))

    firsts, second_arrived = [], []

    def start_high(first):
        firsts.append(first)
        second_arrived.append(swapped(first, "tbit", 0))

    def low_level(chunk):
        return first_level(chunk, ranks, points, interpolants, parts[chunk], arrived[chunk])

    start_low(0, None)
    if networked:
        start_low(1, arrived[0])
        start_low(2, arrived[0])
    else:
        for chunk in range(1, CHUNKS):
            start_low(chunk, arrived[-1])
    start_high(low_level(0))
    if networked:
        owner_row, _ = lax.optimization_barrier((owner_row, firsts[0]))
        out_shape = (2, capacity, chips, 2, rank_width, width)
        *plan, rounds, out, stage = plan_switch(owner_row, out_shape)
        arrived[1], plan, rounds, out, stage = lax.optimization_barrier(
            (arrived[1], plan, rounds, out, stage)
        )
        most = jnp.broadcast_to(rounds, (8, 128))
    start_high(low_level(1))
    if networked:
        start_low(3, firsts[1])
    if not networked:
        for chunk in range(2, CHUNKS):
            start_high(low_level(chunk))
        pool = ()
        for chunk in range(CHUNKS):
            pool = (
                later_levels(
                    chunk, ranks, points, interpolants, firsts[chunk], second_arrived[chunk], pool_shape, pool
                ),
            )
        (pool,) = pool
        slot_parent, slot_used = slot_table(owner_row, box_count, capacity)
        outgoing = jnp.take(jnp.swapaxes(pool, 0, 1), slot_parent.T, axis=1)
        outgoing = jnp.where(slot_used.T[None, :, :, None, None], outgoing, 0.0)
        switched = lax.all_to_all(outgoing, "box", split_axis=2, concat_axis=2, tiled=True)
        return switched[None, None]

    state = (out, stage)
    received, crossed = {}, {}

    def exchange(packed):
        return (along_line(packed[0], chips, 0), along_line(packed[1], chips, 1))

    def cross(value):
        return lax.ppermute(value, "box", [(box, box ^ 1) for box in range(box_count)])

    def cross_pair(pair):
        return (cross(pair[0]), cross(pair[1]))

    staged = STATIC_ROUNDS - CROSS_LAG
    for step in range(STATIC_ROUNDS):
        high, low = None, None
        if step in (CHUNKS, CHUNKS + 2):
            received[step - LAG], most = lax.optimization_barrier((received[step - LAG], most))
        if step < CHUNKS:
            high = (step, firsts[step], second_arrived[step])
        if step + 2 < CHUNKS:
            low = (step + 2, parts[step + 2], arrived[step + 2])
        state, results = switch_round(
            plan,
            place,
            jnp.full((1,), step, jnp.int32),
            ranks,
            {LAG: received[step - LAG]} if step >= LAG else {},
            {CROSS_LAG: crossed[step - CROSS_LAG]} if step - CROSS_LAG >= staged else {},
            state,
            step < staged + LAG,
            True,
            [points, interpolants],
            high,
            low,
        )
        received[step] = exchange(results[:2])
        if low is not None:
            start_high(results[2])
        if step == 0:
            cut(early, CHUNKS, results[0])
        if step + 4 < CHUNKS:
            start_low(step + 4, results[0])
        if step >= staged:
            crossed[step] = cross_pair(received[step])
        if step == staged + LAG - 1:
            stage_crossed = cross(state[2])
            state = state[:2]
        if step in (CHUNKS - 3, CHUNKS - 1):
            most, _ = lax.optimization_barrier((most, results[0]))
            most = jnp.maximum(most, swapped(most, "tbit", 1 if step == CHUNKS - 3 else 0))
        if step == STATIC_ROUNDS - 1:
            state = (state[0], join_cores(place, stage_crossed, state[1]))

    most = jnp.maximum(most[0, 0], STATIC_ROUNDS)

    def more(carry):
        return carry[0] < most

    def again(carry):
        step, state, (older, newer), pending = carry
        state, packed = switch_round(
            plan, place, step[None], ranks, {LAG: older}, {CROSS_LAG: pending[0]}, state, False, True
        )
        return (step + 1, state, (newer, exchange(packed)), pending[1:] + (cross_pair(newer),))

    final = STATIC_ROUNDS
    step, state, (older, newer), pending = lax.while_loop(
        more,
        again,
        (
            jnp.int32(final),
            state,
            (received[final - 2], received[final - 1]),
            tuple(crossed[final - back] for back in range(CROSS_LAG, 1, -1)),
        ),
    )
    pending = pending + (cross_pair(newer),)
    state, _ = switch_round(
        plan,
        place,
        step[None],
        ranks,
        {2: older, 1: newer},
        {CROSS_LAG - index: pair for index, pair in enumerate(pending)},
        state,
        False,
        False,
    )
    return state[1].reshape(1, 1, 2, capacity, box_count, rank_width, width)


def solution(mesh):
    return jax.shard_map(
        per_device,
        mesh=mesh,
        in_specs=(
            P(None, "box", "tbit", None, None),
            P(None, "box", None, None),
            P(None, "box", None, None),
            P(None, "box", None, None),
            P(),
            P(),
            P(),
            P(None, "box", "tbit"),
            P(None, "box", "tbit"),
            P(),
            P(),
            P(),
        ),
        out_specs=P("tbit", "box", None, None, None, None, None),
        check_vma=False,
    )
```

```python
import functools
import math

import jax
import jax.numpy as jnp
from jax import lax
from jax.experimental import pallas as pl
from jax.experimental.pallas import tpu as pltpu
from jax.sharding import PartitionSpec as P

NPTS = 1048576
PHASE_BITS = 20
CHUNKS = 16
MAIN_LANES = 4
LANES = 6
LAG = 2
CROSS_LAG = 2
STATIC_ROUNDS = 20
PER_STEP = 4
VMEM_BYTES = 32 * 1024 * 1024
CODE_SHIFT = 16
SLOT_SHIFT = 16
SHORT = pl.CostEstimate(flops=1, bytes_accessed=1, transcendentals=0)
POINTS_SECOND = 2
POINTS_THIRD = 4
TARGETS_LOW = 5
TARGETS_HIGH = 6

SIN_TERMS = (
    1.0,
    -1.0 / 6.0,
    1.0 / 120.0,
    -1.0 / 5040.0,
    1.0 / 362880.0,
    -1.0 / 39916800.0,
    1.0 / 6227020800.0,
)


def swapped(value, axis, bit):
    mask = 2**bit
    pairs = [(source, source ^ mask) for source in range(lax.axis_size(axis))]
    return lax.ppermute(value, axis, pairs)


def slot_table(owner_row, box_count, capacity):
    parent_count = owner_row.shape[0]
    onehot = (owner_row[:, None] == jnp.arange(box_count, dtype=jnp.int32)[None, :]).astype(
        jnp.int32
    )
    earlier = jnp.cumsum(onehot, axis=0, dtype=jnp.int32) - onehot
    slot_of = jnp.sum(earlier * onehot, axis=1, dtype=jnp.int32)
    matches = (onehot.T[:, None, :] == 1) & (
        slot_of[None, None, :] == jnp.arange(capacity, dtype=jnp.int32)[None, :, None]
    )
    slot_parent = jnp.sum(
        jnp.where(matches, jnp.arange(parent_count, dtype=jnp.int32)[None, None, :], 0), axis=2
    )
    slot_used = jnp.any(matches, axis=2)
    return (slot_parent, slot_used)


def pick_slot(values, position):
    return lax.dynamic_index_in_dim(values, position, 2, keepdims=False)


def cos_kernel(targets, points):
    shift = 32 - PHASE_BITS
    phase = lax.shift_right_arithmetic(
        lax.shift_left(targets * points, jnp.int32(shift)), jnp.int32(shift)
    )
    offset = NPTS // 4 - jnp.abs(phase)
    y = offset.astype(jnp.float32) * jnp.float32(2.0 * math.pi / NPTS)
    square = y * y
    total = jnp.float32(SIN_TERMS[-1])
    for term in SIN_TERMS[-2::-1]:
        total = total * square + jnp.float32(term)
    return total * y


def split(value):
    high = value.astype(jnp.bfloat16)
    low = (value - high.astype(jnp.float32)).astype(jnp.bfloat16)
    return high, low


def stack_left(value):
    high, low = split(value)
    return jnp.concatenate(
        [jnp.concatenate([high, high], axis=1), jnp.concatenate([low, low], axis=1)], axis=0
    )


def product(left, right):
    rows = left.shape[0] // 2
    both = jnp.dot(
        left, jnp.concatenate(split(right), axis=0), preferred_element_type=jnp.float32
    )
    return both[:rows] + both[rows:]


def live(weights, rank):
    rows = lax.broadcasted_iota(jnp.int32, weights.shape, 0)
    return jnp.where(rows < rank, weights, 0.0)


def column(tile, row, begin, length):
    return jnp.transpose(tile)[begin : begin + length, row : row + 1]


def pair_weights(matrix, left, right, left_rank, right_rank):
    width = left.shape[1]
    both = product(matrix, jnp.concatenate([left, right], axis=1))
    return live(both[:, :width], left_rank), live(both[:, width:], right_rank)


def first_parent(tile, matrix, ranks, mine, arrived):
    rank_width = mine.shape[1]
    targets = column(tile, TARGETS_LOW, 0, rank_width)
    kernels = [cos_kernel(targets, tile[box : box + 1]) for box in range(2)]
    weights = pair_weights(matrix, *kernels, *ranks)
    return [
        product(stack_left(weights[box]), jnp.concatenate([mine[box], arrived[box]], axis=0))
        for box in range(2)
    ]


def later_parent(tile, matrices, ranks_second, ranks_third, mine, arrived):
    rank_width = mine.shape[1]
    targets = column(tile, TARGETS_LOW, rank_width, rank_width)
    kernels = [
        cos_kernel(targets, tile[POINTS_SECOND + box : POINTS_SECOND + box + 1]) for box in range(2)
    ]
    weights = pair_weights(matrices[0], *kernels, *ranks_second)
    seconds = [
        product(stack_left(weights[box]), jnp.concatenate([mine[box], arrived[box]], axis=0))
        for box in range(2)
    ]
    targets = column(tile, TARGETS_HIGH, 0, 2 * rank_width)
    kernel = cos_kernel(targets, tile[POINTS_THIRD : POINTS_THIRD + 1])
    weights = pair_weights(matrices[1], kernel[:rank_width], kernel[rank_width:], *ranks_third)
    stacked = jnp.concatenate(seconds, axis=0)
    return product(stack_left(jnp.concatenate(weights, axis=0)), stacked)


def ranks_of(ranks, level, parents, parent):
    start = 2 * (level * parents + parent)
    return ranks[start], ranks[start + 1]


def first_kernel(chunk, parents, ranks, points, matrices, mine, arrived, merged):
    matrix = stack_left(matrices[0])
    for member in range(mine.shape[0]):
        parent = (chunk * pl.num_programs(0) + pl.program_id(0)) * mine.shape[0] + member
        results = first_parent(
            points[member], matrix, ranks_of(ranks, 0, parents, parent), mine[member], arrived[member]
        )
        for box in range(2):
            merged[member, box] = results[box]


def later_kernel(chunk, parents, ranks, points, matrices, mine, arrived, *pool):
    merged = pool[-1]
    rank_width = mine.shape[2]
    stacks = [stack_left(matrices[1]), stack_left(matrices[2])]
    for member in range(mine.shape[0]):
        parent = (chunk * pl.num_programs(0) + pl.program_id(0)) * mine.shape[0] + member
        third = later_parent(
            points[member],
            stacks,
            ranks_of(ranks, 1, parents, parent),
            ranks_of(ranks, 2, parents, parent),
            mine[member],
            arrived[member],
        )
        for child in range(2):
            merged[member, child] = third[child * rank_width : (child + 1) * rank_width]


def chunk_spec(shape, chunk, steps, per_step):
    block = (per_step,) + tuple(shape[1:])
    rest = (0,) * (len(shape) - 1)
    return pl.BlockSpec(block, lambda step, *_: (chunk * steps + step,) + rest)


def whole_spec(shape):
    rest = (0,) * len(shape)
    return pl.BlockSpec(tuple(shape), lambda step, *_: rest)


def first_level(chunk, ranks, points, matrices, mine, arrived):
    per_step = PER_STEP
    steps = mine.shape[0] // per_step
    return pl.pallas_call(
        functools.partial(first_kernel, chunk, points.shape[0]),
        grid_spec=pltpu.PrefetchScalarGridSpec(
            num_scalar_prefetch=1,
            grid=(steps,),
            in_specs=[
                chunk_spec(points.shape, chunk, steps, per_step),
                whole_spec(matrices.shape),
                chunk_spec(mine.shape, 0, steps, per_step),
                chunk_spec(arrived.shape, 0, steps, per_step),
            ],
            out_specs=chunk_spec(arrived.shape, 0, steps, per_step),
        ),
        out_shape=jax.ShapeDtypeStruct(arrived.shape, jnp.float32),
        compiler_params=pltpu.CompilerParams(vmem_limit_bytes=VMEM_BYTES),
        name="first_level",
    )(ranks, points, matrices, mine, arrived)


def later_levels(chunk, ranks, points, matrices, mine, arrived, pool_shape, pool):
    per_step = PER_STEP
    steps = mine.shape[0] // per_step
    return pl.pallas_call(
        functools.partial(later_kernel, chunk, points.shape[0]),
        grid_spec=pltpu.PrefetchScalarGridSpec(
            num_scalar_prefetch=1,
            grid=(steps,),
            in_specs=[
                chunk_spec(points.shape, chunk, steps, per_step),
                whole_spec(matrices.shape),
                chunk_spec(mine.shape, 0, steps, per_step),
                chunk_spec(arrived.shape, 0, steps, per_step),
            ]
            + [pl.BlockSpec(memory_space=pl.ANY)] * len(pool),
            out_specs=chunk_spec(pool_shape, chunk, steps, per_step),
        ),
        out_shape=jax.ShapeDtypeStruct(pool_shape, jnp.float32),
        input_output_aliases={5: 0} if pool else {},
        compiler_params=pltpu.CompilerParams(vmem_limit_bytes=VMEM_BYTES),
        name="later_levels",
    )(ranks, points, matrices, mine, arrived, *pool)


def plan_kernel(
    chips, limit, chunks, owners, table, counts, slots, rounds, out, stage, own, ahead, used, zeros, sem
):
    parents = owners.shape[0]
    zeros[...] = jnp.zeros_like(zeros)
    fills = []
    for child in range(out.shape[0]):
        for slot in range(out.shape[1]):
            fills.append(pltpu.make_async_copy(zeros, out.at[child, slot], sem.at[len(fills)]))
            part = zeros.at[:, 0]
            fills.append(pltpu.make_async_copy(part, stage.at[child, slot], sem.at[len(fills)]))
    for fill in fills:
        fill.start()
    count = parents // chunks
    rows = chips + 1
    span = limit * LANES

    def clear(index, carry):
        counts[index] = 0
        return carry

    lax.fori_loop(0, 2 * rows * limit, clear, 0, unroll=16)
    for box in range(2 * chips):
        used[box] = 0

    def take_slot(parent, carry):
        owner = owners[parent]
        slot = used[owner]
        slots[parent] = (owner << SLOT_SHIFT) | slot
        used[owner] = slot + 1
        return carry

    lax.fori_loop(0, parents, take_slot, 0)
    width = chips * parents
    pairs = [(chip, goal) for chip in range(1, chips) for goal in range(chip + 1, chips)]
    last = []
    for direction in range(2):

        def true_chip(chip):
            return chip if direction == 0 else chips - 1 - chip

        total = 0
        for box in range(2 * chips):
            hops = true_chip(box // 2)
            total = total + used[box] * (hops * (hops + 1) // 2)

        def one_round(state):
            step, left, ready, own_head, head, tail, older = state
            ready, own_head, head, tail = list(ready), list(own_head), list(head), list(tail)
            for index in range(count):
                parent = jnp.minimum(step * count + index, parents - 1)
                goal = owners[parent] >> 1
                goal = goal if direction == 0 else chips - 1 - goal
                for chip in range(1, chips):
                    own[chip * parents + jnp.minimum(ready[chip], parents - 1)] = parent
                    here = (goal == chip) & (step < chunks)
                    ready[chip] = ready[chip] + here.astype(jnp.int32)
            seen = older[0]
            room = jnp.where(step < chunks, MAIN_LANES, LANES)
            for chip in range(chips - 1):
                row = (direction * rows + 1 + chip) * limit + step
                sent = jnp.int32(0)
                for goal in range(chips - 1, chip, -1):
                    onward = pairs.index((chip + 1, goal)) if (chip + 1, goal) in pairs else None
                    for forwarded in (True, False):
                        if forwarded and (chip, goal) not in pairs:
                            continue
                        if forwarded:
                            queue = pairs.index((chip, goal))
                            start, stop = head[queue], seen[queue]
                        else:
                            queue = chip * chips + goal
                            start, stop = own_head[queue], ready[goal]
                        number = jnp.minimum(stop - start, room - sent)

                        def move(index, carry):
                            if forwarded:
                                code = ahead[queue * width + start + index]
                            else:
                                code = own[goal * parents + start + index]
                                code = code | (true_chip(chip) << CODE_SHIFT)
                            table[row * LANES + sent + index] = code
                            if onward is not None:
                                ahead[onward * width + tail[onward] + index] = code
                            return carry

                        lax.fori_loop(0, number, move, 0)
                        sent = sent + number
                        if onward is not None:
                            tail[onward] = tail[onward] + number
                        if forwarded:
                            head[queue] = start + number
                        else:
                            own_head[queue] = start + number
                counts[row] = sent
                left = left - sent
            return (
                step + 1,
                left,
                tuple(ready),
                tuple(own_head),
                tuple(head),
                tuple(tail),
                tuple(older[1:]) + (tuple(tail),),
            )

        zero = jnp.int32(0)
        none = (zero,) * len(pairs)
        state = lax.while_loop(
            lambda state: (state[1] > 0) & (state[0] < limit),
            one_round,
            (zero, jnp.int32(total), (zero,) * chips, (zero,) * (chips * chips), none, none, (none,) * LAG),
        )
        last.append(state[0])
    rounds[0] = jnp.maximum(last[0], last[1])
    for fill in fills:
        fill.wait()


def plan_switch(owner_row, out_shape):
    parents = owner_row.shape[0]
    chips = out_shape[2]
    anywhere = pl.BlockSpec(memory_space=pl.ANY)
    limit = round_limit(parents)
    smem = pl.BlockSpec(memory_space=pltpu.SMEM)
    return pl.pallas_call(
        functools.partial(plan_kernel, chips, limit, CHUNKS),
        in_specs=[smem],
        out_specs=[smem] * 4 + [anywhere] * 2,
        out_shape=[
            jax.ShapeDtypeStruct((2 * (chips + 1) * limit * LANES,), jnp.int32),
            jax.ShapeDtypeStruct((2 * (chips + 1) * limit,), jnp.int32),
            jax.ShapeDtypeStruct((parents,), jnp.int32),
            jax.ShapeDtypeStruct((1,), jnp.int32),
            jax.ShapeDtypeStruct(out_shape, jnp.float32),
            jax.ShapeDtypeStruct(out_shape[:3] + out_shape[4:], jnp.float32),
        ],
        scratch_shapes=[
            pltpu.SMEM((chips * parents,), jnp.int32),
            pltpu.SMEM((chips * chips * chips * parents,), jnp.int32),
            pltpu.SMEM((2 * chips,), jnp.int32),
            pltpu.VMEM(out_shape[2:], jnp.float32),
            pltpu.SemaphoreType.DMA((2 * out_shape[0] * out_shape[1],)),
        ],
        name="plan_switch",
    )(owner_row)


def round_limit(parents):
    return 4 * parents // MAIN_LANES


def round_kernel(chips, limit, parents, receives, crossings, staging, high, low, sends, pooled, *refs):
    table, counts, slots, place, now, ranks = refs[:6]
    refs = refs[6:]
    sources = receives + crossings
    received, refs = refs[: 2 * len(sources)], refs[2 * len(sources) :]
    points, matrices = refs[:2] if high is not None or low is not None else (None, None)
    refs = refs[2:] if points is not None else refs
    mine_high, arrived_high = refs[:2] if high is not None else (None, None)
    refs = refs[2:] if high is not None else refs
    mine_low, arrived_low = refs[:2] if low is not None else (None, None)
    refs = refs[2:] if low is not None else refs
    refs = refs[1 + staging + pooled :]
    pool, out = refs[:2]
    stage = refs[2] if staging else None
    refs = refs[2 + staging :]
    outgoing = refs[: 2 * sends]
    merged = refs[2 * sends] if low is not None else None
    kept, sems = refs[-2:]
    fresh = 0 if high is None else mine_high.shape[0]
    last_sem = LANES * max(2 * len(sources), 2)
    z, core = place[0], place[1]
    odd = z & 1

    def row_of(direction, receiving, step):
        spot = jnp.where(direction == 0, z, chips - 1 - z)
        return (direction * (chips + 1) + (1 - receiving) + spot) * limit + step

    def home(sem, from_chip, parent, source, begin, crossed=False):
        spot = slots[parent]
        owner, slot = spot >> SLOT_SHIFT, spot & ((1 << SLOT_SHIFT) - 1)
        here = (owner >> 1) == z
        same = (owner & 1) == core

        @pl.when(here & same)
        def _():
            from_core = 1 - core if crossed else core
            copy = pltpu.make_async_copy(source, out.at[:, slot, from_chip, from_core], sem)
            copy.start() if begin else copy.wait()

        if staging and not crossed:

            @pl.when(here & jnp.logical_not(same))
            def _():
                copy = pltpu.make_async_copy(source, stage.at[:, slot, from_chip], sem)
                copy.start() if begin else copy.wait()

        return here

    def of_code(code):
        from_chip, parent = code >> CODE_SHIFT, code & ((1 << CODE_SHIFT) - 1)
        return from_chip, parent, from_chip * parents + parent

    def take_in(begin):
        for place_of, back in enumerate(sources):
            crossed = place_of >= len(receives)
            for port in range(2):
                step = now[0] - back
                row = row_of(1 - (odd ^ port), 1, jnp.maximum(step, 0))
                number = jnp.where(step >= 0, counts[row], 0)
                base = (2 * place_of + port) * LANES

                def one(lane, carry):
                    from_chip, parent, held = of_code(table[row * LANES + lane])
                    source = received[2 * place_of + port].at[lane]
                    sem = sems.at[base + lane]
                    here = home(sem, from_chip, parent, source, begin, crossed)
                    if not crossed:

                        @pl.when(jnp.logical_not(here))
                        def _():
                            copy = pltpu.make_async_copy(source, pool.at[held], sem)
                            copy.start() if begin else copy.wait()

                    return carry

                lax.fori_loop(0, number, one, 0)

    def send(begin):
        for port in range(2):
            row = row_of(odd ^ port, 0, now[0])

            def one(lane, carry):
                _, _, held = of_code(table[row * LANES + lane])
                copy = pltpu.make_async_copy(
                    pool.at[held], outgoing[port].at[lane], sems.at[port * LANES + lane]
                )
                copy.start() if begin else copy.wait()
                return carry

            lax.fori_loop(0, counts[row], one, 0)

    def keep(begin):
        def one(member, carry):
            parent = high * fresh + member
            home(sems.at[last_sem + member], z, parent, kept.at[member], begin)
            return carry

        lax.fori_loop(0, fresh, one, 0)

    take_in(True)
    if high is not None:
        rank_width = mine_high.shape[2]
        stacks = [stack_left(matrices[1]), stack_left(matrices[2])]
        for member in range(fresh):
            parent = high * fresh + member
            third = later_parent(
                points[parent],
                stacks,
                ranks_of(ranks, 1, parents, parent),
                ranks_of(ranks, 2, parents, parent),
                mine_high[member],
                arrived_high[member],
            )
            for child in range(2):
                kept[member, child] = third[child * rank_width : (child + 1) * rank_width]
        fill = pltpu.make_async_copy(
            kept, pool.at[pl.ds(z * parents + high * fresh, fresh)], sems.at[last_sem + fresh]
        )
        fill.start()
        keep(True)
    take_in(False)
    if high is not None:
        fill.wait()
    if sends:
        send(True)
    if low is not None:
        matrix = stack_left(matrices[0])
        for member in range(mine_low.shape[0]):
            parent = low * mine_low.shape[0] + member
            results = first_parent(
                points[parent],
                matrix,
                ranks_of(ranks, 0, parents, parent),
                mine_low[member],
                arrived_low[member],
            )
            for box in range(2):
                merged[member, box] = results[box]
    if high is not None:
        keep(False)
    if sends:
        send(False)


def switch_round(plan, place, now, ranks, received, crossed, state, staging, sends, levels=None, high=None, low=None):
    table, counts, slots = plan
    pooled = len(state) - 1 - int(staging)
    out = state[pooled]
    parents = slots.shape[0]
    chips = out.shape[2]
    block = (out.shape[0],) + out.shape[4:]
    inputs = [array for pair in [*received.values(), *crossed.values()] for array in pair]
    waiting = len(inputs)
    if high is not None or low is not None:
        inputs += levels
    for work in (high, low):
        if work is not None:
            inputs += work[1:]
    fresh = 0 if high is None else high[1].shape[0]
    anywhere = pl.BlockSpec(memory_space=pl.ANY)
    inside = pl.BlockSpec(memory_space=pltpu.VMEM)
    shapes = [jax.ShapeDtypeStruct((chips * parents,) + block, jnp.float32)]
    shapes += [jax.ShapeDtypeStruct(array.shape, array.dtype) for array in state[pooled:]]
    held = len(shapes)
    lanes = MAIN_LANES if high is not None else LANES
    shapes += [jax.ShapeDtypeStruct((lanes,) + block, jnp.float32)] * (2 * int(sends))
    if low is not None:
        shapes += [jax.ShapeDtypeStruct(low[1].shape, jnp.float32)]
    first = 6 + len(inputs)
    results = pl.pallas_call(
        functools.partial(
            round_kernel,
            chips,
            round_limit(parents),
            parents,
            tuple(received),
            tuple(crossed),
            int(staging),
            None if high is None else high[0],
            None if low is None else low[0],
            int(sends),
            pooled,
        ),
        grid_spec=pltpu.PrefetchScalarGridSpec(
            num_scalar_prefetch=6,
            grid=(),
            in_specs=[inside] * len(inputs) + [anywhere] * len(state),
            out_specs=[anywhere] * held + [inside] * (len(shapes) - held),
            scratch_shapes=[
                pltpu.VMEM((max(fresh, 1),) + block, jnp.float32),
                pltpu.SemaphoreType.DMA((LANES * max(waiting, 2) + fresh + 1,)),
            ],
        ),
        out_shape=shapes,
        input_output_aliases={first + index: index + 1 - pooled for index in range(len(state))},
        cost_estimate=SHORT,
        compiler_params=pltpu.CompilerParams(vmem_limit_bytes=VMEM_BYTES),
        name="switch_round",
    )(table, counts, slots, place, now, ranks, *inputs, *state)
    return tuple(results[:held]), tuple(results[held:])


def join_kernel(place, arrived, out_before, out):
    for child in range(2):
        for chip in range(arrived.shape[2]):
            out[child, 0, chip, 0] = arrived[child, 0, chip]


def join_cores(place, arrived, out):
    children, capacity, chips, _, rank_width, width = out.shape
    return pl.pallas_call(
        join_kernel,
        grid_spec=pltpu.PrefetchScalarGridSpec(
            num_scalar_prefetch=1,
            grid=(capacity,),
            in_specs=[
                pl.BlockSpec(
                    (children, 1, chips, rank_width, width), lambda slot, place: (0, slot, 0, 0, 0)
                ),
                pl.BlockSpec(memory_space=pl.ANY),
            ],
            out_specs=pl.BlockSpec(
                (children, 1, chips, 1, rank_width, width),
                lambda slot, place: (0, slot, 0, 1 - place[1], 0, 0),
            ),
        ),
        out_shape=jax.ShapeDtypeStruct(out.shape, out.dtype),
        input_output_aliases={2: 0},
        cost_estimate=SHORT,
        compiler_params=pltpu.CompilerParams(vmem_limit_bytes=VMEM_BYTES),
        name="join_cores",
    )(place, arrived, out)


def along_line(value, chips, port):
    pairs = []
    for chip in range(port, chips - 1, 2):
        for core in range(2):
            low, high = 2 * chip + core, 2 * (chip + 1) + core
            pairs += [(low, high), (high, low)]
    return lax.ppermute(value, "box", pairs)


def per_device(
    coeffs,
    skeleton_first,
    skeleton_second,
    skeleton_third,
    checks_first,
    checks_second,
    checks_third,
    ranks_first,
    ranks_second,
    ranks_third,
    interpolants,
    owners,
):
    tbit_index = lax.axis_index("tbit")
    box_index = lax.axis_index("box")
    box_count = lax.axis_size("box")
    parent_count = coeffs.shape[0]
    rank_width = coeffs.shape[3]
    capacity = 2 * parent_count // box_count
    group_count = 2 * box_count
    local_boxes = 2 * box_index + jnp.arange(2, dtype=jnp.int32)[None, :, None]

    def targets_of(checks, per_parent, picked, width):
        boxes = per_parent * parent_count
        absolute = jnp.arange(boxes, dtype=jnp.int32)[:, None] * (NPTS // boxes) + checks
        return lax.dynamic_index_in_dim(absolute.reshape(parent_count, -1, width), picked, 1)

    def first_points(slot):
        box = 4 * local_boxes + 2 * (slot % 2) + slot // 2
        return box * (NPTS // (4 * group_count)) + pick_slot(skeleton_first, slot)

    def second_points(slot):
        box = 2 * local_boxes + slot % 2
        return box * (NPTS // (2 * group_count)) + pick_slot(skeleton_second, slot)

    partner_high = jnp.bitwise_xor(tbit_index, 2)
    partner_low = jnp.bitwise_xor(tbit_index, 1)
    points_third = local_boxes * (NPTS // group_count) + pick_slot(skeleton_third, tbit_index)
    low_targets = jnp.concatenate(
        [
            targets_of(checks_first, 2, tbit_index // 2, rank_width),
            targets_of(checks_second, 4, tbit_index, rank_width),
        ],
        axis=2,
    )
    high_targets = targets_of(checks_third, 8, tbit_index, 2 * rank_width)
    points = jnp.concatenate(
        [
            jnp.concatenate([first_points(tbit_index), first_points(partner_high)], axis=2),
            jnp.concatenate([second_points(tbit_index), second_points(partner_low)], axis=2),
            points_third.reshape(parent_count, 1, 2 * rank_width),
            low_targets,
            high_targets,
            jnp.zeros_like(high_targets),
        ],
        axis=1,
    )
    rank_three = lax.dynamic_index_in_dim(
        lax.dynamic_index_in_dim(ranks_third, tbit_index, 1, keepdims=False),
        box_index,
        2,
        keepdims=False,
    )
    ranks = jnp.concatenate(
        [ranks_first.reshape(-1), ranks_second.reshape(-1), rank_three.reshape(-1)]
    )

    mine = coeffs[:, :, 0]
    count = parent_count // CHUNKS
    chips = box_count // 2
    networked = chips <= 4
    place = jnp.stack([box_index // 2, box_index % 2]).astype(jnp.int32)
    owner_row = lax.dynamic_index_in_dim(owners, tbit_index, 0, keepdims=False)
    width = coeffs.shape[-1]
    pool_shape = (chips * parent_count, 2, rank_width, width)
    if not networked:
        pool_shape = (parent_count, 2, rank_width, width)

    parts, arrived = [mine[:count]], []

    def cut(begin, end, after):
        others, _ = lax.optimization_barrier((mine, after))
        for chunk in range(begin, end):
            parts.append(others[chunk * count : (chunk + 1) * count])

    early = 5 if networked else CHUNKS
    cut(1, early, parts[0])

    def start_low(chunk, after):
        outgoing = parts[chunk]
        if after is not None:
            outgoing, _ = lax.optimization_barrier((outgoing, after))
        arrived.append(swapped(outgoing, "tbit", 1))

    firsts, second_arrived = [], []

    def start_high(first):
        firsts.append(first)
        second_arrived.append(swapped(first, "tbit", 0))

    def low_level(chunk):
        return first_level(chunk, ranks, points, interpolants, parts[chunk], arrived[chunk])

    start_low(0, None)
    if networked:
        start_low(1, arrived[0])
        start_low(2, arrived[0])
    else:
        for chunk in range(1, CHUNKS):
            start_low(chunk, arrived[-1])
    start_high(low_level(0))
    if networked:
        start_low(3, firsts[0])
    start_high(low_level(1))
    if networked:
        owner_row, _ = lax.optimization_barrier((owner_row, firsts[1]))
        out_shape = (2, capacity, chips, 2, rank_width, width)
        *plan, rounds, out, stage = plan_switch(owner_row, out_shape)
        most = jnp.broadcast_to(rounds, (8, 128))
    if not networked:
        for chunk in range(2, CHUNKS):
            start_high(low_level(chunk))
        pool = ()
        for chunk in range(CHUNKS):
            pool = (
                later_levels(
                    chunk, ranks, points, interpolants, firsts[chunk], second_arrived[chunk], pool_shape, pool
                ),
            )
        (pool,) = pool
        slot_parent, slot_used = slot_table(owner_row, box_count, capacity)
        outgoing = jnp.take(jnp.swapaxes(pool, 0, 1), slot_parent.T, axis=1)
        outgoing = jnp.where(slot_used.T[None, :, :, None, None], outgoing, 0.0)
        switched = lax.all_to_all(outgoing, "box", split_axis=2, concat_axis=2, tiled=True)
        return switched[None, None]

    state = (out, stage)
    received, crossed = {}, {}

    def exchange(packed):
        return (along_line(packed[0], chips, 0), along_line(packed[1], chips, 1))

    def cross(value):
        return lax.ppermute(value, "box", [(box, box ^ 1) for box in range(box_count)])

    def cross_pair(pair):
        return (cross(pair[0]), cross(pair[1]))

    staged = STATIC_ROUNDS - CROSS_LAG
    for step in range(STATIC_ROUNDS):
        high, low = None, None
        if step in (CHUNKS, CHUNKS + 2):
            received[step - LAG], most = lax.optimization_barrier((received[step - LAG], most))
        if step < CHUNKS:
            high = (step, firsts[step], second_arrived[step])
        if step + 2 < CHUNKS:
            low = (step + 2, parts[step + 2], arrived[step + 2])
        state, results = switch_round(
            plan,
            place,
            jnp.full((1,), step, jnp.int32),
            ranks,
            {LAG: received[step - LAG]} if step >= LAG else {},
            {CROSS_LAG: crossed[step - CROSS_LAG]} if step - CROSS_LAG >= staged else {},
            state,
            step < staged + LAG,
            True,
            [points, interpolants],
            high,
            low,
        )
        received[step] = exchange(results[:2])
        if low is not None:
            start_high(results[2])
        if step == 0:
            cut(early, CHUNKS, results[0])
        if step + 4 < CHUNKS:
            start_low(step + 4, results[0])
        if step >= staged:
            crossed[step] = cross_pair(received[step])
        if step == staged + LAG - 1:
            stage_crossed = cross(state[2])
            state = state[:2]
        if step in (CHUNKS - 3, CHUNKS - 1):
            most, _ = lax.optimization_barrier((most, results[0]))
            most = jnp.maximum(most, swapped(most, "tbit", 1 if step == CHUNKS - 3 else 0))
        if step == STATIC_ROUNDS - 1:
            state = (state[0], join_cores(place, stage_crossed, state[1]))

    most = jnp.maximum(most[0, 0], STATIC_ROUNDS)

    def more(carry):
        return carry[0] < most

    def again(carry):
        step, state, (older, newer), pending = carry
        state, packed = switch_round(
            plan, place, step[None], ranks, {LAG: older}, {CROSS_LAG: pending[0]}, state, False, True
        )
        return (step + 1, state, (newer, exchange(packed)), pending[1:] + (cross_pair(newer),))

    final = STATIC_ROUNDS
    step, state, (older, newer), pending = lax.while_loop(
        more,
        again,
        (
            jnp.int32(final),
            state,
            (received[final - 2], received[final - 1]),
            tuple(crossed[final - back] for back in range(CROSS_LAG, 1, -1)),
        ),
    )
    pending = pending + (cross_pair(newer),)
    state, _ = switch_round(
        plan,
        place,
        step[None],
        ranks,
        {2: older, 1: newer},
        {CROSS_LAG - index: pair for index, pair in enumerate(pending)},
        state,
        False,
        False,
    )
    return state[1].reshape(1, 1, 2, capacity, box_count, rank_width, width)


def solution(mesh):
    return jax.shard_map(
        per_device,
        mesh=mesh,
        in_specs=(
            P(None, "box", "tbit", None, None),
            P(None, "box", None, None),
            P(None, "box", None, None),
            P(None, "box", None, None),
            P(),
            P(),
            P(),
            P(None, "box", "tbit"),
            P(None, "box", "tbit"),
            P(),
            P(),
            P(),
        ),
        out_specs=P("tbit", "box", None, None, None, None, None),
        check_vma=False,
    )
```
